128 devices in a mesh: energy: 32 (over z, y, x_lo), mom: 4 (over x_hi, core).
Axes of the slice: x: 4 (x_hi: 2, x_lo: 2; x = x_hi * 2 + x_lo), y: 4, z: 4, core: 2. Of those that a mesh axis runs over, the one named last changes fastest.
Arguments:
- green_ret: bfloat16 [16, 64, 2, 512, 512], P('mom', 'energy'), may hold values from -0.25 to 0.25
- broadening: float32 [16, 64, 512], P('mom', 'energy'), may hold values from 0.2 to 2
- coupling: bfloat16 [16, 512, 512], P(None, 'mom'), may hold values from -1.5 to 1.5
- shift_steps: int32 [4], replicated, may hold values from 1 to 2, as said below
- mode_weight: float32 [4], replicated, may hold values from 0.05 to 0.25
- occupation: float32 [4], replicated, may hold values from 0.1 to 2
- momentum_map: int32 [16, 16], replicated, may hold values from 0 to 15, as said below
Outputs:
- self_energy: bfloat16 [16, 64, 2, 512, 512], P(None, 'energy', None, 'mom')
- density: float32 [512, 16, 2, 512], P('energy', 'mom')
The draws below stay inside these ranges and needn't reach their ends.
Inputs may be any that keep to these rules, and one draw needn't show every extreme that they name: `shift_steps`: some entry equals 2. `momentum_map`: every row and every column holds each of the 16 momentum indices once.
All inputs are finite; a program needn't handle non-finite values.
Results may differ from the reference program's by a relative error of at most 0.02.
Values may be sent and summed in bfloat16 or wider, within the bound.
A program may use at most 192 MiB of HBM per device.

```python
import math
import jax
import jax.numpy as jnp
from jax import lax

NORB = 512
NK = 16
NMODE = 4
SHIFT_MAX = 2
NE = 64


def draw_shift_steps(key, part):
    first_key, second_key = jax.random.split(jax.random.fold_in(key, 11))
    values = jax.random.randint(first_key, (NMODE,), 1, SHIFT_MAX + 1)
    chosen = jax.random.randint(second_key, (), 0, NMODE)
    return jnp.where(jnp.arange(NMODE) == chosen, SHIFT_MAX, values).astype(jnp.int32)


def draw_momentum_map(key, part):
    first_key, second_key = jax.random.split(jax.random.fold_in(key, 23))
    row_perm = jax.random.permutation(first_key, NK)
    column_perm = jax.random.permutation(second_key, NK)
    return ((row_perm[:, None] + column_perm[None, :]) % NK).astype(jnp.int32)


def block_levels(own_key, shape, cuts, least, high):
    factor_of, own = 1.0, jax.random.fold_in(own_key, 6)
    for position, blocks in cuts:
        heights = jnp.exp(jax.random.uniform(jax.random.fold_in(own, position), (blocks,), jnp.float32, least / len(cuts), high / len(cuts)))
        factor_of = factor_of * jnp.repeat(heights, shape[position] // blocks).reshape([-1 if axis == position else 1 for axis in range(len(shape))])
    return factor_of


def scatter_about(own_key, dims, width, reach, shards=(), held_as=jnp.bfloat16):
    drawn = jax.random.normal(own_key, dims, jnp.float32) * width
    if len(shards) > 0:
        drawn = block_levels(own_key, dims, shards, -0.22, 0.18) * drawn
    return jnp.clip(drawn, min=-reach, max=reach).astype(held_as)


def setup_inputs(seed: int = 0) -> dict:
    keys = jax.random.split(jax.random.key(seed), 8)
    green_ret = scatter_about(keys[0], (NK, NE, 2, NORB, NORB), NORB ** -0.5, 0.25, ((0, 4), (1, 32)))
    broadening = jnp.clip(jnp.exp(math.log(2.0) - 2.3025851 * jax.random.uniform(keys[1], (NK, NE, NORB), jnp.float32) ** block_levels(keys[1], (NK, NE, NORB), ((0, 4), (1, 32)), -0.2, 0.2)), 0.2, 2.0)
    coupling = scatter_about(keys[2], (NK, NORB, NORB), 0.25, 1.5, ((1, 4),))
    shift_steps = draw_shift_steps(jax.random.fold_in(keys[7], 71), 0)
    mode_weight = jnp.clip(jnp.exp(jax.random.uniform(keys[4], (NMODE,), jnp.float32, math.log(0.05), math.log(0.25))), 0.05, 0.25)
    occupation = jnp.clip(jnp.exp(jax.random.uniform(keys[5], (NMODE,), jnp.float32, math.log(0.1), math.log(2.0))), 0.1, 2.0)
    momentum_map = draw_momentum_map(jax.random.fold_in(keys[7], 71), 0)
    return dict(green_ret=green_ret, broadening=broadening, coupling=coupling, shift_steps=shift_steps, mode_weight=mode_weight, occupation=occupation, momentum_map=momentum_map)


def sandwich(left, right):
    left_full = left.astype(jnp.float32)
    right_full = right.astype(jnp.float32)
    real_part = jnp.einsum('ecij,ecmj->eim', left_full, right_full)
    imag_part = jnp.einsum('eij,emj->eim', left_full[:, 1], right_full[:, 0]) - jnp.einsum('eij,emj->eim', left_full[:, 0], right_full[:, 1])
    return jnp.stack([real_part, imag_part], axis=1)


def complex_product(left, right):
    left_full = left.astype(jnp.float32)
    right_full = right.astype(jnp.float32)
    real_part = jnp.einsum('eij,ejm->eim', left_full[:, 0], right_full[:, 0]) - jnp.einsum('eij,ejm->eim', left_full[:, 1], right_full[:, 1])
    imag_part = jnp.einsum('eij,ejm->eim', left_full[:, 0], right_full[:, 1]) + jnp.einsum('eij,ejm->eim', left_full[:, 1], right_full[:, 0])
    return jnp.stack([real_part, imag_part], axis=1)


def scale_columns(green, gamma):
    return (green.astype(jnp.float32) * gamma[:, None, None, :]).astype(jnp.bfloat16)


def reference(green_ret, broadening, coupling, shift_steps, mode_weight, occupation, momentum_map):
    def first_pass(inputs):
        green, gamma = inputs
        return sandwich(scale_columns(green, gamma), green).astype(jnp.bfloat16)

    lesser = lax.map(first_pass, (green_ret, broadening))
    padded = jnp.pad(lesser, ((0, 0), (SHIFT_MAX, SHIFT_MAX), (0, 0), (0, 0), (0, 0)))

    def shifted(padded_one):
        total = jnp.zeros((NE,) + padded_one.shape[1:], jnp.float32)
        for branch in range(NMODE):
            offset = shift_steps[branch].astype(jnp.int32)
            above = lax.dynamic_slice_in_dim(padded_one, (SHIFT_MAX + offset).astype(jnp.int32), NE, 0).astype(jnp.float32)
            below = lax.dynamic_slice_in_dim(padded_one, (SHIFT_MAX - offset).astype(jnp.int32), NE, 0).astype(jnp.float32)
            total = total + mode_weight[branch] * ((occupation[branch] + 1.0) * above + occupation[branch] * below)
        return total.astype(jnp.bfloat16)

    source = lax.map(shifted, padded)

    def convolve(target):
        def add_term(qpoint, total):
            donor_index = momentum_map[target, qpoint].astype(jnp.int32)
            donor = lax.dynamic_index_in_dim(source, donor_index, 0, keepdims=False).astype(jnp.float32)
            weight = lax.dynamic_index_in_dim(coupling, qpoint, 0, keepdims=False).astype(jnp.float32)
            return total + weight[None, None] * donor

        total = lax.fori_loop(0, NK, add_term, jnp.zeros(source.shape[1:], jnp.float32))
        return total.astype(jnp.bfloat16)

    self_energy = lax.map(convolve, jnp.arange(NK, dtype=jnp.int32))

    def second_pass(inputs):
        green, gamma, sigma = inputs
        scaled = scale_columns(green, gamma)
        mixed = (complex_product(green, sigma) + scaled.astype(jnp.float32)).astype(jnp.bfloat16)
        return jnp.sum(sandwich(mixed, green), axis=0) / NE

    density_blocks = lax.map(second_pass, (green_ret, broadening, self_energy))
    density = jnp.transpose(density_blocks, (2, 0, 1, 3))
    return self_energy, density
```

```python
import functools

import jax
import jax.numpy as jnp
from jax import lax
from jax.experimental import pallas as pl
from jax.experimental.pallas import tpu as pltpu
from jax.sharding import PartitionSpec as P

SHIFT_MAX = 2
BOTH = ("energy", "mom")
MIB = 1 << 20
NT = (((1,), (1,)), ((), ()))


def dot_nt(left, right):
    return lax.dot_general(left, right, NT, preferred_element_type=jnp.float32)


def dot_nn(left, right):
    return jnp.dot(left, right, preferred_element_type=jnp.float32)


def scale(block, gamma):
    return (block.astype(jnp.float32) * gamma).astype(jnp.bfloat16)


def lesser_kernel(half, green, gamma, out):
    g_re = green[0, 0, 0]
    g_im = green[0, 0, 1]
    gam = gamma[0, 0]
    wide_re = g_re.astype(jnp.float32)
    wide_im = g_im.astype(jnp.float32)
    less = (wide_re - wide_im).astype(jnp.bfloat16)
    more = (wide_re + wide_im).astype(jnp.bfloat16)
    total = dot_nt(scale(g_re, gam), less) + dot_nt(scale(g_im, gam), more)
    out[0, 0] = total.astype(jnp.bfloat16)


def packed_lesser(half, green, gamma):
    energies, norb = green.shape[1], green.shape[-1]
    count = green.shape[0] // 2
    return pl.pallas_call(
        lesser_kernel,
        grid_spec=pltpu.PrefetchScalarGridSpec(
            num_scalar_prefetch=1,
            grid=(count, energies),
            in_specs=[
                pl.BlockSpec((1, 1, 2, norb, norb), lambda k, e, h: (h[0] * count + k, e, 0, 0, 0)),
                pl.BlockSpec((1, 1, 1, norb), lambda k, e, h: (h[0] * count + k, e, 0, 0)),
            ],
            out_specs=pl.BlockSpec((1, 1, norb, norb), lambda k, e, h: (k, e, 0, 0)),
        ),
        out_shape=jax.ShapeDtypeStruct((count, energies, norb, norb), jnp.bfloat16),
        compiler_params=pltpu.CompilerParams(vmem_limit_bytes=32 * MIB),
        cost_estimate=pl.CostEstimate(
            flops=4 * count * energies * norb**3,
            bytes_accessed=6 * count * energies * norb**2,
            transcendentals=0,
        ),
        name="lesser",
    )(half, green, gamma)


def shift_kernel(place, weights, own, got, own_halo, got_halo, out_own, out_other):
    rows = own.shape[2]
    step = 16

    def run(first, second, third, fourth, outs):
        def slab(i, carry):
            at = pl.ds(pl.multiple_of(i * step, step), step)
            levels = [
                ref[0, e, at, :].astype(jnp.float32)
                for ref in (first, second, third, fourth)
                for e in range(2)
            ]
            for o in range(4):
                total = weights[0] * levels[o + 3] + weights[1] * levels[o + 4]
                total = total + weights[2] * levels[o + 1] + weights[3] * levels[o]
                outs[o // 2][0, o % 2, at, :] = total.astype(jnp.bfloat16)
            return carry

        lax.fori_loop(0, rows // step, slab, 0)

    @pl.when(place[0] == 0)
    def _():
        run(got_halo, own, got, own_halo, (out_own, out_other))

    @pl.when(place[0] != 0)
    def _():
        run(own_halo, got, own, got_halo, (out_other, out_own))


def shifted(place, weights, own, got, own_halo, got_halo):
    count, energies, norb, _ = own.shape
    rows = norb // 4
    block = pl.BlockSpec((1, energies, rows, norb), lambda k, i, p, w: (k, 0, i, 0))
    out = jax.ShapeDtypeStruct(own.shape, jnp.bfloat16)
    return pl.pallas_call(
        shift_kernel,
        grid_spec=pltpu.PrefetchScalarGridSpec(
            num_scalar_prefetch=2,
            grid=(count, norb // rows),
            in_specs=[block] * 4,
            out_specs=[block] * 2,
        ),
        out_shape=[out, out],
        compiler_params=pltpu.CompilerParams(vmem_limit_bytes=32 * MIB),
        cost_estimate=pl.CostEstimate(
            flops=32 * count * norb**2, bytes_accessed=24 * count * norb**2, transcendentals=0
        ),
        name="shifted",
    )(place, weights, own, got, own_halo, got_halo)


def convolve_kernel(tiles, table, *refs):
    n = 8
    rows_of, cols_of = refs[:n], refs[n : 2 * n]
    coup, coup_t, out, along, across = refs[2 * n :]
    targets, _, _, height, norb = out.shape
    group = pl.program_id(0) * targets

    def spread(sources, factor, at, store):
        acc = [[None, None] for _ in range(targets)]
        for quad in range(n // 2):
            donors = [(s, kk) for s in (2 * quad, 2 * quad + 1) for kk in range(2)]
            held = [[sources[s][kk, e, at[0], at[1]] for e in range(2)] for s, kk in donors]
            for t in range(targets):
                pick = [table[(group + t) * 2 * n + 4 * quad + d] for d in range(4)]
                c = [factor[0, q, at[0], at[1]] for q in pick]
                for e in range(2):
                    part = (c[0] * held[0][e] + c[1] * held[1][e]) + (
                        c[2] * held[2][e] + c[3] * held[3][e]
                    )
                    part = part.astype(jnp.float32)
                    acc[t][e] = part if acc[t][e] is None else acc[t][e] + part
        for t in range(targets):
            for e in range(2):
                store[t, e, at[0], at[1]] = acc[t][e]

    def over_rows(i, carry):
        r, l = i // 2, i % 2
        at = (
            pl.ds(pl.multiple_of(r * 16, 16), 16),
            pl.ds(pl.multiple_of(l * (norb // 2), norb // 2), norb // 2),
        )
        spread(rows_of, coup, at, along)
        return carry

    def over_cols(i, carry):
        at = (pl.ds(pl.multiple_of(i * 32, 32), 32), slice(None))
        spread(cols_of, coup_t, at, across)
        return carry

    lax.fori_loop(0, height // 16 * 2, over_rows, 0)
    lax.fori_loop(0, norb // 32, over_cols, 0)

    def finish(i, carry):
        t, e = i // 2, i % 2
        for b in range(norb // height):
            span = slice(b * height, (b + 1) * height)
            u = along[t, e, :, span]
            v = across[t, e, span, :].T
            out[t, e, 0, :, span] = (u + v).astype(jnp.bfloat16)
            out[t, e, 1, :, span] = (u - v).astype(jnp.bfloat16)
        return carry

    lax.fori_loop(0, targets * 2, finish, 0)


def convolved(tiles, table, sources, coup, coup_t, groups, steps, targets, name):
    norb = sources[0].shape[-1]
    height = coup.shape[2]
    points = coup.shape[1]
    row_block = pl.BlockSpec((2, 2, height, norb), lambda g, i, t, q: (0, 0, t[i], 0))
    col_block = pl.BlockSpec((2, 2, norb, height), lambda g, i, t, q: (0, 0, 0, t[i]))
    slot = lambda g, i, t, q: (t[steps + i], 0, 0, 0)
    return pl.pallas_call(
        convolve_kernel,
        grid_spec=pltpu.PrefetchScalarGridSpec(
            num_scalar_prefetch=2,
            grid=(groups, steps),
            in_specs=[row_block] * 8
            + [col_block] * 8
            + [
                pl.BlockSpec((1, points, height, norb), slot),
                pl.BlockSpec((1, points, norb, height), slot),
            ],
            out_specs=pl.BlockSpec((targets, 2, 2, height, norb), lambda g, i, t, q: (g, 0, 0, i, 0)),
            scratch_shapes=[
                pltpu.VMEM((targets, 2, height, norb), jnp.float32),
                pltpu.VMEM((targets, 2, norb, height), jnp.float32),
            ],
        ),
        out_shape=jax.ShapeDtypeStruct(
            (groups * targets, 2, 2, steps * height, norb), jnp.bfloat16
        ),
        compiler_params=pltpu.CompilerParams(vmem_limit_bytes=56 * MIB),
        cost_estimate=pl.CostEstimate(
            flops=8 * groups * steps * targets * points * height * norb,
            bytes_accessed=12 * MIB * steps + 2 * MIB * steps * groups,
            transcendentals=0,
        ),
        name=name,
    )(tiles, table, *sources, *sources, coup, coup_t)


def density_kernel(inverse, green, gamma, sigma, out):
    d_re = d_im = None
    for e in range(green.shape[1]):
        g_re, g_im = green[0, e, 0], green[0, e, 1]
        s_re, s_im = sigma[0, e, 0], sigma[0, e, 1]
        gam = gamma[0, e]
        m_re = dot_nn(g_re, s_re) - dot_nn(g_im, s_im) + scale(g_re, gam).astype(jnp.float32)
        m_im = dot_nn(g_re, s_im) + dot_nn(g_im, s_re) + scale(g_im, gam).astype(jnp.float32)
        m_re, m_im = m_re.astype(jnp.bfloat16), m_im.astype(jnp.bfloat16)
        one = dot_nt(m_re, g_re) + dot_nt(m_im, g_im)
        two = dot_nt(m_im, g_re) - dot_nt(m_re, g_im)
        d_re = one if d_re is None else d_re + one
        d_im = two if d_im is None else d_im + two
    out[0, 0] = (d_re * inverse).astype(jnp.bfloat16)
    out[0, 1] = (d_im * inverse).astype(jnp.bfloat16)


def partial_density(green, gamma, sigma, inverse):
    count, energies, _, norb, _ = green.shape
    whole = pl.BlockSpec((1, energies, 2, norb, norb), lambda k: (k, 0, 0, 0, 0))
    return pl.pallas_call(
        functools.partial(density_kernel, inverse),
        grid=(count,),
        in_specs=[
            whole,
            pl.BlockSpec((1, energies, 1, norb), lambda k: (k, 0, 0, 0)),
            whole,
        ],
        out_specs=pl.BlockSpec((1, 2, norb, norb), lambda k: (k, 0, 0, 0)),
        out_shape=jax.ShapeDtypeStruct((count, 2, norb, norb), jnp.bfloat16),
        compiler_params=pltpu.CompilerParams(vmem_limit_bytes=48 * MIB),
        cost_estimate=pl.CostEstimate(
            flops=16 * count * energies * norb**3,
            bytes_accessed=(8 * energies + 4) * count * norb**2,
            transcendentals=0,
        ),
        name="density",
    )(green, gamma, sigma)


def on_device(green, broadening, coupling, shift_steps, mode_weight, occupation, momentum_map):
    n_energy, n_mom = lax.axis_size("energy"), lax.axis_size("mom")
    pairs = n_energy // 2
    local_k = green.shape[0]
    half = local_k // 2
    points = momentum_map.shape[1]
    energy, mom = lax.axis_index("energy"), lax.axis_index("mom")
    x_lo = energy % 2

    def flip(x, lo, mo):
        perm = [
            (e * n_mom + m, (e ^ lo) * n_mom + (m ^ mo))
            for e in range(n_energy)
            for m in range(n_mom)
        ]
        return lax.ppermute(x, BOTH, perm)

    def along_pairs(x, step_of_low):
        moves = []
        for j in range(pairs):
            for lo in range(2):
                to = j + (step_of_low if lo == 0 else -step_of_low)
                if 0 <= to < pairs:
                    moves.append((2 * j + lo, 2 * to + lo))
        return lax.ppermute(x, "energy", moves)

    gamma = broadening[:, :, None, :]
    place = x_lo.astype(jnp.int32)[None]

    sent = packed_lesser(1 - place, green, gamma)
    got = flip(sent, 1, 0)
    coup_b = flip(coupling, 1, 2)
    coup_c = flip(coupling, 0, 1)
    own = packed_lesser(place, green, gamma)
    own_halo = along_pairs(own, -1)
    got_halo = along_pairs(got, 1)
    coup_bc = flip(coup_b, 0, 1)

    def weight_of(step, factor):
        return 0.5 * jnp.sum(jnp.where(shift_steps == step, mode_weight * factor, 0.0))

    weights = jnp.stack(
        [weight_of(s, occupation + 1.0) for s in (1, 2)] + [weight_of(s, occupation) for s in (1, 2)]
    ).astype(jnp.float32)

    source_own, source_other = shifted(place, weights, own, got, own_halo, got_halo)
    near = [
        source_own,
        flip(source_other, 1, 0),
        flip(source_other, 1, 2),
        flip(source_own, 0, 2),
    ]
    moves = [(0, 0), (1, 0), (1, 2), (0, 2)]
    sources = near + [flip(x, 0, 1) for x in near]
    moves = moves + [(lo, mo ^ 1) for lo, mo in moves]

    coup = jnp.stack([coupling, coup_c, coup_b, coup_bc])
    coup_t = jnp.swapaxes(coup, 2, 3)

    donors = jnp.stack(
        [(mom ^ mo) * local_k + (x_lo ^ lo) * half + kk for lo, mo in moves for kk in range(half)]
    ).astype(jnp.int32)
    table = jnp.sum(
        jnp.where(
            momentum_map[:, :, None] == donors[None, None, :],
            jnp.arange(points, dtype=jnp.int32)[None, :, None],
            0,
        ),
        axis=1,
    ).astype(jnp.int32)
    table_home = lax.dynamic_slice_in_dim(table, mom * local_k, local_k, 0)

    every = jnp.arange(n_mom, dtype=jnp.int32)
    tiles_home = jnp.concatenate([every, every ^ mom.astype(jnp.int32)])
    tiles_out = jnp.stack([mom.astype(jnp.int32), jnp.zeros((), jnp.int32)])

    sigma_home = convolved(
        tiles_home, table_home.reshape(-1), sources, coup, coup_t, 1, n_mom, local_k, "home"
    )
    part = partial_density(green, gamma, sigma_home, 1.0 / (green.shape[1] * n_energy))
    summed = lax.psum_scatter(part, "energy", scatter_dimension=2, tiled=True)
    density = jnp.transpose(summed, (2, 0, 1, 3)).astype(jnp.float32)
    self_energy = convolved(
        tiles_out, table.reshape(-1), sources, coup, coup_t, n_mom, 1, local_k, "rows"
    )
    return (self_energy, density)


def solution(mesh):
    return jax.shard_map(
        on_device,
        mesh=mesh,
        in_specs=(
            P("mom", "energy", None, None, None),
            P("mom", "energy", None),
            P(None, "mom", None),
            P(),
            P(),
            P(),
            P(),
        ),
        out_specs=(P(None, "energy", None, "mom", None), P("energy", "mom", None, None)),
        check_vma=False,
    )
```

```python
import functools

import jax
import jax.numpy as jnp
from jax import lax
from jax.experimental import pallas as pl
from jax.experimental.pallas import tpu as pltpu
from jax.sharding import PartitionSpec as P

CHUNKS = 2
BOTH = ("energy", "mom")
MIB = 1 << 20
NT = (((1,), (1,)), ((), ()))


def dot_nt(left, right):
    return lax.dot_general(left, right, NT, preferred_element_type=jnp.float32)


def dot_nn(left, right):
    return jnp.dot(left, right, preferred_element_type=jnp.float32)


def scale(block, gamma):
    return (block.astype(jnp.float32) * gamma).astype(jnp.bfloat16)


def lesser_kernel(chunk, half, green, gamma, out):
    rows = out.shape[2]
    span = slice(chunk * rows, (chunk + 1) * rows)
    gam = gamma[0, 0]
    wide_re = green[0, 0, 0].astype(jnp.float32)
    wide_im = green[0, 0, 1].astype(jnp.float32)
    less = (wide_re - wide_im).astype(jnp.bfloat16)
    more = (wide_re + wide_im).astype(jnp.bfloat16)
    total = dot_nt(scale(green[0, 0, 0, span], gam), less) + dot_nt(
        scale(green[0, 0, 1, span], gam), more
    )
    out[0, 0] = total.astype(jnp.bfloat16)


def packed_lesser(half, green, gamma, chunk):
    energies, norb = green.shape[1], green.shape[-1]
    count = green.shape[0] // 2
    rows = norb // CHUNKS
    return pl.pallas_call(
        functools.partial(lesser_kernel, chunk),
        grid_spec=pltpu.PrefetchScalarGridSpec(
            num_scalar_prefetch=1,
            grid=(count, energies),
            in_specs=[
                pl.BlockSpec((1, 1, 2, norb, norb), lambda k, e, h: (h[0] * count + k, e, 0, 0, 0)),
                pl.BlockSpec((1, 1, 1, norb), lambda k, e, h: (h[0] * count + k, e, 0, 0)),
            ],
            out_specs=pl.BlockSpec((1, 1, rows, norb), lambda k, e, h: (k, e, 0, 0)),
        ),
        out_shape=jax.ShapeDtypeStruct((count, energies, rows, norb), jnp.bfloat16),
        compiler_params=pltpu.CompilerParams(vmem_limit_bytes=32 * MIB),
        cost_estimate=pl.CostEstimate(
            flops=4 * count * energies * rows * norb**2,
            bytes_accessed=6 * count * energies * norb**2,
            transcendentals=0,
        ),
        name="lesser",
    )(half, green, gamma)


def shift_kernel(place, weights, own, got, own_halo, got_halo, early, out_own, out_other):
    rows = own.shape[2]
    step = 16

    def run(first, second, third, fourth, outs):
        def slab(i, carry):
            at = pl.ds(pl.multiple_of(i * step, step), step)
            levels = [
                ref[0, e, at, :].astype(jnp.float32)
                for ref in (first, second, third, fourth)
                for e in range(2)
            ]
            for o in range(4):
                total = weights[0] * levels[o + 3] + weights[1] * levels[o + 4]
                total = total + weights[2] * levels[o + 1] + weights[3] * levels[o]
                outs[o // 2][0, o % 2, at, :] = total.astype(jnp.bfloat16)
            return carry

        lax.fori_loop(0, rows // step, slab, 0)

    @pl.when(place[0] == 0)
    def _():
        run(got_halo, own, got, own_halo, (out_own, out_other))

    @pl.when(place[0] != 0)
    def _():
        run(own_halo, got, own, got_halo, (out_other, out_own))


def shifted(place, weights, own, got, own_halo, got_halo, early):
    count, energies, height, norb = own.shape
    rows = height // 2
    block = pl.BlockSpec((1, energies, rows, norb), lambda k, i, p, w: (k, 0, i, 0))
    out = jax.ShapeDtypeStruct(own.shape, jnp.bfloat16)
    return pl.pallas_call(
        shift_kernel,
        grid_spec=pltpu.PrefetchScalarGridSpec(
            num_scalar_prefetch=2,
            grid=(count, height // rows),
            in_specs=[block] * 4 + [pl.BlockSpec(memory_space=pl.ANY)],
            out_specs=[block] * 2,
        ),
        out_shape=[out, out],
        compiler_params=pltpu.CompilerParams(vmem_limit_bytes=32 * MIB),
        cost_estimate=pl.CostEstimate(
            flops=32 * count * height * norb,
            bytes_accessed=24 * count * height * norb,
            transcendentals=0,
        ),
        name="shifted",
    )(place, weights, own, got, own_halo, got_halo, early)


def identity(n):
    rows = lax.broadcasted_iota(jnp.int32, (n, n), 0)
    cols = lax.broadcasted_iota(jnp.int32, (n, n), 1)
    return (rows == cols).astype(jnp.float32).astype(jnp.bfloat16)


def fold_kernel(tiles, *refs):
    parts, (out, out_t) = refs[:4], refs[4:]
    points, height, norb = parts[0].shape
    turn = identity(norb // 2)
    for s in range(4):

        @pl.when(pl.program_id(0) == s)
        def _(part=parts[s]):
            for q in range(points):
                out[q] = part[q]
                for b in range(2):
                    span = slice(b * (norb // 2), (b + 1) * (norb // 2))
                    out_t[q, span, :] = dot_nt(turn, part[q, :, span]).astype(jnp.bfloat16)


def folded(tiles, parts):
    points, height, norb = parts[0].shape
    some = points // 4
    given = pl.BlockSpec((some, height, norb), lambda s, q, t: (q, 0, 0))
    whole = jax.ShapeDtypeStruct((points, norb, norb), jnp.bfloat16)
    return pl.pallas_call(
        fold_kernel,
        grid_spec=pltpu.PrefetchScalarGridSpec(
            num_scalar_prefetch=1,
            grid=(4, points // some),
            in_specs=[given] * 4,
            out_specs=[
                pl.BlockSpec((some, height, norb), lambda s, q, t: (q, t[s], 0)),
                pl.BlockSpec((some, norb, height), lambda s, q, t: (q, 0, t[s])),
            ],
        ),
        out_shape=[whole, whole],
        compiler_params=pltpu.CompilerParams(vmem_limit_bytes=48 * MIB),
        cost_estimate=pl.CostEstimate(
            flops=4 * points * norb**3 // 2, bytes_accessed=14 * points * norb**2, transcendentals=0
        ),
        name="fold",
    )(tiles, *parts)


def add_products(targets, picks, sources, factor, at, store):
    acc = [[None, None] for _ in range(targets)]
    for quad in range(4):
        donors = [(s, kk) for s in (2 * quad, 2 * quad + 1) for kk in range(2)]
        held = [[sources[s][kk, e, at[0], at[1]] for e in range(2)] for s, kk in donors]
        for t in range(targets):
            c = [factor[picks(t, 4 * quad + d), at[0], at[1]] for d in range(4)]
            for e in range(2):
                part = (c[0] * held[0][e] + c[1] * held[1][e]) + (
                    c[2] * held[2][e] + c[3] * held[3][e]
                )
                part = part.astype(jnp.float32)
                acc[t][e] = part if acc[t][e] is None else acc[t][e] + part
    for t in range(targets):
        for e in range(2):
            store[t, e, at[0], at[1]] = acc[t][e].astype(store.dtype)


def home_kernel(table, *refs):
    sources, (coup, coup_t, out, out_t) = refs[:8], refs[8:]
    targets, _, height, norb = out.shape

    def picks(t, d):
        return table[t * 16 + d]

    def slab(i, carry):
        at = (
            pl.ds(pl.multiple_of(i // 2 * 16, 16), 16),
            pl.ds(pl.multiple_of(i % 2 * (norb // 2), norb // 2), norb // 2),
        )
        add_products(targets, picks, sources, coup, at, out)
        add_products(targets, picks, sources, coup_t, at, out_t)
        return carry

    lax.fori_loop(0, height // 16 * 2, slab, 0)


def home_sums(table, sources, coup, coup_t, chunk, targets):
    _, _, rows, norb = sources[0].shape
    points = coup.shape[0]
    height = 128
    steps = rows // height
    given = pl.BlockSpec((2, 2, height, norb), lambda i, q: (0, 0, i, 0))
    factor = pl.BlockSpec((points, height, norb), lambda i, q: (0, chunk * steps + i, 0))
    result = pl.BlockSpec((targets, 2, height, norb), lambda i, q: (0, 0, i, 0))
    out = jax.ShapeDtypeStruct((targets, 2, rows, norb), jnp.bfloat16)
    return pl.pallas_call(
        home_kernel,
        grid_spec=pltpu.PrefetchScalarGridSpec(
            num_scalar_prefetch=1,
            grid=(steps,),
            in_specs=[given] * 8 + [factor] * 2,
            out_specs=[result] * 2,
        ),
        out_shape=[out, out],
        compiler_params=pltpu.CompilerParams(vmem_limit_bytes=48 * MIB),
        cost_estimate=pl.CostEstimate(
            flops=40 * targets * points * rows * norb,
            bytes_accessed=10 * MIB * steps,
            transcendentals=0,
        ),
        name="home",
    )(table, *sources, coup, coup_t)


def rows_kernel(tile, table, *refs):
    rows_of, cols_of = refs[:16], refs[16:32]
    coup, coup_t, out, picked, along, across = refs[32:]
    targets, _, _, height, norb = out.shape
    group = pl.program_id(0) * targets
    part = norb // CHUNKS

    for c in range(CHUNKS):

        @pl.when((pl.program_id(0) == 0) & (tile[0] // CHUNKS == c))
        def _(held=rows_of[8 * c : 8 * c + 8]):
            for s in range(8):
                picked[s] = held[s][...]

    def picks(t, d):
        return table[(group + t) * 16 + d]

    def over_rows(i, carry):
        at = (
            pl.ds(pl.multiple_of(i // 2 * 16, 16), 16),
            pl.ds(pl.multiple_of(i % 2 * (norb // 2), norb // 2), norb // 2),
        )
        add_products(targets, picks, [picked.at[s] for s in range(8)], coup, at, along)
        return carry

    lax.fori_loop(0, height // 16 * 2, over_rows, 0)
    for c in range(CHUNKS):

        def over_cols(i, carry, c=c):
            at = (pl.ds(pl.multiple_of(i * 32, 32), 32), slice(None))
            add_products(
                targets,
                picks,
                cols_of[8 * c : 8 * c + 8],
                coup_t.at[:, c * part : (c + 1) * part],
                at,
                across.at[:, :, c * part : (c + 1) * part],
            )
            return carry

        lax.fori_loop(0, part // 32, over_cols, 0)

    turn = identity(height)
    for t in range(targets):
        for e in range(2):
            u = along[t, e]
            v = dot_nt(turn, across[t, e])
            out[t, e, 0] = (u + v).astype(jnp.bfloat16)
            out[t, e, 1] = (u - v).astype(jnp.bfloat16)


def row_sums(tile, table, chunks, coup, coup_t, targets):
    _, _, part, norb = chunks[0][0].shape
    points = coup.shape[0]
    height = 128
    steps = part // height
    groups = points // targets
    row_block = pl.BlockSpec((2, 2, height, norb), lambda g, t, q: (0, 0, t[0] % steps, 0))
    col_block = pl.BlockSpec((2, 2, part, height), lambda g, t, q: (0, 0, 0, t[0]))
    sources = [x for chunk in chunks for x in chunk]
    return pl.pallas_call(
        rows_kernel,
        grid_spec=pltpu.PrefetchScalarGridSpec(
            num_scalar_prefetch=2,
            grid=(groups,),
            in_specs=[row_block] * 16
            + [col_block] * 16
            + [
                pl.BlockSpec((points, height, norb), lambda g, t, q: (0, t[0], 0)),
                pl.BlockSpec((points, norb, height), lambda g, t, q: (0, 0, t[0])),
            ],
            out_specs=pl.BlockSpec((targets, 2, 2, height, norb), lambda g, t, q: (g, 0, 0, 0, 0)),
            scratch_shapes=[
                pltpu.VMEM((8, 2, 2, height, norb), jnp.bfloat16),
                pltpu.VMEM((targets, 2, height, norb), jnp.float32),
                pltpu.VMEM((targets, 2, norb, height), jnp.bfloat16),
            ],
        ),
        out_shape=jax.ShapeDtypeStruct((points, 2, 2, height, norb), jnp.bfloat16),
        compiler_params=pltpu.CompilerParams(vmem_limit_bytes=56 * MIB),
        cost_estimate=pl.CostEstimate(
            flops=40 * points * points * height * norb,
            bytes_accessed=24 * MIB,
            transcendentals=0,
        ),
        name="rows",
    )(tile, table, *sources, *sources, coup, coup_t)


def density_kernel(inverse, green, gamma, *refs):
    us, vs, out = refs[:CHUNKS], refs[CHUNKS : 2 * CHUNKS], refs[-1]
    norb = green.shape[-1]
    part = norb // CHUNKS
    d_re = d_im = None
    for e in range(green.shape[1]):
        g_re, g_im = green[0, e, 0], green[0, e, 1]
        gam = gamma[0, e]
        wide_re, wide_im = g_re.astype(jnp.float32), g_im.astype(jnp.float32)
        less = (wide_re - wide_im).astype(jnp.bfloat16)
        more = (wide_re + wide_im).astype(jnp.bfloat16)
        u = jnp.concatenate([ref[0, e] for ref in us], axis=0)
        v = jnp.concatenate([ref[0, e] for ref in vs], axis=0)
        m_re = dot_nn(less, u) + dot_nt(more, v) + scale(g_re, gam).astype(jnp.float32)
        m_im = dot_nn(more, u) - dot_nt(less, v) + scale(g_im, gam).astype(jnp.float32)
        m_re, m_im = m_re.astype(jnp.bfloat16), m_im.astype(jnp.bfloat16)
        one = dot_nt(m_re, g_re) + dot_nt(m_im, g_im)
        two = dot_nt(m_im, g_re) - dot_nt(m_re, g_im)
        d_re = one if d_re is None else d_re + one
        d_im = two if d_im is None else d_im + two
    out[0, 0] = (d_re * inverse).astype(jnp.bfloat16)
    out[0, 1] = (d_im * inverse).astype(jnp.bfloat16)


def partial_density(green, gamma, sums, sums_t, inverse, first, count):
    _, energies, _, norb, _ = green.shape
    part = pl.BlockSpec((1, energies, norb // CHUNKS, norb), lambda k: (first + k, 0, 0, 0))
    return pl.pallas_call(
        functools.partial(density_kernel, inverse),
        grid=(count,),
        in_specs=[
            pl.BlockSpec((1, energies, 2, norb, norb), lambda k: (first + k, 0, 0, 0, 0)),
            pl.BlockSpec((1, energies, 1, norb), lambda k: (first + k, 0, 0, 0)),
        ]
        + [part] * (2 * CHUNKS),
        out_specs=pl.BlockSpec((1, 2, norb, norb), lambda k: (k, 0, 0, 0)),
        out_shape=jax.ShapeDtypeStruct((count, 2, norb, norb), jnp.bfloat16),
        compiler_params=pltpu.CompilerParams(vmem_limit_bytes=48 * MIB),
        cost_estimate=pl.CostEstimate(
            flops=16 * count * energies * norb**3,
            bytes_accessed=(8 * energies + 4) * count * norb**2,
            transcendentals=0,
        ),
        name="density",
    )(green, gamma, *sums, *sums_t)


def on_device(green, broadening, coupling, shift_steps, mode_weight, occupation, momentum_map):
    n_energy, n_mom = lax.axis_size("energy"), lax.axis_size("mom")
    pairs = n_energy // 2
    local_k = green.shape[0]
    norb = green.shape[-1]
    half = local_k // 2
    points = momentum_map.shape[1]
    energy, mom = lax.axis_index("energy"), lax.axis_index("mom")
    x_lo = energy % 2

    def flip(x, lo, mo):
        perm = [
            (e * n_mom + m, (e ^ lo) * n_mom + (m ^ mo))
            for e in range(n_energy)
            for m in range(n_mom)
        ]
        return lax.ppermute(x, BOTH, perm)

    def along_pairs(x, step_of_low):
        moves = []
        for j in range(pairs):
            for lo in range(2):
                to = j + (step_of_low if lo == 0 else -step_of_low)
                if 0 <= to < pairs:
                    moves.append((2 * j + lo, 2 * to + lo))
        return lax.ppermute(x, "energy", moves)

    def weight_of(step, factor):
        return 0.5 * jnp.sum(jnp.where(shift_steps == step, mode_weight * factor, 0.0))

    weights = jnp.stack(
        [weight_of(s, occupation + 1.0) for s in (1, 2)] + [weight_of(s, occupation) for s in (1, 2)]
    ).astype(jnp.float32)

    gamma = broadening[:, :, None, :]
    place = x_lo.astype(jnp.int32)[None]

    coup_b = flip(coupling, 1, 2)
    coup_c = flip(coupling, 0, 1)
    coup_bc = flip(coup_b, 0, 1)
    early = (coup_b, coup_bc)

    sent = [packed_lesser(1 - place, green, gamma, c) for c in range(CHUNKS)]
    got = [flip(x, 1, 0) for x in sent]
    own = [packed_lesser(place, green, gamma, c) for c in range(CHUNKS)]
    own_halo = [along_pairs(x, -1) for x in own]
    got_halo = [along_pairs(x, 1) for x in got]

    moves = [(0, 0), (1, 0), (1, 2), (0, 2)]
    moves = moves + [(lo, mo ^ 1) for lo, mo in moves]
    chunks = []
    for c in range(CHUNKS):
        mine, other = shifted(place, weights, own[c], got[c], own_halo[c], got_halo[c], early[c])
        near = [mine, flip(other, 1, 0), flip(other, 1, 2), flip(mine, 0, 2)]
        chunks.append(near + [flip(x, 0, 1) for x in near])

    tile = mom.astype(jnp.int32)
    coup, coup_t = folded(
        jnp.arange(4, dtype=jnp.int32) ^ tile, [coupling, coup_c, coup_b, coup_bc]
    )

    donors = jnp.stack(
        [(mom ^ mo) * local_k + (x_lo ^ lo) * half + kk for lo, mo in moves for kk in range(half)]
    ).astype(jnp.int32)
    table = jnp.sum(
        jnp.where(
            momentum_map[:, :, None] == donors[None, None, :],
            jnp.arange(points, dtype=jnp.int32)[None, :, None],
            0,
        ),
        axis=1,
    ).astype(jnp.int32)
    table_home = lax.dynamic_slice_in_dim(table, mom * local_k, local_k, 0).reshape(-1)

    sums = [home_sums(table_home, chunks[c], coup, coup_t, c, local_k) for c in range(CHUNKS)]
    us, vs = [s[0] for s in sums], [s[1] for s in sums]
    inverse = 1.0 / (green.shape[1] * n_energy)
    received = []
    for first in range(0, local_k, half):
        part = partial_density(green, gamma, us, vs, inverse, first, half)
        part = part.reshape(half, 2, n_energy, norb // n_energy, norb)
        received.append(lax.all_to_all(part, "energy", split_axis=2, concat_axis=2, tiled=True))
    self_energy = row_sums(tile[None], table.reshape(-1), chunks, coup, coup_t, local_k)
    summed = jnp.concatenate(
        [jnp.sum(x.astype(jnp.float32), axis=2) for x in received], axis=0
    )
    density = jnp.transpose(summed, (2, 0, 1, 3))
    return (self_energy, density)


def solution(mesh):
    return jax.shard_map(
        on_device,
        mesh=mesh,
        in_specs=(
            P("mom", "energy", None, None, None),
            P("mom", "energy", None),
            P(None, "mom", None),
            P(),
            P(),
            P(),
            P(),
        ),
        out_specs=(P(None, "energy", None, "mom", None), P("energy", "mom", None, None)),
        check_vma=False,
    )
```

```python
import functools

import jax
import jax.numpy as jnp
from jax import lax
from jax.experimental import pallas as pl
from jax.experimental.pallas import tpu as pltpu
from jax.sharding import PartitionSpec as P

CHUNKS = 2
BOTH = ("energy", "mom")
MIB = 1 << 20
LIGHT = pl.CostEstimate(flops=1, bytes_accessed=1, transcendentals=0)
NT = (((1,), (1,)), ((), ()))


def dot_nt(left, right):
    return lax.dot_general(left, right, NT, preferred_element_type=jnp.float32)


def dot_nn(left, right):
    return jnp.dot(left, right, preferred_element_type=jnp.float32)


def scale(block, gamma):
    return (block.astype(jnp.float32) * gamma).astype(jnp.bfloat16)


def lesser_kernel(chunk, half, green, gamma, out):
    rows = out.shape[2]
    span = slice(chunk * rows, (chunk + 1) * rows)
    gam = gamma[0, 0]
    wide_re = green[0, 0, 0].astype(jnp.float32)
    wide_im = green[0, 0, 1].astype(jnp.float32)
    less = (wide_re - wide_im).astype(jnp.bfloat16)
    more = (wide_re + wide_im).astype(jnp.bfloat16)
    total = dot_nt(scale(green[0, 0, 0, span], gam), less) + dot_nt(
        scale(green[0, 0, 1, span], gam), more
    )
    out[0, 0] = total.astype(jnp.bfloat16)


def packed_lesser(half, green, gamma, chunk):
    energies, norb = green.shape[1], green.shape[-1]
    count = green.shape[0] // 2
    rows = norb // CHUNKS
    return pl.pallas_call(
        functools.partial(lesser_kernel, chunk),
        grid_spec=pltpu.PrefetchScalarGridSpec(
            num_scalar_prefetch=1,
            grid=(count, energies),
            in_specs=[
                pl.BlockSpec((1, 1, 2, norb, norb), lambda k, e, h: (h[0] * count + k, e, 0, 0, 0)),
                pl.BlockSpec((1, 1, 1, norb), lambda k, e, h: (h[0] * count + k, e, 0, 0)),
            ],
            out_specs=pl.BlockSpec((1, 1, rows, norb), lambda k, e, h: (k, e, 0, 0)),
        ),
        out_shape=jax.ShapeDtypeStruct((count, energies, rows, norb), jnp.bfloat16),
        compiler_params=pltpu.CompilerParams(vmem_limit_bytes=32 * MIB),
        cost_estimate=LIGHT,
        name="lesser",
    )(half, green, gamma)


def shift_kernel(place, weights, own, got, own_halo, got_halo, early, *outs):
    rows = own.shape[2]
    step = 16

    def run(first, second, third, fourth, outs):
        def slab(i, carry):
            at = pl.ds(pl.multiple_of(i * step, step), step)
            levels = [
                ref[0, e, at, :].astype(jnp.float32)
                for ref in (first, second, third, fourth)
                for e in range(2)
            ]
            for o in range(4):
                total = weights[0] * levels[o + 3] + weights[1] * levels[o + 4]
                total = total + weights[2] * levels[o + 1] + weights[3] * levels[o]
                outs[o][0, at, :] = total.astype(jnp.bfloat16)
            return carry

        lax.fori_loop(0, rows // step, slab, 0)

    @pl.when(place[0] == 0)
    def _():
        run(got_halo, own, got, own_halo, outs)

    @pl.when(place[0] != 0)
    def _():
        run(own_halo, got, own, got_halo, outs[2:] + outs[:2])


def shifted(place, weights, own, got, own_halo, got_halo, early):
    count, energies, height, norb = own.shape
    rows = height // 2
    block = pl.BlockSpec((1, energies, rows, norb), lambda k, i, p, w: (k, 0, i, 0))
    result = pl.BlockSpec((1, rows, norb), lambda k, i, p, w: (k, i, 0))
    out = jax.ShapeDtypeStruct((count, height, norb), own.dtype)
    return pl.pallas_call(
        shift_kernel,
        grid_spec=pltpu.PrefetchScalarGridSpec(
            num_scalar_prefetch=2,
            grid=(count, height // rows),
            in_specs=[block] * 4 + [pl.BlockSpec(memory_space=pl.ANY)],
            out_specs=[result] * 4,
        ),
        out_shape=[out] * 4,
        compiler_params=pltpu.CompilerParams(vmem_limit_bytes=32 * MIB),
        cost_estimate=LIGHT,
        name="shifted",
    )(place, weights, own, got, own_halo, got_halo, early)


def held_back(arrays, waited):
    return pl.pallas_call(
        lambda *refs: None,
        in_specs=[pl.BlockSpec(memory_space=pl.ANY)] * (len(arrays) + len(waited)),
        out_specs=[pl.BlockSpec(memory_space=pl.ANY)] * len(arrays),
        out_shape=[jax.ShapeDtypeStruct(x.shape, x.dtype) for x in arrays],
        input_output_aliases={i: i for i in range(len(arrays))},
        cost_estimate=LIGHT,
        name="held_back",
    )(*arrays, *waited)


def identity(n):
    rows = lax.broadcasted_iota(jnp.int32, (n, n), 0)
    cols = lax.broadcasted_iota(jnp.int32, (n, n), 1)
    return (rows == cols).astype(jnp.float32).astype(jnp.bfloat16)


def fold_kernel(tiles, *refs):
    parts, (out, out_t) = refs[:4], refs[4:]
    points, height, norb = parts[0].shape
    turn = identity(norb // 2)
    for s in range(4):

        @pl.when(pl.program_id(0) == s)
        def _(part=parts[s]):
            for q in range(points):
                out[q] = part[q]
                for b in range(2):
                    span = slice(b * (norb // 2), (b + 1) * (norb // 2))
                    out_t[q, span, :] = dot_nt(turn, part[q, :, span]).astype(jnp.bfloat16)


def folded(tiles, parts):
    points, height, norb = parts[0].shape
    some = points // 4
    given = pl.BlockSpec((some, height, norb), lambda s, q, t: (q, 0, 0))
    whole = jax.ShapeDtypeStruct((points, norb, norb), jnp.bfloat16)
    return pl.pallas_call(
        fold_kernel,
        grid_spec=pltpu.PrefetchScalarGridSpec(
            num_scalar_prefetch=1,
            grid=(4, points // some),
            in_specs=[given] * 4,
            out_specs=[
                pl.BlockSpec((some, height, norb), lambda s, q, t: (q, t[s], 0)),
                pl.BlockSpec((some, norb, height), lambda s, q, t: (q, 0, t[s])),
            ],
        ),
        out_shape=[whole, whole],
        compiler_params=pltpu.CompilerParams(vmem_limit_bytes=48 * MIB),
        cost_estimate=LIGHT,
        name="fold",
    )(tiles, *parts)


def add_products(targets, streams, picks, donor, factor, at, store):
    acc = [[None] * streams for _ in range(targets)]
    kept = {}
    for quad in range(4):
        held = [[donor(4 * quad + d, n, at) for n in range(streams)] for d in range(4)]
        for t in range(targets):
            c = [factor[picks(t, 4 * quad + d), at[0], at[1]] for d in range(4)]
            for n in range(streams):
                part = (c[0] * held[0][n] + c[1] * held[1][n]) + (
                    c[2] * held[2][n] + c[3] * held[3][n]
                )
                if quad % 2 == 0:
                    kept[t, n] = part
                    continue
                part = (kept.pop((t, n)) + part).astype(jnp.float32)
                acc[t][n] = part if acc[t][n] is None else acc[t][n] + part
    for t in range(targets):
        for n in range(streams):
            store(t, n, at, acc[t][n])


def home_kernel(table, *refs):
    sources, (coup, coup_t, out, out_t) = refs[:8], refs[8:]
    targets, height, norb = out.shape

    def picks(t, d):
        return table[t * 16 + d]

    def donor(d, n, at):
        return sources[d // 2][d % 2, at[0], at[1]]

    def into(ref):
        def store(t, n, at, value):
            ref[t, at[0], at[1]] = value.astype(jnp.bfloat16)

        return store

    def slab(i, carry):
        at = (pl.ds(pl.multiple_of(i * 16, 16), 16), slice(None))
        add_products(targets, 1, picks, donor, coup, at, into(out))
        add_products(targets, 1, picks, donor, coup_t, at, into(out_t))
        return carry

    lax.fori_loop(0, height // 16, slab, 0)


def home_sums(table, sources, coup, coup_t, chunk, targets):
    _, rows, norb = sources[0].shape
    points = coup.shape[0]
    height = 64
    steps = rows // height
    given = pl.BlockSpec((2, height, norb), lambda i, q: (0, i, 0))
    factor = pl.BlockSpec((points, height, norb), lambda i, q: (0, chunk * steps + i, 0))
    result = pl.BlockSpec((targets, height, norb), lambda i, q: (0, i, 0))
    out = jax.ShapeDtypeStruct((targets, rows, norb), jnp.bfloat16)
    return pl.pallas_call(
        home_kernel,
        grid_spec=pltpu.PrefetchScalarGridSpec(
            num_scalar_prefetch=1,
            grid=(steps,),
            in_specs=[given] * 8 + [factor] * 2,
            out_specs=[result] * 2,
        ),
        out_shape=[out, out],
        compiler_params=pltpu.CompilerParams(vmem_limit_bytes=32 * MIB),
        cost_estimate=LIGHT,
        name="home",
    )(table, *sources, coup, coup_t)


def rows_kernel(tile, table, *refs):
    rows_of, cols_of = refs[:16], refs[16:32]
    coup, out, source = refs[32], refs[-2], refs[-1]
    targets, _, _, height, norb = out.shape
    group = pl.program_id(0) * targets
    part = norb // CHUNKS

    for c in range(CHUNKS):

        @pl.when((pl.program_id(0) == 0) & (tile[0] // CHUNKS == c))
        def _(held=rows_of[8 * c : 8 * c + 8]):
            turn = identity(height)

            for d in range(16):
                for b in range(CHUNKS):
                    span = slice(b * part, (b + 1) * part)
                    straight = held[d // 2][d % 2, :, span].astype(jnp.float32)
                    turned = turn_over(turn, cols_of[8 * b + d // 2][d % 2])
                    source[d, 0, :, span] = (straight + turned).astype(jnp.bfloat16)
                    source[d, 1, :, span] = (straight - turned).astype(jnp.bfloat16)

    def picks(t, d):
        return table[(group + t) * 16 + d]

    def donor(d, n, at):
        return source[d, n, at[0], at[1]]

    def store(t, n, at, value):
        out[t, 0, n, at[0], at[1]] = value.astype(jnp.bfloat16)

    def slab(i, carry):
        at = (
            pl.ds(pl.multiple_of(i // 2 * 16, 16), 16),
            pl.ds(pl.multiple_of(i % 2 * (norb // 2), norb // 2), norb // 2),
        )
        add_products(targets, 2, picks, donor, coup, at, store)
        return carry

    lax.fori_loop(0, height // 16 * 2, slab, 0)


def turn_over(turn, block):
    return dot_nt(turn, block)


def row_sums(tile, table, chunks, coupling, targets, energy, before):
    _, part, norb = chunks[0][0].shape
    points, height, _ = coupling.shape
    steps = part // height
    row_block = pl.BlockSpec((2, height, norb), lambda g, t, q: (0, t[0] % steps, 0))
    col_block = pl.BlockSpec((2, part, height), lambda g, t, q: (0, 0, t[0]))
    sources = [x for chunk in chunks for x in chunk]
    out = jax.ShapeDtypeStruct((points, 2, 2, height, norb), jnp.bfloat16)
    given = [tile, table, *sources, *sources, coupling] + ([] if before is None else [before])
    return pl.pallas_call(
        rows_kernel,
        grid_spec=pltpu.PrefetchScalarGridSpec(
            num_scalar_prefetch=2,
            grid=(points // targets,),
            in_specs=[row_block] * 16
            + [col_block] * 16
            + [pl.BlockSpec((points, height, norb), lambda g, t, q: (0, 0, 0))]
            + ([] if before is None else [pl.BlockSpec(memory_space=pl.ANY)]),
            out_specs=pl.BlockSpec(
                (targets, 1, 2, height, norb), lambda g, t, q: (g, energy, 0, 0, 0)
            ),
            scratch_shapes=[pltpu.VMEM((16, 2, height, norb), jnp.bfloat16)],
        ),
        out_shape=out,
        input_output_aliases={} if before is None else {len(given) - 1: 0},
        compiler_params=pltpu.CompilerParams(vmem_limit_bytes=40 * MIB),
        cost_estimate=LIGHT,
        name="rows",
    )(*given)


def density_kernel(inverse, green, gamma, *refs):
    us, vs, rest = refs[:CHUNKS], refs[CHUNKS : 2 * CHUNKS], refs[2 * CHUNKS :]
    g_re, g_im = green[0, 0, 0], green[0, 0, 1]
    gam = gamma[0, 0]
    wide_re, wide_im = g_re.astype(jnp.float32), g_im.astype(jnp.float32)
    less = (wide_re - wide_im).astype(jnp.bfloat16)
    more = (wide_re + wide_im).astype(jnp.bfloat16)
    u = jnp.concatenate([ref[0] for ref in us], axis=0)
    v = jnp.concatenate([ref[0] for ref in vs], axis=0)
    m_re = dot_nn(less, u) + dot_nt(more, v) + scale(g_re, gam).astype(jnp.float32)
    m_im = dot_nn(more, u) - dot_nt(less, v) + scale(g_im, gam).astype(jnp.float32)
    m_re, m_im = m_re.astype(jnp.bfloat16), m_im.astype(jnp.bfloat16)
    d_re = dot_nt(m_re, g_re) + dot_nt(m_im, g_im)
    d_im = dot_nt(m_im, g_re) - dot_nt(m_re, g_im)
    out = rest[-1]
    if len(rest) == 1:
        out[0, 0] = d_re
        out[0, 1] = d_im
    else:
        shape = out.shape[2:]
        out[0, 0] = ((d_re + rest[0][0, 0]) * inverse).astype(jnp.bfloat16).reshape(shape)
        out[0, 1] = ((d_im + rest[0][0, 1]) * inverse).astype(jnp.bfloat16).reshape(shape)


def partial_density(green, gamma, sums, sums_t, energy, before, inverse, owners):
    count, _, _, norb, _ = green.shape
    part = pl.BlockSpec((1, norb // CHUNKS, norb), lambda k: (k, 0, 0))
    whole = pl.BlockSpec((1, 2, norb, norb), lambda k: (k, 0, 0, 0))
    if before is None:
        out_spec = whole
        out = jax.ShapeDtypeStruct((count, 2, norb, norb), jnp.float32)
    else:
        rows = norb // owners
        out_spec = pl.BlockSpec((1, 2, owners, rows, norb), lambda k: (k, 0, 0, 0, 0))
        out = jax.ShapeDtypeStruct((count, 2, owners, rows, norb), jnp.bfloat16)
    return pl.pallas_call(
        functools.partial(density_kernel, inverse),
        grid=(count,),
        in_specs=[
            pl.BlockSpec((1, 1, 2, norb, norb), lambda k: (k, energy, 0, 0, 0)),
            pl.BlockSpec((1, 1, 1, norb), lambda k: (k, energy, 0, 0)),
        ]
        + [part] * (2 * CHUNKS)
        + ([] if before is None else [whole]),
        out_specs=out_spec,
        out_shape=out,
        compiler_params=pltpu.CompilerParams(vmem_limit_bytes=40 * MIB),
        cost_estimate=LIGHT,
        name="density",
    )(green, gamma, *sums, *sums_t, *([] if before is None else [before]))


def on_device(green, broadening, coupling, shift_steps, mode_weight, occupation, momentum_map):
    n_energy, n_mom = lax.axis_size("energy"), lax.axis_size("mom")
    pairs = n_energy // 2
    local_k, local_e = green.shape[:2]
    half = local_k // 2
    points = momentum_map.shape[1]
    energy, mom = lax.axis_index("energy"), lax.axis_index("mom")
    x_lo = energy % 2

    def flip(x, lo, mo):
        perm = [
            (e * n_mom + m, (e ^ lo) * n_mom + (m ^ mo))
            for e in range(n_energy)
            for m in range(n_mom)
        ]
        return lax.ppermute(x, BOTH, perm)

    def along_pairs(x, step_of_low):
        moves = []
        for j in range(pairs):
            for lo in range(2):
                to = j + (step_of_low if lo == 0 else -step_of_low)
                if 0 <= to < pairs:
                    moves.append((2 * j + lo, 2 * to + lo))
        return lax.ppermute(x, "energy", moves)

    def weight_of(step, factor):
        return 0.5 * jnp.sum(jnp.where(shift_steps == step, mode_weight * factor, 0.0))

    weights = jnp.stack(
        [weight_of(s, occupation + 1.0) for s in (1, 2)] + [weight_of(s, occupation) for s in (1, 2)]
    ).astype(jnp.float32)

    gamma = broadening[:, :, None, :]
    place = x_lo.astype(jnp.int32)[None]
    tile = mom.astype(jnp.int32)

    moves = [(0, 0), (1, 0), (1, 2), (0, 2)]
    moves = moves + [(lo, mo ^ 1) for lo, mo in moves]
    donors = jnp.stack(
        [(mom ^ mo) * local_k + (x_lo ^ lo) * half + kk for lo, mo in moves for kk in range(half)]
    ).astype(jnp.int32)
    table = jnp.sum(
        jnp.where(
            momentum_map[:, :, None] == donors[None, None, :],
            jnp.arange(points, dtype=jnp.int32)[None, :, None],
            0,
        ),
        axis=1,
    ).astype(jnp.int32)
    table_home = lax.dynamic_slice_in_dim(table, mom * local_k, local_k, 0).reshape(-1)

    coup_b = flip(coupling, 1, 2)
    coup_c = flip(coupling, 0, 1)

    sent = [packed_lesser(1 - place, green, gamma, c) for c in range(CHUNKS)]
    got = [flip(x, 1, 0) for x in sent]
    own = [packed_lesser(place, green, gamma, c) for c in range(CHUNKS)]
    own_halo = [along_pairs(x, -1) for x in own]
    got_halo = [along_pairs(x, 1) for x in got]
    (coup_b,) = held_back([coup_b], [got[1], own[1]])
    coup_bc = flip(coup_b, 0, 1)

    coup, coup_t = folded(
        jnp.arange(4, dtype=jnp.int32) ^ tile, [coupling, coup_c, coup_b, coup_bc]
    )
    early = (coup_bc, coup_t)
    near = [[None] * CHUNKS for _ in range(local_e)]
    for c in range(CHUNKS):
        mine_other = shifted(place, weights, own[c], got[c], own_halo[c], got_halo[c], early[c])
        for e in range(local_e):
            mine, other = mine_other[e], mine_other[2 + e]
            near[e][c] = [mine, flip(other, 1, 0), flip(other, 1, 2), flip(mine, 0, 2)]
        last = mine

    def with_other_core(block, waited):
        block = block[:1] + list(held_back(block[1:], waited))
        return block + [flip(x, 0, 1) for x in block]

    def sums_of(block, c):
        return home_sums(table_home, block, coup, coup_t, c, local_k)

    inverse = 1.0 / (local_e * n_energy)

    def density_of(sums, e, before):
        us, vs = [s[0] for s in sums], [s[1] for s in sums]
        return partial_density(green, gamma, us, vs, e, before, inverse, n_energy)

    def rows_at(chunks, e, before):
        return row_sums(tile[None], table.reshape(-1), chunks, coupling, local_k, e, before)

    first = [with_other_core(near[0][c], [last]) for c in range(CHUNKS)]
    sums = [sums_of(first[c], c) for c in range(CHUNKS)]
    density = density_of(sums, 0, None)
    self_energy = rows_at(first, 0, None)

    second, sums = [], []
    waited = [density]
    for c in range(CHUNKS):
        second.append(with_other_core(near[1][c], waited))
        sums.append(sums_of(second[c], c))
        waited = [sums[c][0], self_energy]
    density = density_of(sums, 1, density)
    parts = lax.all_to_all(density, "energy", split_axis=2, concat_axis=2, tiled=True)
    self_energy = rows_at(second, 1, self_energy)
    density = jnp.transpose(jnp.sum(parts.astype(jnp.float32), axis=2), (2, 0, 1, 3))
    return (self_energy, density)


def solution(mesh):
    return jax.shard_map(
        on_device,
        mesh=mesh,
        in_specs=(
            P("mom", "energy", None, None, None),
            P("mom", "energy", None),
            P(None, "mom", None),
            P(),
            P(),
            P(),
            P(),
        ),
        out_specs=(P(None, "energy", None, "mom", None), P("energy", "mom", None, None)),
        check_vma=False,
    )
```

```python
import functools

import jax
import jax.numpy as jnp
from jax import lax
from jax.experimental import pallas as pl
from jax.experimental.pallas import tpu as pltpu
from jax.sharding import PartitionSpec as P

CHUNKS = 2
BOTH = ("energy", "mom")
MIB = 1 << 20
NT = (((1,), (1,)), ((), ()))


def dot_nt(left, right):
    return lax.dot_general(left, right, NT, preferred_element_type=jnp.float32)


def dot_nn(left, right):
    return jnp.dot(left, right, preferred_element_type=jnp.float32)


def scale(block, gamma):
    return (block.astype(jnp.float32) * gamma).astype(jnp.bfloat16)


def lesser_kernel(place, green, gamma, *outs):
    norb = green.shape[-1]
    rows = norb // CHUNKS
    gam = gamma[0, 0]
    g_re, g_im = green[0, 0, 0], green[0, 0, 1]
    wide_re = g_re.astype(jnp.float32)
    wide_im = g_im.astype(jnp.float32)
    less = (wide_re - wide_im).astype(jnp.bfloat16)
    more = (wide_re + wide_im).astype(jnp.bfloat16)
    total = dot_nt(scale(g_re, gam), less) + dot_nt(scale(g_im, gam), more)
    total = total.astype(jnp.bfloat16)
    for side in range(2):

        @pl.when(pl.program_id(0) // 2 == side)
        def _():
            for c in range(CHUNKS):
                outs[side * CHUNKS + c][0, 0] = total[c * rows : (c + 1) * rows]


def packed_lesser(place, green, gamma):
    energies, norb = green.shape[1], green.shape[-1]
    half = green.shape[0] // 2
    rows = norb // CHUNKS

    def which(k, p):
        return ((p[0] + 1 + k // half) % 2) * half + k % half

    def block_of(side):
        def index(k, e, p):
            if side == 0:
                return (jnp.minimum(k, half - 1), jnp.where(k < half, e, energies - 1), 0, 0)
            return (jnp.maximum(k - half, 0), jnp.where(k < half, 0, e), 0, 0)

        return pl.BlockSpec((1, 1, rows, norb), index)

    out = jax.ShapeDtypeStruct((half, energies, rows, norb), jnp.bfloat16)
    outs = pl.pallas_call(
        lesser_kernel,
        grid_spec=pltpu.PrefetchScalarGridSpec(
            num_scalar_prefetch=1,
            grid=(2 * half, energies),
            in_specs=[
                pl.BlockSpec((1, 1, 2, norb, norb), lambda k, e, p: (which(k, p), e, 0, 0, 0)),
                pl.BlockSpec((1, 1, 1, norb), lambda k, e, p: (which(k, p), e, 0, 0)),
            ],
            out_specs=[block_of(0)] * CHUNKS + [block_of(1)] * CHUNKS,
        ),
        out_shape=[out] * (2 * CHUNKS),
        compiler_params=pltpu.CompilerParams(vmem_limit_bytes=60 * MIB),
        cost_estimate=pl.CostEstimate(
            flops=8 * half * energies * norb**3,
            bytes_accessed=12 * half * energies * norb**2,
            transcendentals=0,
        ),
        name="lesser",
    )(place, green, gamma)
    return outs[:CHUNKS], outs[CHUNKS:]


def shift_kernel(place, weights, own, got, own_halo, got_halo, early, out_own, out_other):
    rows = own.shape[2]
    step = 16

    def run(first, second, third, fourth, outs):
        def slab(i, carry):
            at = pl.ds(pl.multiple_of(i * step, step), step)
            levels = [
                ref[0, e, at, :].astype(jnp.float32)
                for ref in (first, second, third, fourth)
                for e in range(2)
            ]
            for o in range(4):
                total = weights[0] * levels[o + 3] + weights[1] * levels[o + 4]
                total = total + weights[2] * levels[o + 1] + weights[3] * levels[o]
                outs[o // 2][0, o % 2, at, :] = total.astype(jnp.bfloat16)
            return carry

        lax.fori_loop(0, rows // step, slab, 0)

    @pl.when(place[0] == 0)
    def _():
        run(got_halo, own, got, own_halo, (out_own, out_other))

    @pl.when(place[0] != 0)
    def _():
        run(own_halo, got, own, got_halo, (out_other, out_own))


def shifted(place, weights, own, got, own_halo, got_halo, early):
    count, energies, height, norb = own.shape
    rows = height // 2
    block = pl.BlockSpec((1, energies, rows, norb), lambda k, i, p, w: (k, 0, i, 0))
    out = jax.ShapeDtypeStruct(own.shape, jnp.bfloat16)
    return pl.pallas_call(
        shift_kernel,
        grid_spec=pltpu.PrefetchScalarGridSpec(
            num_scalar_prefetch=2,
            grid=(count, height // rows),
            in_specs=[block] * 4 + [pl.BlockSpec(memory_space=pl.ANY)],
            out_specs=[block] * 2,
        ),
        out_shape=[out, out],
        compiler_params=pltpu.CompilerParams(vmem_limit_bytes=32 * MIB),
        cost_estimate=pl.CostEstimate(
            flops=32 * count * height * norb,
            bytes_accessed=24 * count * height * norb,
            transcendentals=0,
        ),
        name="shifted",
    )(place, weights, own, got, own_halo, got_halo, early)


def held_back(arrays, waited):
    return pl.pallas_call(
        lambda *refs: None,
        in_specs=[pl.BlockSpec(memory_space=pltpu.HBM)] * (len(arrays) + len(waited)),
        out_specs=[pl.BlockSpec(memory_space=pltpu.HBM)] * len(arrays),
        out_shape=[jax.ShapeDtypeStruct(x.shape, x.dtype) for x in arrays],
        input_output_aliases={i: i for i in range(len(arrays))},
        compiler_params=pltpu.CompilerParams(vmem_limit_bytes=60 * MIB),
        name="held_back",
    )(*arrays, *waited)


def identity(n):
    rows = lax.broadcasted_iota(jnp.int32, (n, n), 0)
    cols = lax.broadcasted_iota(jnp.int32, (n, n), 1)
    return (rows == cols).astype(jnp.float32).astype(jnp.bfloat16)


def fold_kernel(tiles, *refs):
    parts, (out, out_t) = refs[:4], refs[4:]
    points, height, norb = parts[0].shape
    turn = identity(norb // 2)
    for s in range(4):

        @pl.when(pl.program_id(0) == s)
        def _(part=parts[s]):
            for q in range(points):
                out[q] = part[q]
                for b in range(2):
                    span = slice(b * (norb // 2), (b + 1) * (norb // 2))
                    out_t[q, span, :] = dot_nt(turn, part[q, :, span]).astype(jnp.bfloat16)


def folded(tiles, parts):
    points, height, norb = parts[0].shape
    some = points // 4
    given = pl.BlockSpec((some, height, norb), lambda s, q, t: (q, 0, 0))
    whole = jax.ShapeDtypeStruct((points, norb, norb), jnp.bfloat16)
    return pl.pallas_call(
        fold_kernel,
        grid_spec=pltpu.PrefetchScalarGridSpec(
            num_scalar_prefetch=1,
            grid=(4, points // some),
            in_specs=[given] * 4,
            out_specs=[
                pl.BlockSpec((some, height, norb), lambda s, q, t: (q, t[s], 0)),
                pl.BlockSpec((some, norb, height), lambda s, q, t: (q, 0, t[s])),
            ],
        ),
        out_shape=[whole, whole],
        compiler_params=pltpu.CompilerParams(vmem_limit_bytes=60 * MIB),
        cost_estimate=pl.CostEstimate(
            flops=4 * points * norb**3 // 2, bytes_accessed=14 * points * norb**2, transcendentals=0
        ),
        name="fold",
    )(tiles, *parts)


def add_products(targets, streams, picks, donor, factor, at, store):
    acc = [[None] * streams for _ in range(targets)]
    kept = {}
    for quad in range(4):
        held = [[donor(4 * quad + d, n, at) for n in range(streams)] for d in range(4)]
        for t in range(targets):
            c = [factor[picks(t, 4 * quad + d), at[0], at[1]] for d in range(4)]
            for n in range(streams):
                part = (c[0] * held[0][n] + c[1] * held[1][n]) + (
                    c[2] * held[2][n] + c[3] * held[3][n]
                )
                if quad % 2 == 0:
                    kept[t, n] = part
                    continue
                part = (kept.pop((t, n)) + part).astype(jnp.float32)
                acc[t][n] = part if acc[t][n] is None else acc[t][n] + part
    for t in range(targets):
        for n in range(streams):
            store(t, n, at, acc[t][n])


def home_kernel(table, *refs):
    sources, (coup, coup_t, out, out_t) = refs[:8], refs[8:]
    targets, _, height, norb = out.shape

    def picks(t, d):
        return table[t * 16 + d]

    def donor(d, n, at):
        return sources[d // 2][d % 2, n, at[0], at[1]]

    def into(ref):
        def store(t, n, at, value):
            ref[t, n, at[0], at[1]] = value.astype(jnp.bfloat16)

        return store

    def slab(i, carry):
        at = (
            pl.ds(pl.multiple_of(i // 2 * 16, 16), 16),
            pl.ds(pl.multiple_of(i % 2 * (norb // 2), norb // 2), norb // 2),
        )
        add_products(targets, 2, picks, donor, coup, at, into(out))
        add_products(targets, 2, picks, donor, coup_t, at, into(out_t))
        return carry

    lax.fori_loop(0, height // 16 * 2, slab, 0)


def home_sums(table, sources, coup, coup_t, chunk, targets):
    _, _, rows, norb = sources[0].shape
    points = coup.shape[0]
    height = 64
    steps = rows // height
    given = pl.BlockSpec((2, 2, height, norb), lambda i, q: (0, 0, i, 0))
    factor = pl.BlockSpec((points, height, norb), lambda i, q: (0, chunk * steps + i, 0))
    result = pl.BlockSpec((targets, 2, height, norb), lambda i, q: (0, 0, i, 0))
    out = jax.ShapeDtypeStruct((targets, 2, rows, norb), jnp.bfloat16)
    return pl.pallas_call(
        home_kernel,
        grid_spec=pltpu.PrefetchScalarGridSpec(
            num_scalar_prefetch=1,
            grid=(steps,),
            in_specs=[given] * 8 + [factor] * 2,
            out_specs=[result] * 2,
        ),
        out_shape=[out, out],
        compiler_params=pltpu.CompilerParams(vmem_limit_bytes=60 * MIB),
        cost_estimate=pl.CostEstimate(
            flops=20 * targets * points * rows * norb,
            bytes_accessed=12 * MIB,
            transcendentals=0,
        ),
        name="home",
    )(table, *sources, coup, coup_t)


def rows_kernel(tile, table, *refs):
    rows_of, cols_of = refs[:16], refs[16:32]
    coup, out, source = refs[32], refs[-2], refs[-1]
    targets, _, _, height, norb = out.shape
    group = pl.program_id(1) * targets
    part = norb // CHUNKS

    for c in range(CHUNKS):

        @pl.when((pl.program_id(1) == 0) & (tile[0] // CHUNKS == c))
        def _(held=rows_of[8 * c : 8 * c + 8]):
            turn = identity(height)

            for d in range(16):
                for b in range(CHUNKS):
                    span = slice(b * part, (b + 1) * part)
                    straight = held[d // 2][d % 2, 0, :, span].astype(jnp.float32)
                    turned = turn_over(turn, cols_of[8 * b + d // 2][d % 2, 0])
                    source[d, 0, :, span] = (straight + turned).astype(jnp.bfloat16)
                    source[d, 1, :, span] = (straight - turned).astype(jnp.bfloat16)

    def picks(t, d):
        return table[(group + t) * 16 + d]

    def donor(d, n, at):
        return source[d, n, at[0], at[1]]

    def store(t, n, at, value):
        out[t, 0, n, at[0], at[1]] = value.astype(jnp.bfloat16)

    def slab(i, carry):
        at = (
            pl.ds(pl.multiple_of(i // 2 * 16, 16), 16),
            pl.ds(pl.multiple_of(i % 2 * (norb // 2), norb // 2), norb // 2),
        )
        add_products(targets, 2, picks, donor, coup, at, store)
        return carry

    lax.fori_loop(0, height // 16 * 2, slab, 0)


def turn_over(turn, block):
    return dot_nt(turn, block)


def row_sums(tile, table, chunks, coupling, targets):
    _, energies, part, norb = chunks[0][0].shape
    points, height, _ = coupling.shape
    steps = part // height
    row_block = pl.BlockSpec((2, 1, height, norb), lambda e, g, t, q: (0, e, t[0] % steps, 0))
    col_block = pl.BlockSpec((2, 1, part, height), lambda e, g, t, q: (0, e, 0, t[0]))
    sources = [x for chunk in chunks for x in chunk]
    return pl.pallas_call(
        rows_kernel,
        grid_spec=pltpu.PrefetchScalarGridSpec(
            num_scalar_prefetch=2,
            grid=(energies, points // targets),
            in_specs=[row_block] * 16
            + [col_block] * 16
            + [pl.BlockSpec((points, height, norb), lambda e, g, t, q: (0, 0, 0))],
            out_specs=pl.BlockSpec(
                (targets, 1, 2, height, norb), lambda e, g, t, q: (g, e, 0, 0, 0)
            ),
            scratch_shapes=[pltpu.VMEM((16, 2, height, norb), jnp.bfloat16)],
        ),
        out_shape=jax.ShapeDtypeStruct((points, energies, 2, height, norb), jnp.bfloat16),
        compiler_params=pltpu.CompilerParams(vmem_limit_bytes=60 * MIB),
        cost_estimate=pl.CostEstimate(
            flops=40 * points * points * height * norb,
            bytes_accessed=24 * MIB,
            transcendentals=0,
        ),
        name="rows",
    )(tile, table, *sources, *sources, coupling)


def density_kernel(inverse, green, gamma, *refs):
    us, vs, out = refs[:CHUNKS], refs[CHUNKS : 2 * CHUNKS], refs[-1]
    norb = green.shape[-1]
    part = norb // CHUNKS
    d_re = d_im = None
    for e in range(green.shape[1]):
        g_re, g_im = green[0, e, 0], green[0, e, 1]
        gam = gamma[0, e]
        wide_re, wide_im = g_re.astype(jnp.float32), g_im.astype(jnp.float32)
        less = (wide_re - wide_im).astype(jnp.bfloat16)
        more = (wide_re + wide_im).astype(jnp.bfloat16)
        u = jnp.concatenate([ref[0, e] for ref in us], axis=0)
        v = jnp.concatenate([ref[0, e] for ref in vs], axis=0)
        m_re = dot_nn(less, u) + dot_nt(more, v) + scale(g_re, gam).astype(jnp.float32)
        m_im = dot_nn(more, u) - dot_nt(less, v) + scale(g_im, gam).astype(jnp.float32)
        m_re, m_im = m_re.astype(jnp.bfloat16), m_im.astype(jnp.bfloat16)
        one = dot_nt(m_re, g_re) + dot_nt(m_im, g_im)
        two = dot_nt(m_im, g_re) - dot_nt(m_re, g_im)
        d_re = one if d_re is None else d_re + one
        d_im = two if d_im is None else d_im + two
    out[0, 0] = (d_re * inverse).astype(jnp.bfloat16)
    out[0, 1] = (d_im * inverse).astype(jnp.bfloat16)


def partial_density(green, gamma, sums, sums_t, inverse, first, count):
    _, energies, _, norb, _ = green.shape
    part = pl.BlockSpec((1, energies, norb // CHUNKS, norb), lambda k: (first + k, 0, 0, 0))
    return pl.pallas_call(
        functools.partial(density_kernel, inverse),
        grid=(count,),
        in_specs=[
            pl.BlockSpec((1, energies, 2, norb, norb), lambda k: (first + k, 0, 0, 0, 0)),
            pl.BlockSpec((1, energies, 1, norb), lambda k: (first + k, 0, 0, 0)),
        ]
        + [part] * (2 * CHUNKS),
        out_specs=pl.BlockSpec((1, 2, norb, norb), lambda k: (k, 0, 0, 0)),
        out_shape=jax.ShapeDtypeStruct((count, 2, norb, norb), jnp.bfloat16),
        compiler_params=pltpu.CompilerParams(vmem_limit_bytes=60 * MIB),
        cost_estimate=pl.CostEstimate(
            flops=16 * count * energies * norb**3,
            bytes_accessed=(8 * energies + 4) * count * norb**2,
            transcendentals=0,
        ),
        name="density",
    )(green, gamma, *sums, *sums_t)


def on_device(green, broadening, coupling, shift_steps, mode_weight, occupation, momentum_map):
    n_energy, n_mom = lax.axis_size("energy"), lax.axis_size("mom")
    pairs = n_energy // 2
    local_k = green.shape[0]
    norb = green.shape[-1]
    half = local_k // 2
    points = momentum_map.shape[1]
    energy, mom = lax.axis_index("energy"), lax.axis_index("mom")
    x_lo = energy % 2

    def flip(x, lo, mo):
        perm = [
            (e * n_mom + m, (e ^ lo) * n_mom + (m ^ mo))
            for e in range(n_energy)
            for m in range(n_mom)
        ]
        return lax.ppermute(x, BOTH, perm)

    def along_pairs(x, step_of_low):
        moves = []
        for j in range(pairs):
            for lo in range(2):
                to = j + (step_of_low if lo == 0 else -step_of_low)
                if 0 <= to < pairs:
                    moves.append((2 * j + lo, 2 * to + lo))
        return lax.ppermute(x, "energy", moves)

    def weight_of(step, factor):
        return 0.5 * jnp.sum(jnp.where(shift_steps == step, mode_weight * factor, 0.0))

    weights = jnp.stack(
        [weight_of(s, occupation + 1.0) for s in (1, 2)] + [weight_of(s, occupation) for s in (1, 2)]
    ).astype(jnp.float32)

    gamma = broadening[:, :, None, :]
    place = x_lo.astype(jnp.int32)[None]

    coup_b = flip(coupling, 1, 2)
    coup_c = flip(coupling, 0, 1)

    sent, own = packed_lesser(place, green, gamma)
    got = [flip(x, 1, 0) for x in sent]
    own_halo = [along_pairs(x, -1) for x in own]
    got_halo = [along_pairs(x, 1) for x in got]
    (coup_o,) = held_back([coup_b], [got[1], got_halo[0]])
    coup_bc = flip(coup_o, 0, 1)

    tile = mom.astype(jnp.int32)
    coup, coup_t = folded(
        jnp.arange(4, dtype=jnp.int32) ^ tile, [coupling, coup_c, coup_o, coup_bc]
    )
    early = (coup_b, coup_t)
    moves = [(0, 0), (1, 0), (1, 2), (0, 2)]
    moves = moves + [(lo, mo ^ 1) for lo, mo in moves]
    near = []
    for c in range(CHUNKS):
        mine, other = shifted(place, weights, own[c], got[c], own_halo[c], got_halo[c], early[c])
        near.append([mine, flip(other, 1, 0), flip(other, 1, 2), flip(mine, 0, 2)])

    def with_other_core(block, waited):
        block = block[:1] + list(held_back(block[1:], waited))
        return block + [flip(x, 0, 1) for x in block]

    donors = jnp.stack(
        [(mom ^ mo) * local_k + (x_lo ^ lo) * half + kk for lo, mo in moves for kk in range(half)]
    ).astype(jnp.int32)
    table = jnp.sum(
        jnp.where(
            momentum_map[:, :, None] == donors[None, None, :],
            jnp.arange(points, dtype=jnp.int32)[None, :, None],
            0,
        ),
        axis=1,
    ).astype(jnp.int32)
    table_home = lax.dynamic_slice_in_dim(table, mom * local_k, local_k, 0).reshape(-1)

    sums, chunks, waited = [], [], mine
    for c in range(CHUNKS):
        chunks.append(with_other_core(near[c], [waited]))
        sums.append(home_sums(table_home, chunks[c], coup, coup_t, c, local_k))
        waited = sums[c][0]
    us, vs = [s[0] for s in sums], [s[1] for s in sums]
    inverse = 1.0 / (green.shape[1] * n_energy)
    received = []
    for first in range(0, local_k, half):
        part = partial_density(green, gamma, us, vs, inverse, first, half)
        part = part.reshape(half, 2, n_energy, norb // n_energy, norb)
        received.append(lax.all_to_all(part, "energy", split_axis=2, concat_axis=2, tiled=True))
    self_energy = row_sums(tile[None], table.reshape(-1), chunks, coupling, local_k)
    summed = jnp.concatenate(
        [jnp.sum(x.astype(jnp.float32), axis=2) for x in received], axis=0
    )
    density = jnp.transpose(summed, (2, 0, 1, 3))
    return (self_energy, density)


def solution(mesh):
    return jax.shard_map(
        on_device,
        mesh=mesh,
        in_specs=(
            P("mom", "energy", None, None, None),
            P("mom", "energy", None),
            P(None, "mom", None),
            P(),
            P(),
            P(),
            P(),
        ),
        out_specs=(P(None, "energy", None, "mom", None), P("energy", "mom", None, None)),
        check_vma=False,
    )
```

```python
import functools

import jax
import jax.numpy as jnp
from jax import lax
from jax.experimental import pallas as pl
from jax.experimental.pallas import tpu as pltpu
from jax.sharding import PartitionSpec as P

MIB = 1 << 20
NT = (((1,), (1,)), ((), ()))


def dot_nt(left, right):
    return lax.dot_general(left, right, NT, preferred_element_type=jnp.float32)


def dot_nn(left, right):
    return jnp.dot(left, right, preferred_element_type=jnp.float32)


def scale(block, gamma):
    return (block.astype(jnp.float32) * gamma).astype(jnp.bfloat16)


def lesser_kernel(place, green, gamma, *outs):
    norb = green.shape[-1]
    rows = outs[0].shape[3]
    gam = gamma[0, 0]
    g_re, g_im = green[0, 0, 0], green[0, 0, 1]
    wide_re = g_re.astype(jnp.float32)
    wide_im = g_im.astype(jnp.float32)
    less = (wide_re - wide_im).astype(jnp.bfloat16)
    more = (wide_re + wide_im).astype(jnp.bfloat16)
    total = dot_nt(scale(g_re, gam), less) + dot_nt(scale(g_im, gam), more)
    total = total.astype(jnp.bfloat16)
    for side in range(2):

        @pl.when(pl.program_id(0) // 2 == side)
        def _():
            for c in range(norb // rows):
                outs[side][c, 0, 0] = total[c * rows : (c + 1) * rows]


def packed_lesser(place, green, gamma, chunks):
    energies, norb = green.shape[1], green.shape[-1]
    half = green.shape[0] // 2
    rows = norb // chunks

    def which(k, p):
        return ((p[0] + 1 + k // half) % 2) * half + k % half

    def block_of(side):
        def index(k, e, p):
            if side == 0:
                return (0, jnp.minimum(k, half - 1), jnp.where(k < half, e, energies - 1), 0, 0)
            return (0, jnp.maximum(k - half, 0), jnp.where(k < half, 0, e), 0, 0)

        return pl.BlockSpec((chunks, 1, 1, rows, norb), index)

    out = jax.ShapeDtypeStruct((chunks, half, energies, rows, norb), jnp.bfloat16)
    outs = pl.pallas_call(
        lesser_kernel,
        grid_spec=pltpu.PrefetchScalarGridSpec(
            num_scalar_prefetch=1,
            grid=(2 * half, energies),
            in_specs=[
                pl.BlockSpec((1, 1, 2, norb, norb), lambda k, e, p: (which(k, p), e, 0, 0, 0)),
                pl.BlockSpec((1, 1, 1, norb), lambda k, e, p: (which(k, p), e, 0, 0)),
            ],
            out_specs=[block_of(0), block_of(1)],
        ),
        out_shape=[out] * 2,
        compiler_params=pltpu.CompilerParams(vmem_limit_bytes=60 * MIB),
        cost_estimate=pl.CostEstimate(
            flops=8 * half * energies * norb**3,
            bytes_accessed=12 * half * energies * norb**2,
            transcendentals=0,
        ),
        name="lesser",
    )(place, green, gamma)
    return outs


def identity(n):
    rows = lax.broadcasted_iota(jnp.int32, (n, n), 0)
    cols = lax.broadcasted_iota(jnp.int32, (n, n), 1)
    return (rows == cols).astype(jnp.float32).astype(jnp.bfloat16)


def exchange_kernel(
    weights, sent, own, coupling, src, coup, coup_t,
    got, own_halo, got_halo, mine, other, tiles, turned, send, recv, local,
):
    energy, mom = lax.axis_index("energy"), lax.axis_index("mom")
    pairs = lax.axis_size("energy") // 2
    x_lo, pair = energy % 2, energy // 2
    chunks, half, _, rows, norb = sent.shape
    points, height, _ = coupling.shape
    energy_a = energy + 1 - 2 * x_lo
    mom_core = mom + 1 - 2 * (mom % 2)
    mom_hi = mom + 2 - 4 * (mom // 2)
    mom_both = 3 - mom
    place = [mom, mom_core, mom_hi, mom_both]
    ring_a, ring_b, ring_ab = (energy_a, mom), (energy_a, mom_hi), (energy, mom_hi)
    core = (energy, mom_core)
    own_to = (energy - 2 + 4 * x_lo, mom)
    got_to = (energy + 2 - 4 * x_lo, mom)
    low, high = pair > 0, pair < pairs - 1
    first = x_lo == 0
    has_own_to = jnp.logical_or(
        jnp.logical_and(first, low), jnp.logical_and(jnp.logical_not(first), high)
    )
    has_got_to = jnp.logical_or(
        jnp.logical_and(first, high), jnp.logical_and(jnp.logical_not(first), low)
    )

    def remote(kind, c, source, target, device):
        return pltpu.make_async_remote_copy(
            src_ref=source,
            dst_ref=target,
            send_sem=send.at[kind, c],
            recv_sem=recv.at[kind, c],
            device_id=device,
            device_id_type=pl.DeviceIdType.MESH,
        )

    swap = [remote(0, c, sent.at[c], got.at[c], ring_a) for c in range(chunks)]
    to_own = [remote(1, c, own.at[c], own_halo.at[c], own_to) for c in range(chunks)]
    to_got = [remote(2, c, got.at[c], got_halo.at[c], got_to) for c in range(chunks)]
    near = [
        [
            remote(3, c, other.at[c], src.at[c, 1], ring_a),
            remote(4, c, other.at[c], src.at[c, 2], ring_b),
            remote(5, c, mine.at[c], src.at[c, 3], ring_ab),
        ]
        for c in range(chunks)
    ]
    far = [
        [remote(6, c, mine.at[c], src.at[c, 4], core)]
        + [remote(6 + s, c, src.at[c, s], src.at[c, 4 + s], core) for s in (1, 2, 3)]
        for c in range(chunks)
    ]
    stay = [pltpu.make_async_copy(mine.at[c], src.at[c, 0], local.at[c]) for c in range(chunks)]
    tile_core = remote(10, 0, coupling, tiles.at[1], core)
    tile_b = remote(10, 1, coupling, tiles.at[2], ring_b)
    tile_bc = remote(10, 2, tiles.at[2], tiles.at[3], core)
    tile_own = pltpu.make_async_copy(coupling, tiles.at[0], local.at[chunks])
    placed = [
        (
            pltpu.make_async_copy(
                tiles.at[s],
                coup.at[:, pl.ds(pl.multiple_of(place[s] * height, height), height), :],
                local.at[chunks + 1 + 2 * s],
            ),
            pltpu.make_async_copy(
                turned.at[s],
                coup_t.at[:, :, pl.ds(pl.multiple_of(place[s] * height, height), height)],
                local.at[chunks + 2 + 2 * s],
            ),
        )
        for s in range(4)
    ]

    barrier = pltpu.get_barrier_semaphore()

    def greet(device):
        pl.semaphore_signal(
            barrier, inc=1, device_id=device, device_id_type=pl.DeviceIdType.MESH
        )

    for device in (ring_a, ring_b, ring_ab, core):
        greet(device)

    @pl.when(has_own_to)
    def _():
        greet(own_to)

    @pl.when(has_got_to)
    def _():
        greet(got_to)

    pl.semaphore_wait(barrier, 4 + jnp.where(low, 1, 0) + jnp.where(high, 1, 0))

    swap[0].start()
    swap[1].start()

    @pl.when(has_own_to)
    def _():
        for c in range(chunks):
            to_own[c].start()

    tile_b.start()
    tile_core.start()
    tile_own.start()

    step = 16
    slabs = rows // step

    def clear(halo):
        def one(i, carry):
            c, r = i // slabs, i % slabs
            at = pl.ds(pl.multiple_of(r * step, step), step)
            for k in range(half):
                for e in range(2):
                    halo[c, k, e, at, :] = jnp.zeros((step, norb), halo.dtype)
            return carry

        lax.fori_loop(0, chunks * slabs, one, 0)

    @pl.when(jnp.logical_not(has_got_to))
    def _():
        clear(own_halo)

    @pl.when(jnp.logical_not(has_own_to))
    def _():
        clear(got_halo)

    turn = identity(norb // 2)

    def fold(s):
        def one(q, carry):
            for b in range(2):
                span = slice(b * (norb // 2), (b + 1) * (norb // 2))
                turned[s, q, span, :] = dot_nt(turn, tiles[s, q, :, span]).astype(turned.dtype)
            return carry

        lax.fori_loop(0, points, one, 0)
        for copy in placed[s]:
            copy.start()

    def shift(c, parts, outs):
        def one(i, carry):
            k, r = i // slabs, i % slabs
            at = pl.ds(pl.multiple_of(r * step, step), step)
            levels = [ref[c, k, e, at, :].astype(jnp.float32) for ref in parts for e in range(2)]
            for o in range(4):
                total = weights[0] * levels[o + 3] + weights[1] * levels[o + 4]
                total = total + weights[2] * levels[o + 1] + weights[3] * levels[o]
                outs[o // 2][c, k, o % 2, at, :] = total.astype(mine.dtype)
            return carry

        lax.fori_loop(0, half * slabs, one, 0)

    for c in range(chunks + 1):
        if c < chunks:
            swap[c].wait_recv()

            @pl.when(has_got_to)
            def _(copy=to_got[c]):
                copy.start()

            if c + 2 < chunks:
                swap[c + 2].start()
        if c == 0:
            tile_own.wait()
            fold(0)
        else:
            d = c - 1

            @pl.when(has_got_to)
            def _(copy=to_own[d]):
                copy.wait_recv()

            @pl.when(has_own_to)
            def _(copy=to_got[d]):
                copy.wait_recv()

            @pl.when(first)
            def _(d=d):
                shift(d, (got_halo, own, got, own_halo), (mine, other))

            @pl.when(jnp.logical_not(first))
            def _(d=d):
                shift(d, (own_halo, got, own, got_halo), (other, mine))

            for copy in near[d]:
                copy.start()
            far[d][0].start()
            stay[d].start()
        if c == 1:
            tile_core.wait_recv()
            fold(1)

    tile_b.wait_recv()
    tile_bc.start()
    fold(2)
    for c in range(chunks):
        for s in (1, 2, 3):
            near[c][s - 1].wait_recv()
            far[c][s].start()
        if c == 0:
            tile_bc.wait_recv()
            fold(3)
    for c in range(chunks):
        for copy in far[c]:
            copy.wait_recv()
        for copy in [swap[c]] + near[c] + far[c]:
            copy.wait_send()
        stay[c].wait()

        @pl.when(has_own_to)
        def _(copy=to_own[c]):
            copy.wait_send()

        @pl.when(has_got_to)
        def _(copy=to_got[c]):
            copy.wait_send()

    for copy in (tile_core, tile_b, tile_bc):
        copy.wait_send()
    for pair_of in placed:
        for copy in pair_of:
            copy.wait()


def exchanged(weights, sent, own, coupling):
    chunks, half, energies, rows, norb = sent.shape
    points, height, _ = coupling.shape
    whole = jax.ShapeDtypeStruct((points, norb, norb), jnp.bfloat16)
    vmem = pl.BlockSpec(memory_space=pltpu.VMEM)
    hbm = pl.BlockSpec(memory_space=pl.ANY)
    part = pltpu.VMEM(sent.shape, jnp.bfloat16)
    return pl.pallas_call(
        exchange_kernel,
        in_specs=[pl.BlockSpec(memory_space=pltpu.SMEM), vmem, vmem, hbm],
        out_specs=[hbm] * 3,
        out_shape=[
            jax.ShapeDtypeStruct((chunks, 8, half, energies, rows, norb), jnp.bfloat16),
            whole,
            whole,
        ],
        scratch_shapes=[part] * 5
        + [
            pltpu.VMEM((4, points, height, norb), jnp.bfloat16),
            pltpu.VMEM((4, points, norb, height), jnp.bfloat16),
            pltpu.SemaphoreType.DMA((11, chunks)),
            pltpu.SemaphoreType.DMA((11, chunks)),
            pltpu.SemaphoreType.DMA((chunks + 9,)),
        ],
        compiler_params=pltpu.CompilerParams(
            collective_id=0, has_side_effects=True, vmem_limit_bytes=60 * MIB
        ),
        name="exchange",
    )(weights, sent, own, coupling)


def add_products(targets, streams, picks, donor, factor, at, store):
    acc = [[None] * streams for _ in range(targets)]
    kept = {}
    for quad in range(4):
        held = [[donor(4 * quad + d, n, at) for n in range(streams)] for d in range(4)]
        for t in range(targets):
            c = [factor[picks(t, 4 * quad + d), at[0], at[1]] for d in range(4)]
            for n in range(streams):
                part = (c[0] * held[0][n] + c[1] * held[1][n]) + (
                    c[2] * held[2][n] + c[3] * held[3][n]
                )
                if quad % 2 == 0:
                    kept[t, n] = part
                    continue
                part = (kept.pop((t, n)) + part).astype(jnp.float32)
                acc[t][n] = part if acc[t][n] is None else acc[t][n] + part
    for t in range(targets):
        for n in range(streams):
            store(t, n, at, acc[t][n])


def home_kernel(table, *refs):
    sources, coup, coup_t, out, out_t = refs
    targets, _, height, norb = out.shape

    def picks(t, d):
        return table[t * 16 + d]

    def donor(d, n, at):
        return sources[0, d // 2, d % 2, n, at[0], at[1]]

    def into(ref):
        def store(t, n, at, value):
            ref[t, n, at[0], at[1]] = value.astype(jnp.bfloat16)

        return store

    def slab(i, carry):
        at = (
            pl.ds(pl.multiple_of(i // 2 * 16, 16), 16),
            pl.ds(pl.multiple_of(i % 2 * (norb // 2), norb // 2), norb // 2),
        )
        add_products(targets, 2, picks, donor, coup, at, into(out))
        add_products(targets, 2, picks, donor, coup_t, at, into(out_t))
        return carry

    lax.fori_loop(0, height // 16 * 2, slab, 0)


def home_sums(table, src, coup, coup_t, targets):
    chunks, _, half, energies, rows, norb = src.shape
    points = coup.shape[0]
    height = rows // 2
    steps = rows // height
    given = pl.BlockSpec(
        (1, 8, half, energies, height, norb), lambda i, q: (i // steps, 0, 0, 0, i % steps, 0)
    )
    factor = pl.BlockSpec((points, height, norb), lambda i, q: (0, i, 0))
    result = pl.BlockSpec((targets, energies, height, norb), lambda i, q: (0, 0, i, 0))
    out = jax.ShapeDtypeStruct((targets, energies, chunks * rows, norb), jnp.bfloat16)
    return pl.pallas_call(
        home_kernel,
        grid_spec=pltpu.PrefetchScalarGridSpec(
            num_scalar_prefetch=1,
            grid=(chunks * steps,),
            in_specs=[given] + [factor] * 2,
            out_specs=[result] * 2,
        ),
        out_shape=[out, out],
        compiler_params=pltpu.CompilerParams(vmem_limit_bytes=60 * MIB),
        name="home",
    )(table, src, coup, coup_t)


def rows_kernel(tile, table, rows_of, cols_of, coup, out, source):
    targets, _, _, height, norb = out.shape
    group = pl.program_id(1) * targets

    @pl.when(pl.program_id(1) == 0)
    def _():
        turn = identity(height)
        for d in range(16):
            for b in range(norb // height):
                span = slice(b * height, (b + 1) * height)
                straight = rows_of[0, d // 2, d % 2, 0, :, span].astype(jnp.float32)
                turned = dot_nt(turn, cols_of[b, d // 2, d % 2, 0])
                source[d, 0, :, span] = (straight + turned).astype(jnp.bfloat16)
                source[d, 1, :, span] = (straight - turned).astype(jnp.bfloat16)

    def picks(t, d):
        return table[(group + t) * 16 + d]

    def donor(d, n, at):
        return source[d, n, at[0], at[1]]

    def store(t, n, at, value):
        out[t, 0, n, at[0], at[1]] = value.astype(jnp.bfloat16)

    def slab(i, carry):
        at = (
            pl.ds(pl.multiple_of(i // 2 * 16, 16), 16),
            pl.ds(pl.multiple_of(i % 2 * (norb // 2), norb // 2), norb // 2),
        )
        add_products(targets, 2, picks, donor, coup, at, store)
        return carry

    lax.fori_loop(0, height // 16 * 2, slab, 0)


def row_sums(tile, table, src, coupling, targets):
    chunks, _, half, energies, rows, norb = src.shape
    points, height, _ = coupling.shape
    row_block = pl.BlockSpec(
        (1, 8, half, 1, rows, norb), lambda e, g, t, q: (t[0], 0, 0, e, 0, 0)
    )
    col_block = pl.BlockSpec(
        (chunks, 8, half, 1, rows, height), lambda e, g, t, q: (0, 0, 0, e, 0, t[0])
    )
    return pl.pallas_call(
        rows_kernel,
        grid_spec=pltpu.PrefetchScalarGridSpec(
            num_scalar_prefetch=2,
            grid=(energies, points // targets),
            in_specs=[
                row_block,
                col_block,
                pl.BlockSpec((points, height, norb), lambda e, g, t, q: (0, 0, 0)),
            ],
            out_specs=pl.BlockSpec(
                (targets, 1, 2, height, norb), lambda e, g, t, q: (g, e, 0, 0, 0)
            ),
            scratch_shapes=[pltpu.VMEM((16, 2, height, norb), jnp.bfloat16)],
        ),
        out_shape=jax.ShapeDtypeStruct((points, energies, 2, height, norb), jnp.bfloat16),
        compiler_params=pltpu.CompilerParams(vmem_limit_bytes=60 * MIB),
        name="rows",
    )(tile, table, src, src, coupling)


def density_kernel(inverse, green, gamma, us, vs, out):
    d_re = d_im = None
    for e in range(green.shape[1]):
        g_re, g_im = green[0, e, 0], green[0, e, 1]
        gam = gamma[0, e]
        wide_re, wide_im = g_re.astype(jnp.float32), g_im.astype(jnp.float32)
        less = (wide_re - wide_im).astype(jnp.bfloat16)
        more = (wide_re + wide_im).astype(jnp.bfloat16)
        u, v = us[0, e], vs[0, e]
        m_re = dot_nn(less, u) + dot_nt(more, v) + scale(g_re, gam).astype(jnp.float32)
        m_im = dot_nn(more, u) - dot_nt(less, v) + scale(g_im, gam).astype(jnp.float32)
        m_re, m_im = m_re.astype(jnp.bfloat16), m_im.astype(jnp.bfloat16)
        one = dot_nt(m_re, g_re) + dot_nt(m_im, g_im)
        two = dot_nt(m_im, g_re) - dot_nt(m_re, g_im)
        d_re = one if d_re is None else d_re + one
        d_im = two if d_im is None else d_im + two
    shape = out.shape[2:]
    out[0, 0] = (d_re * inverse).astype(jnp.bfloat16).reshape(shape)
    out[0, 1] = (d_im * inverse).astype(jnp.bfloat16).reshape(shape)


def partial_density(green, gamma, us, vs, inverse, owners):
    count, energies, _, norb, _ = green.shape
    rows = norb // owners
    part = pl.BlockSpec((1, energies, norb, norb), lambda k: (k, 0, 0, 0))
    return pl.pallas_call(
        functools.partial(density_kernel, inverse),
        grid=(count,),
        in_specs=[
            pl.BlockSpec((1, energies, 2, norb, norb), lambda k: (k, 0, 0, 0, 0)),
            pl.BlockSpec((1, energies, 1, norb), lambda k: (k, 0, 0, 0)),
            part,
            part,
        ],
        out_specs=pl.BlockSpec((1, 2, owners, rows, norb), lambda k: (k, 0, 0, 0, 0)),
        out_shape=jax.ShapeDtypeStruct((count, 2, owners, rows, norb), jnp.bfloat16),
        compiler_params=pltpu.CompilerParams(vmem_limit_bytes=60 * MIB),
        name="density",
    )(green, gamma, us, vs)


def on_device(green, broadening, coupling, shift_steps, mode_weight, occupation, momentum_map):
    n_energy, n_mom = lax.axis_size("energy"), lax.axis_size("mom")
    local_k, local_e = green.shape[:2]
    half = local_k // 2
    points = momentum_map.shape[1]
    energy, mom = lax.axis_index("energy"), lax.axis_index("mom")
    x_lo = energy % 2

    def weight_of(step, factor):
        return 0.5 * jnp.sum(jnp.where(shift_steps == step, mode_weight * factor, 0.0))

    weights = jnp.stack(
        [weight_of(s, occupation + 1.0) for s in (1, 2)] + [weight_of(s, occupation) for s in (1, 2)]
    ).astype(jnp.float32)

    gamma = broadening[:, :, None, :]
    sent, own = packed_lesser(x_lo.astype(jnp.int32)[None], green, gamma, n_mom)
    src, coup, coup_t = exchanged(weights, sent, own, coupling)

    moves = [(0, 0), (1, 0), (1, 2), (0, 2)]
    moves = moves + [(lo, mo ^ 1) for lo, mo in moves]
    donors = jnp.stack(
        [(mom ^ mo) * local_k + (x_lo ^ lo) * half + kk for lo, mo in moves for kk in range(half)]
    ).astype(jnp.int32)
    table = jnp.sum(
        jnp.where(
            momentum_map[:, :, None] == donors[None, None, :],
            jnp.arange(points, dtype=jnp.int32)[None, :, None],
            0,
        ),
        axis=1,
    ).astype(jnp.int32)
    table_home = lax.dynamic_slice_in_dim(table, mom * local_k, local_k, 0).reshape(-1)

    us, vs = home_sums(table_home, src, coup, coup_t, local_k)
    part = partial_density(green, gamma, us, vs, 1.0 / (local_e * n_energy), n_energy)
    parts = lax.all_to_all(part, "energy", split_axis=2, concat_axis=2, tiled=True)
    self_energy = row_sums(
        mom.astype(jnp.int32)[None], table.reshape(-1), src, coupling, local_k
    )
    density = jnp.transpose(jnp.sum(parts.astype(jnp.float32), axis=2), (2, 0, 1, 3))
    return (self_energy, density)


def solution(mesh):
    return jax.shard_map(
        on_device,
        mesh=mesh,
        in_specs=(
            P("mom", "energy", None, None, None),
            P("mom", "energy", None),
            P(None, "mom", None),
            P(),
            P(),
            P(),
            P(),
        ),
        out_specs=(P(None, "energy", None, "mom", None), P("energy", "mom", None, None)),
        check_vma=False,
    )
```

```python
import functools

import jax
import jax.numpy as jnp
from jax import lax
from jax.experimental import pallas as pl
from jax.experimental.pallas import tpu as pltpu
from jax.sharding import PartitionSpec as P

MIB = 1 << 20
NT = (((1,), (1,)), ((), ()))


def dot_nt(left, right):
    return lax.dot_general(left, right, NT, preferred_element_type=jnp.float32)


def dot_nn(left, right):
    return jnp.dot(left, right, preferred_element_type=jnp.float32)


def scale(block, gamma):
    return (block.astype(jnp.float32) * gamma).astype(jnp.bfloat16)


def lesser_kernel(place, green, gamma, *outs):
    norb = green.shape[-1]
    rows = outs[0].shape[3]
    gam = gamma[0, 0]
    g_re, g_im = green[0, 0, 0], green[0, 0, 1]
    wide_re = g_re.astype(jnp.float32)
    wide_im = g_im.astype(jnp.float32)
    less = (wide_re - wide_im).astype(jnp.bfloat16)
    more = (wide_re + wide_im).astype(jnp.bfloat16)
    total = dot_nt(scale(g_re, gam), less) + dot_nt(scale(g_im, gam), more)
    total = total.astype(jnp.bfloat16)
    for side in range(2):

        @pl.when(pl.program_id(0) // 2 == side)
        def _():
            for c in range(norb // rows):
                outs[side][c, 0, 0] = total[c * rows : (c + 1) * rows]


def packed_lesser(place, green, gamma, chunks):
    energies, norb = green.shape[1], green.shape[-1]
    half = green.shape[0] // 2
    rows = norb // chunks

    def which(k, p):
        return ((p[0] + 1 + k // half) % 2) * half + k % half

    def block_of(side):
        def index(k, e, p):
            if side == 0:
                return (0, jnp.minimum(k, half - 1), jnp.where(k < half, e, energies - 1), 0, 0)
            return (0, jnp.maximum(k - half, 0), jnp.where(k < half, 0, e), 0, 0)

        return pl.BlockSpec((chunks, 1, 1, rows, norb), index)

    out = jax.ShapeDtypeStruct((chunks, half, energies, rows, norb), jnp.bfloat16)
    outs = pl.pallas_call(
        lesser_kernel,
        grid_spec=pltpu.PrefetchScalarGridSpec(
            num_scalar_prefetch=1,
            grid=(2 * half, energies),
            in_specs=[
                pl.BlockSpec((1, 1, 2, norb, norb), lambda k, e, p: (which(k, p), e, 0, 0, 0)),
                pl.BlockSpec((1, 1, 1, norb), lambda k, e, p: (which(k, p), e, 0, 0)),
            ],
            out_specs=[block_of(0), block_of(1)],
        ),
        out_shape=[out] * 2,
        compiler_params=pltpu.CompilerParams(vmem_limit_bytes=60 * MIB),
        cost_estimate=pl.CostEstimate(
            flops=8 * half * energies * norb**3,
            bytes_accessed=12 * half * energies * norb**2,
            transcendentals=0,
        ),
        name="lesser",
    )(place, green, gamma)
    return outs


def identity(n):
    rows = lax.broadcasted_iota(jnp.int32, (n, n), 0)
    cols = lax.broadcasted_iota(jnp.int32, (n, n), 1)
    return (rows == cols).astype(jnp.float32).astype(jnp.bfloat16)


def exchange_kernel(
    weights, sent, own, coupling, src, coup, coup_t,
    got, own_halo, got_halo, mine, other, tiles, turned, send, recv, local,
):
    energy, mom = lax.axis_index("energy"), lax.axis_index("mom")
    pairs = lax.axis_size("energy") // 2
    x_lo, pair = energy % 2, energy // 2
    chunks, half, _, rows, norb = sent.shape
    points, height, _ = coupling.shape
    energy_a = energy + 1 - 2 * x_lo
    mom_core = mom + 1 - 2 * (mom % 2)
    mom_hi = mom + 2 - 4 * (mom // 2)
    mom_both = 3 - mom
    place = [mom, mom_core, mom_hi, mom_both]
    ring_a, ring_b, ring_ab = (energy_a, mom), (energy_a, mom_hi), (energy, mom_hi)
    core = (energy, mom_core)
    own_to = (energy - 2 + 4 * x_lo, mom)
    got_to = (energy + 2 - 4 * x_lo, mom)
    low, high = pair > 0, pair < pairs - 1
    first = x_lo == 0
    has_own_to = jnp.logical_or(
        jnp.logical_and(first, low), jnp.logical_and(jnp.logical_not(first), high)
    )
    has_got_to = jnp.logical_or(
        jnp.logical_and(first, high), jnp.logical_and(jnp.logical_not(first), low)
    )

    def remote(kind, c, source, target, device):
        return pltpu.make_async_remote_copy(
            src_ref=source,
            dst_ref=target,
            send_sem=send.at[kind, c],
            recv_sem=recv.at[kind, c],
            device_id=device,
            device_id_type=pl.DeviceIdType.MESH,
        )

    swap = [remote(0, c, sent.at[c], got.at[c], ring_a) for c in range(chunks)]
    to_own = [remote(1, c, own.at[c], own_halo.at[c], own_to) for c in range(chunks)]
    to_got = [remote(2, c, got.at[c], got_halo.at[c], got_to) for c in range(chunks)]
    near = [
        [
            remote(3, c, other.at[c], src.at[c, 1], ring_a),
            remote(4, c, other.at[c], src.at[c, 2], ring_b),
            remote(5, c, mine.at[c], src.at[c, 3], ring_ab),
        ]
        for c in range(chunks)
    ]
    far = [
        [remote(6, c, mine.at[c], src.at[c, 4], core)]
        + [remote(6 + s, c, src.at[c, s], src.at[c, 4 + s], core) for s in (1, 2, 3)]
        for c in range(chunks)
    ]
    stay = [pltpu.make_async_copy(mine.at[c], src.at[c, 0], local.at[c]) for c in range(chunks)]
    tile_core = remote(10, 0, coupling, tiles.at[1], core)
    tile_b = remote(10, 1, coupling, tiles.at[2], ring_b)
    tile_bc = remote(10, 2, tiles.at[2], tiles.at[3], core)
    tile_own = pltpu.make_async_copy(coupling, tiles.at[0], local.at[chunks])
    placed = [
        (
            pltpu.make_async_copy(
                tiles.at[s],
                coup.at[:, pl.ds(pl.multiple_of(place[s] * height, height), height), :],
                local.at[chunks + 1 + 2 * s],
            ),
            pltpu.make_async_copy(
                turned.at[s],
                coup_t.at[:, :, pl.ds(pl.multiple_of(place[s] * height, height), height)],
                local.at[chunks + 2 + 2 * s],
            ),
        )
        for s in range(4)
    ]

    barrier = pltpu.get_barrier_semaphore()

    def greet(device):
        pl.semaphore_signal(
            barrier, inc=1, device_id=device, device_id_type=pl.DeviceIdType.MESH
        )

    for device in (ring_a, ring_b, ring_ab, core):
        greet(device)

    @pl.when(has_own_to)
    def _():
        greet(own_to)

    @pl.when(has_got_to)
    def _():
        greet(got_to)

    pl.semaphore_wait(barrier, 4 + jnp.where(low, 1, 0) + jnp.where(high, 1, 0))

    swap[0].start()
    swap[1].start()

    @pl.when(has_own_to)
    def _():
        for c in range(chunks):
            to_own[c].start()

    tile_b.start()
    tile_core.start()
    tile_own.start()

    step = 16
    slabs = rows // step

    def clear(halo):
        def one(i, carry):
            c, r = i // slabs, i % slabs
            at = pl.ds(pl.multiple_of(r * step, step), step)
            for k in range(half):
                for e in range(2):
                    halo[c, k, e, at, :] = jnp.zeros((step, norb), halo.dtype)
            return carry

        lax.fori_loop(0, chunks * slabs, one, 0)

    @pl.when(jnp.logical_not(has_got_to))
    def _():
        clear(own_halo)

    @pl.when(jnp.logical_not(has_own_to))
    def _():
        clear(got_halo)

    turn = identity(norb // 2)

    def fold(s):
        def one(q, carry):
            for b in range(2):
                span = slice(b * (norb // 2), (b + 1) * (norb // 2))
                turned[s, q, span, :] = dot_nt(turn, tiles[s, q, :, span]).astype(turned.dtype)
            return carry

        lax.fori_loop(0, points, one, 0)
        for copy in placed[s]:
            copy.start()

    def shift(c, parts, outs):
        def one(i, carry):
            k, r = i // slabs, i % slabs
            at = pl.ds(pl.multiple_of(r * step, step), step)
            levels = [ref[c, k, e, at, :].astype(jnp.float32) for ref in parts for e in range(2)]
            for o in range(4):
                total = weights[0] * levels[o + 3] + weights[1] * levels[o + 4]
                total = total + weights[2] * levels[o + 1] + weights[3] * levels[o]
                outs[o // 2][c, k, o % 2, at, :] = total.astype(mine.dtype)
            return carry

        lax.fori_loop(0, half * slabs, one, 0)

    for c in range(chunks + 1):
        if c < chunks:
            swap[c].wait_recv()

            @pl.when(has_got_to)
            def _(copy=to_got[c]):
                copy.start()

            if c + 2 < chunks:
                swap[c + 2].start()
        if c == 0:
            tile_own.wait()
            fold(0)
        else:
            d = c - 1

            @pl.when(has_got_to)
            def _(copy=to_own[d]):
                copy.wait_recv()

            @pl.when(has_own_to)
            def _(copy=to_got[d]):
                copy.wait_recv()

            @pl.when(first)
            def _(d=d):
                shift(d, (got_halo, own, got, own_halo), (mine, other))

            @pl.when(jnp.logical_not(first))
            def _(d=d):
                shift(d, (own_halo, got, own, got_halo), (other, mine))

            for copy in near[d]:
                copy.start()
            far[d][0].start()
            stay[d].start()
        if c == 1:
            tile_core.wait_recv()
            fold(1)

    tile_b.wait_recv()
    tile_bc.start()
    fold(2)
    for c in range(chunks):
        for s in (1, 2, 3):
            near[c][s - 1].wait_recv()
            far[c][s].start()
        if c == 0:
            tile_bc.wait_recv()
            fold(3)
    for c in range(chunks):
        for copy in far[c]:
            copy.wait_recv()
        for copy in [swap[c]] + near[c] + far[c]:
            copy.wait_send()
        stay[c].wait()

        @pl.when(has_own_to)
        def _(copy=to_own[c]):
            copy.wait_send()

        @pl.when(has_got_to)
        def _(copy=to_got[c]):
            copy.wait_send()

    for copy in (tile_core, tile_b, tile_bc):
        copy.wait_send()
    for pair_of in placed:
        for copy in pair_of:
            copy.wait()


def exchanged(weights, sent, own, coupling):
    chunks, half, energies, rows, norb = sent.shape
    points, height, _ = coupling.shape
    whole = jax.ShapeDtypeStruct((points, norb, norb), jnp.bfloat16)
    vmem = pl.BlockSpec(memory_space=pltpu.VMEM)
    hbm = pl.BlockSpec(memory_space=pl.ANY)
    part = pltpu.VMEM(sent.shape, jnp.bfloat16)
    return pl.pallas_call(
        exchange_kernel,
        in_specs=[pl.BlockSpec(memory_space=pltpu.SMEM), vmem, vmem, hbm],
        out_specs=[hbm] * 3,
        out_shape=[
            jax.ShapeDtypeStruct((chunks, 8, half, energies, rows, norb), jnp.bfloat16),
            whole,
            whole,
        ],
        scratch_shapes=[part] * 5
        + [
            pltpu.VMEM((4, points, height, norb), jnp.bfloat16),
            pltpu.VMEM((4, points, norb, height), jnp.bfloat16),
            pltpu.SemaphoreType.DMA((11, chunks)),
            pltpu.SemaphoreType.DMA((11, chunks)),
            pltpu.SemaphoreType.DMA((chunks + 9,)),
        ],
        compiler_params=pltpu.CompilerParams(
            collective_id=0, has_side_effects=True, vmem_limit_bytes=60 * MIB
        ),
        name="exchange",
    )(weights, sent, own, coupling)


def add_products(targets, streams, picks, donor, factor, at, store):
    acc = [[None] * streams for _ in range(targets)]
    kept = {}
    for quad in range(4):
        held = [[donor(4 * quad + d, n, at) for n in range(streams)] for d in range(4)]
        for t in range(targets):
            c = [factor[picks(t, 4 * quad + d), at[0], at[1]] for d in range(4)]
            for n in range(streams):
                part = (c[0] * held[0][n] + c[1] * held[1][n]) + (
                    c[2] * held[2][n] + c[3] * held[3][n]
                )
                if quad % 2 == 0:
                    kept[t, n] = part
                    continue
                part = (kept.pop((t, n)) + part).astype(jnp.float32)
                acc[t][n] = part if acc[t][n] is None else acc[t][n] + part
    for t in range(targets):
        for n in range(streams):
            store(t, n, at, acc[t][n])


def home_kernel(table, *refs):
    sources, coup, coup_t, out, out_t = refs
    targets, _, height, norb = out.shape

    def picks(t, d):
        return table[t * 16 + d]

    def donor(d, n, at):
        return sources[0, d // 2, d % 2, n, at[0], at[1]]

    def into(ref):
        def store(t, n, at, value):
            ref[t, n, at[0], at[1]] = value.astype(jnp.bfloat16)

        return store

    def slab(i, carry):
        at = (
            pl.ds(pl.multiple_of(i // 2 * 16, 16), 16),
            pl.ds(pl.multiple_of(i % 2 * (norb // 2), norb // 2), norb // 2),
        )
        add_products(targets, 2, picks, donor, coup, at, into(out))
        add_products(targets, 2, picks, donor, coup_t, at, into(out_t))
        return carry

    lax.fori_loop(0, height // 16 * 2, slab, 0)


def home_sums(table, src, coup, coup_t, targets):
    chunks, _, half, energies, rows, norb = src.shape
    points = coup.shape[0]
    height = rows // 2
    steps = rows // height
    given = pl.BlockSpec(
        (1, 8, half, energies, height, norb), lambda i, q: (i // steps, 0, 0, 0, i % steps, 0)
    )
    factor = pl.BlockSpec((points, height, norb), lambda i, q: (0, i, 0))
    result = pl.BlockSpec((targets, energies, height, norb), lambda i, q: (0, 0, i, 0))
    out = jax.ShapeDtypeStruct((targets, energies, chunks * rows, norb), jnp.bfloat16)
    return pl.pallas_call(
        home_kernel,
        grid_spec=pltpu.PrefetchScalarGridSpec(
            num_scalar_prefetch=1,
            grid=(chunks * steps,),
            in_specs=[given] + [factor] * 2,
            out_specs=[result] * 2,
        ),
        out_shape=[out, out],
        compiler_params=pltpu.CompilerParams(vmem_limit_bytes=60 * MIB),
        name="home",
    )(table, src, coup, coup_t)


def finish_kernel(
    inverse, table, green, gamma, us, vs, rows_of, cols_of, coup, out, density,
    source, part, came, send, recv,
):
    energy, mom = lax.axis_index("energy"), lax.axis_index("mom")
    owners = lax.axis_size("energy")
    count = part.shape[0]
    targets, _, _, height, norb = out.shape
    index = pl.program_id(0)

    @pl.when(index == 0)
    def _():
        barrier = pltpu.get_barrier_semaphore()

        def greet(n, carry):
            pl.semaphore_signal(
                barrier,
                inc=1,
                device_id=((energy + n) % owners, mom),
                device_id_type=pl.DeviceIdType.MESH,
            )
            return carry

        lax.fori_loop(1, owners, greet, 0)
        pl.semaphore_wait(barrier, owners - 1)

    @pl.when(index < count)
    def _():
        d_re = d_im = None
        for e in range(green.shape[1]):
            g_re, g_im = green[0, e, 0], green[0, e, 1]
            gam = gamma[0, e]
            wide_re, wide_im = g_re.astype(jnp.float32), g_im.astype(jnp.float32)
            less = (wide_re - wide_im).astype(jnp.bfloat16)
            more = (wide_re + wide_im).astype(jnp.bfloat16)
            u, v = us[0, e], vs[0, e]
            m_re = dot_nn(less, u) + dot_nt(more, v) + scale(g_re, gam).astype(jnp.float32)
            m_im = dot_nn(more, u) - dot_nt(less, v) + scale(g_im, gam).astype(jnp.float32)
            m_re, m_im = m_re.astype(jnp.bfloat16), m_im.astype(jnp.bfloat16)
            one = dot_nt(m_re, g_re) + dot_nt(m_im, g_im)
            two = dot_nt(m_im, g_re) - dot_nt(m_re, g_im)
            d_re = one if d_re is None else d_re + one
            d_im = two if d_im is None else d_im + two
        shape = (owners, norb // owners, norb)
        part[index, :, 0] = (d_re * inverse).astype(jnp.bfloat16).reshape(shape)
        part[index, :, 1] = (d_im * inverse).astype(jnp.bfloat16).reshape(shape)
        came[index, energy] = part[index, energy]

        def post(n, carry):
            peer = (energy + n) % owners
            pltpu.make_async_remote_copy(
                src_ref=part.at[index, peer],
                dst_ref=came.at[index, energy],
                send_sem=send.at[index],
                recv_sem=recv.at[index],
                device_id=(peer, mom),
                device_id_type=pl.DeviceIdType.MESH,
            ).start()
            return carry

        lax.fori_loop(1, owners, post, 0)

    place = index - count
    group = place % 4 * targets

    @pl.when(jnp.logical_and(index >= count, place % 4 == 0))
    def _():
        turn = identity(height)
        for d in range(16):
            for b in range(norb // height):
                span = slice(b * height, (b + 1) * height)
                straight = rows_of[0, d // 2, d % 2, 0, :, span].astype(jnp.float32)
                turned = dot_nt(turn, cols_of[b, d // 2, d % 2, 0])
                source[d, 0, :, span] = (straight + turned).astype(jnp.bfloat16)
                source[d, 1, :, span] = (straight - turned).astype(jnp.bfloat16)

    def picks(t, d):
        return table[(group + t) * 16 + d]

    def donor(d, n, at):
        return source[d, n, at[0], at[1]]

    def store(t, n, at, value):
        out[t, 0, n, at[0], at[1]] = value.astype(jnp.bfloat16)

    @pl.when(index >= count)
    def _():
        def slab(i, carry):
            at = (
                pl.ds(pl.multiple_of(i // 2 * 16, 16), 16),
                pl.ds(pl.multiple_of(i % 2 * (norb // 2), norb // 2), norb // 2),
            )
            add_products(targets, 2, picks, donor, coup, at, store)
            return carry

        lax.fori_loop(0, height // 16 * 2, slab, 0)

    @pl.when(index == pl.num_programs(0) - 1)
    def _():
        for k in range(count):
            every = pltpu.make_async_remote_copy(
                src_ref=part.at[k, pl.ds(0, owners - 1)],
                dst_ref=came.at[k, pl.ds(0, owners - 1)],
                send_sem=send.at[k],
                recv_sem=recv.at[k],
                device_id=((energy + 1) % owners, mom),
                device_id_type=pl.DeviceIdType.MESH,
            )
            every.wait_recv()
            every.wait_send()

            def add(n, total):
                return total + came[k, n].astype(jnp.float32)

            total = lax.fori_loop(1, owners, add, came[k, 0].astype(jnp.float32))
            for c in range(2):
                density[:, k, c, :] = total[c]


def finished(table, green, gamma, us, vs, src, coupling, owners, targets):
    chunks, _, half, energies, rows, norb = src.shape
    points, height, _ = coupling.shape
    count = green.shape[0]
    own_rows = norb // owners
    groups = points // targets

    def of_k(i):
        return jnp.minimum(i, count - 1)

    def of_e(i):
        return jnp.maximum(i - count, 0) // groups

    def of_g(i):
        return jnp.maximum(i - count, 0) % groups

    part = pl.BlockSpec((1, energies, norb, norb), lambda i: (of_k(i), 0, 0, 0))
    return pl.pallas_call(
        functools.partial(finish_kernel, 1.0 / (energies * owners)),
        grid=(count + energies * groups,),
        in_specs=[
            pl.BlockSpec(memory_space=pltpu.SMEM),
            pl.BlockSpec((1, energies, 2, norb, norb), lambda i: (of_k(i), 0, 0, 0, 0)),
            pl.BlockSpec((1, energies, 1, norb), lambda i: (of_k(i), 0, 0, 0)),
            part,
            part,
            pl.BlockSpec(
                (1, 8, half, 1, rows, norb),
                lambda i: (lax.axis_index("mom"), 0, 0, of_e(i), 0, 0),
            ),
            pl.BlockSpec(
                (chunks, 8, half, 1, rows, height),
                lambda i: (0, 0, 0, of_e(i), 0, lax.axis_index("mom")),
            ),
            pl.BlockSpec((points, height, norb), lambda i: (0, 0, 0)),
        ],
        out_specs=[
            pl.BlockSpec((targets, 1, 2, height, norb), lambda i: (of_g(i), of_e(i), 0, 0, 0)),
            pl.BlockSpec((own_rows, count, 2, norb), lambda i: (0, 0, 0, 0)),
        ],
        out_shape=[
            jax.ShapeDtypeStruct((points, energies, 2, height, norb), jnp.bfloat16),
            jax.ShapeDtypeStruct((own_rows, count, 2, norb), jnp.float32),
        ],
        scratch_shapes=[
            pltpu.VMEM((16, 2, height, norb), jnp.bfloat16),
            pltpu.VMEM((count, owners, 2, own_rows, norb), jnp.bfloat16),
            pltpu.VMEM((count, owners, 2, own_rows, norb), jnp.bfloat16),
            pltpu.SemaphoreType.DMA((count,)),
            pltpu.SemaphoreType.DMA((count,)),
        ],
        compiler_params=pltpu.CompilerParams(
            collective_id=1, has_side_effects=True, vmem_limit_bytes=60 * MIB
        ),
        name="finish",
    )(table, green, gamma, us, vs, src, src, coupling)


def on_device(green, broadening, coupling, shift_steps, mode_weight, occupation, momentum_map):
    n_energy, n_mom = lax.axis_size("energy"), lax.axis_size("mom")
    local_k = green.shape[0]
    half = local_k // 2
    points = momentum_map.shape[1]
    energy, mom = lax.axis_index("energy"), lax.axis_index("mom")
    x_lo = energy % 2

    def weight_of(step, factor):
        return 0.5 * jnp.sum(jnp.where(shift_steps == step, mode_weight * factor, 0.0))

    weights = jnp.stack(
        [weight_of(s, occupation + 1.0) for s in (1, 2)] + [weight_of(s, occupation) for s in (1, 2)]
    ).astype(jnp.float32)

    gamma = broadening[:, :, None, :]
    sent, own = packed_lesser(x_lo.astype(jnp.int32)[None], green, gamma, n_mom)
    src, coup, coup_t = exchanged(weights, sent, own, coupling)

    moves = [(0, 0), (1, 0), (1, 2), (0, 2)]
    moves = moves + [(lo, mo ^ 1) for lo, mo in moves]
    donors = jnp.stack(
        [(mom ^ mo) * local_k + (x_lo ^ lo) * half + kk for lo, mo in moves for kk in range(half)]
    ).astype(jnp.int32)
    table = jnp.sum(
        jnp.where(
            momentum_map[:, :, None] == donors[None, None, :],
            jnp.arange(points, dtype=jnp.int32)[None, :, None],
            0,
        ),
        axis=1,
    ).astype(jnp.int32)
    table_home = lax.dynamic_slice_in_dim(table, mom * local_k, local_k, 0).reshape(-1)

    us, vs = home_sums(table_home, src, coup, coup_t, local_k)
    return tuple(
        finished(table.reshape(-1), green, gamma, us, vs, src, coupling, n_energy, local_k)
    )


def solution(mesh):
    return jax.shard_map(
        on_device,
        mesh=mesh,
        in_specs=(
            P("mom", "energy", None, None, None),
            P("mom", "energy", None),
            P(None, "mom", None),
            P(),
            P(),
            P(),
            P(),
        ),
        out_specs=(P(None, "energy", None, "mom", None), P("energy", "mom", None, None)),
        check_vma=False,
    )
```

```python
import functools

import jax
import jax.numpy as jnp
from jax import lax
from jax.experimental import pallas as pl
from jax.experimental.pallas import tpu as pltpu
from jax.sharding import PartitionSpec as P

MIB = 1 << 20
NT = (((1,), (1,)), ((), ()))


def dot_nt(left, right):
    return lax.dot_general(left, right, NT, preferred_element_type=jnp.float32)


def dot_nn(left, right):
    return jnp.dot(left, right, preferred_element_type=jnp.float32)


def scale(block, gamma):
    return (block.astype(jnp.float32) * gamma).astype(jnp.bfloat16)


def lesser_kernel(place, green, gamma, *outs):
    norb = green.shape[-1]
    rows = outs[0].shape[3]
    half = gamma.shape[0] // 2
    step = pl.program_id(0)
    gam = gamma[(place[0] + 1 + step // half) % 2 * half + step % half, pl.ds(pl.program_id(1), 1), :]
    g_re, g_im = green[0, 0, 0], green[0, 0, 1]
    wide_re = g_re.astype(jnp.float32)
    wide_im = g_im.astype(jnp.float32)
    less = (wide_re - wide_im).astype(jnp.bfloat16)
    more = (wide_re + wide_im).astype(jnp.bfloat16)
    total = dot_nt(scale(g_re, gam), less) + dot_nt(scale(g_im, gam), more)
    total = total.astype(jnp.bfloat16)
    for side in range(2):

        @pl.when(pl.program_id(0) // 2 == side)
        def _():
            for c in range(norb // rows):
                outs[side][c, 0, 0] = total[c * rows : (c + 1) * rows]


def packed_lesser(place, green, gamma, chunks):
    energies, norb = green.shape[1], green.shape[-1]
    half = green.shape[0] // 2
    rows = norb // chunks

    def which(k, p):
        return ((p[0] + 1 + k // half) % 2) * half + k % half

    def block_of(side):
        def index(k, e, p):
            if side == 0:
                return (0, jnp.minimum(k, half - 1), jnp.where(k < half, e, energies - 1), 0, 0)
            return (0, jnp.maximum(k - half, 0), jnp.where(k < half, 0, e), 0, 0)

        return pl.BlockSpec((chunks, 1, 1, rows, norb), index)

    out = jax.ShapeDtypeStruct((chunks, half, energies, rows, norb), jnp.bfloat16)
    outs = pl.pallas_call(
        lesser_kernel,
        grid_spec=pltpu.PrefetchScalarGridSpec(
            num_scalar_prefetch=1,
            grid=(2 * half, energies),
            in_specs=[
                pl.BlockSpec((1, 1, 2, norb, norb), lambda k, e, p: (which(k, p), e, 0, 0, 0)),
                pl.BlockSpec(gamma.shape, lambda k, e, p: (0, 0, 0)),
            ],
            out_specs=[block_of(0), block_of(1)],
        ),
        out_shape=[out] * 2,
        compiler_params=pltpu.CompilerParams(vmem_limit_bytes=60 * MIB),
        cost_estimate=pl.CostEstimate(
            flops=8 * half * energies * norb**3,
            bytes_accessed=12 * half * energies * norb**2,
            transcendentals=0,
        ),
        name="lesser",
    )(place, green, gamma)
    return outs


def identity(n):
    rows = lax.broadcasted_iota(jnp.int32, (n, n), 0)
    cols = lax.broadcasted_iota(jnp.int32, (n, n), 1)
    return (rows == cols).astype(jnp.float32).astype(jnp.bfloat16)


def exchange_kernel(
    shift_steps, mode_weight, occupation, sent, own, coupling, src, coup, coup_t,
    got, own_halo, got_halo, mine, other, tiles, turned, send, recv, local,
):
    energy, mom = lax.axis_index("energy"), lax.axis_index("mom")
    pairs = lax.axis_size("energy") // 2
    x_lo, pair = energy % 2, energy // 2
    chunks, half, _, rows, norb = sent.shape
    points, height, _ = coupling.shape
    energy_a = energy + 1 - 2 * x_lo
    mom_core = mom + 1 - 2 * (mom % 2)
    mom_hi = mom + 2 - 4 * (mom // 2)
    mom_both = 3 - mom
    place = [mom, mom_core, mom_hi, mom_both]
    ring_a, ring_b, ring_ab = (energy_a, mom), (energy_a, mom_hi), (energy, mom_hi)
    core = (energy, mom_core)
    own_to = (energy - 2 + 4 * x_lo, mom)
    got_to = (energy + 2 - 4 * x_lo, mom)
    low, high = pair > 0, pair < pairs - 1
    first = x_lo == 0
    has_own_to = jnp.logical_or(
        jnp.logical_and(first, low), jnp.logical_and(jnp.logical_not(first), high)
    )
    has_got_to = jnp.logical_or(
        jnp.logical_and(first, high), jnp.logical_and(jnp.logical_not(first), low)
    )

    weights = [0.0] * 4
    for m in range(shift_steps.shape[0]):
        two = shift_steps[m].astype(jnp.float32) - 1.0
        up = 0.5 * mode_weight[m] * (occupation[m] + 1.0)
        down = 0.5 * mode_weight[m] * occupation[m]
        weights[0] += (1.0 - two) * up
        weights[1] += two * up
        weights[2] += (1.0 - two) * down
        weights[3] += two * down

    def remote(kind, c, source, target, device):
        return pltpu.make_async_remote_copy(
            src_ref=source,
            dst_ref=target,
            send_sem=send.at[kind, c],
            recv_sem=recv.at[kind, c],
            device_id=device,
            device_id_type=pl.DeviceIdType.MESH,
        )

    swap = [remote(0, c, sent.at[c], got.at[c], ring_a) for c in range(chunks)]
    to_own = [remote(1, c, own.at[c], own_halo.at[c], own_to) for c in range(chunks)]
    to_got = [remote(2, c, got.at[c], got_halo.at[c], got_to) for c in range(chunks)]
    near = [
        [
            remote(3, c, other.at[c], src.at[c, 1], ring_a),
            remote(4, c, other.at[c], src.at[c, 2], ring_b),
            remote(5, c, mine.at[c], src.at[c, 3], ring_ab),
        ]
        for c in range(chunks)
    ]
    far = [
        [remote(6, c, mine.at[c], src.at[c, 4], core)]
        + [remote(6 + s, c, src.at[c, s], src.at[c, 4 + s], core) for s in (1, 2, 3)]
        for c in range(chunks)
    ]
    stay = [pltpu.make_async_copy(mine.at[c], src.at[c, 0], local.at[c]) for c in range(chunks)]
    tile_core = remote(10, 0, coupling, tiles.at[1], core)
    tile_b = remote(10, 1, coupling, tiles.at[2], ring_b)
    tile_bc = remote(10, 2, tiles.at[2], tiles.at[3], core)
    tile_own = pltpu.make_async_copy(coupling, tiles.at[0], local.at[chunks])
    placed = [
        (
            pltpu.make_async_copy(
                tiles.at[s],
                coup.at[:, pl.ds(pl.multiple_of(place[s] * height, height), height), :],
                local.at[chunks + 1 + 2 * s],
            ),
            pltpu.make_async_copy(
                turned.at[s],
                coup_t.at[:, :, pl.ds(pl.multiple_of(place[s] * height, height), height)],
                local.at[chunks + 2 + 2 * s],
            ),
        )
        for s in range(4)
    ]

    barrier = pltpu.get_barrier_semaphore()

    def greet(device):
        pl.semaphore_signal(
            barrier, inc=1, device_id=device, device_id_type=pl.DeviceIdType.MESH
        )

    for device in (ring_a, ring_b, ring_ab, core):
        greet(device)

    @pl.when(has_own_to)
    def _():
        greet(own_to)

    @pl.when(has_got_to)
    def _():
        greet(got_to)

    pl.semaphore_wait(barrier, 4 + jnp.where(low, 1, 0) + jnp.where(high, 1, 0))

    swap[0].start()
    swap[1].start()

    @pl.when(has_own_to)
    def _():
        for c in range(chunks):
            to_own[c].start()

    tile_b.start()
    tile_core.start()
    tile_own.start()

    step = 16
    slabs = rows // step

    def clear(halo):
        def one(i, carry):
            c, r = i // slabs, i % slabs
            at = pl.ds(pl.multiple_of(r * step, step), step)
            for k in range(half):
                for e in range(2):
                    halo[c, k, e, at, :] = jnp.zeros((step, norb), halo.dtype)
            return carry

        lax.fori_loop(0, chunks * slabs, one, 0)

    @pl.when(jnp.logical_not(has_got_to))
    def _():
        clear(own_halo)

    @pl.when(jnp.logical_not(has_own_to))
    def _():
        clear(got_halo)

    turn = identity(norb // 2)

    def fold(s):
        def one(q, carry):
            for b in range(2):
                span = slice(b * (norb // 2), (b + 1) * (norb // 2))
                turned[s, q, span, :] = dot_nt(turn, tiles[s, q, :, span]).astype(turned.dtype)
            return carry

        lax.fori_loop(0, points, one, 0)
        for copy in placed[s]:
            copy.start()

    def shift(c, parts, outs):
        def one(i, carry):
            k, r = i // slabs, i % slabs
            at = pl.ds(pl.multiple_of(r * step, step), step)
            levels = [ref[c, k, e, at, :].astype(jnp.float32) for ref in parts for e in range(2)]
            for o in range(4):
                total = weights[0] * levels[o + 3] + weights[1] * levels[o + 4]
                total = total + weights[2] * levels[o + 1] + weights[3] * levels[o]
                outs[o // 2][c, k, o % 2, at, :] = total.astype(mine.dtype)
            return carry

        lax.fori_loop(0, half * slabs, one, 0)

    for c in range(chunks + 1):
        if c < chunks:
            swap[c].wait_recv()

            @pl.when(has_got_to)
            def _(copy=to_got[c]):
                copy.start()

            if c + 2 < chunks:
                swap[c + 2].start()
        if c == 0:
            tile_own.wait()
            fold(0)
        else:
            d = c - 1

            @pl.when(has_got_to)
            def _(copy=to_own[d]):
                copy.wait_recv()

            @pl.when(has_own_to)
            def _(copy=to_got[d]):
                copy.wait_recv()

            @pl.when(first)
            def _(d=d):
                shift(d, (got_halo, own, got, own_halo), (mine, other))

            @pl.when(jnp.logical_not(first))
            def _(d=d):
                shift(d, (own_halo, got, own, got_halo), (other, mine))

            for copy in near[d]:
                copy.start()
            far[d][0].start()
            stay[d].start()
        if c == 1:
            tile_core.wait_recv()
            fold(1)

    tile_b.wait_recv()
    tile_bc.start()
    fold(2)
    for c in range(chunks):
        for s in (1, 2, 3):
            near[c][s - 1].wait_recv()
            far[c][s].start()
        if c == 0:
            tile_bc.wait_recv()
            fold(3)
    for c in range(chunks):
        for copy in far[c]:
            copy.wait_recv()
        for copy in [swap[c]] + near[c] + far[c]:
            copy.wait_send()
        stay[c].wait()

        @pl.when(has_own_to)
        def _(copy=to_own[c]):
            copy.wait_send()

        @pl.when(has_got_to)
        def _(copy=to_got[c]):
            copy.wait_send()

    for copy in (tile_core, tile_b, tile_bc):
        copy.wait_send()
    for pair_of in placed:
        for copy in pair_of:
            copy.wait()


def exchanged(shift_steps, mode_weight, occupation, sent, own, coupling):
    chunks, half, energies, rows, norb = sent.shape
    points, height, _ = coupling.shape
    whole = jax.ShapeDtypeStruct((points, norb, norb), jnp.bfloat16)
    vmem = pl.BlockSpec(memory_space=pltpu.VMEM)
    hbm = pl.BlockSpec(memory_space=pl.ANY)
    part = pltpu.VMEM(sent.shape, jnp.bfloat16)
    return pl.pallas_call(
        exchange_kernel,
        in_specs=[pl.BlockSpec(memory_space=pltpu.SMEM)] * 3 + [vmem, vmem, hbm],
        out_specs=[hbm] * 3,
        out_shape=[
            jax.ShapeDtypeStruct((chunks, 8, half, energies, rows, norb), jnp.bfloat16),
            whole,
            whole,
        ],
        scratch_shapes=[part] * 5
        + [
            pltpu.VMEM((4, points, height, norb), jnp.bfloat16),
            pltpu.VMEM((4, points, norb, height), jnp.bfloat16),
            pltpu.SemaphoreType.DMA((11, chunks)),
            pltpu.SemaphoreType.DMA((11, chunks)),
            pltpu.SemaphoreType.DMA((chunks + 9,)),
        ],
        compiler_params=pltpu.CompilerParams(
            collective_id=0, has_side_effects=True, vmem_limit_bytes=60 * MIB
        ),
        name="exchange",
    )(shift_steps, mode_weight, occupation, sent, own, coupling)


def add_products(targets, streams, picks, donor, factor, at, store):
    acc = [[None] * streams for _ in range(targets)]
    kept = {}
    for quad in range(4):
        held = [[donor(4 * quad + d, n, at) for n in range(streams)] for d in range(4)]
        for t in range(targets):
            c = [factor[picks(t, 4 * quad + d), at[0], at[1]] for d in range(4)]
            for n in range(streams):
                part = (c[0] * held[0][n] + c[1] * held[1][n]) + (
                    c[2] * held[2][n] + c[3] * held[3][n]
                )
                if quad % 2 == 0:
                    kept[t, n] = part
                    continue
                part = (kept.pop((t, n)) + part).astype(jnp.float32)
                acc[t][n] = part if acc[t][n] is None else acc[t][n] + part
    for t in range(targets):
        for n in range(streams):
            store(t, n, at, acc[t][n])


def home_kernel(table, *refs):
    sources, coup, coup_t, out, out_t = refs
    targets, _, height, norb = out.shape
    home = lax.axis_index("mom") * targets

    def picks(t, d):
        return table[home + t, d]

    def donor(d, n, at):
        return sources[0, d // 2, d % 2, n, at[0], at[1]]

    def into(ref):
        def store(t, n, at, value):
            ref[t, n, at[0], at[1]] = value.astype(jnp.bfloat16)

        return store

    def slab(i, carry):
        at = (
            pl.ds(pl.multiple_of(i // 2 * 16, 16), 16),
            pl.ds(pl.multiple_of(i % 2 * (norb // 2), norb // 2), norb // 2),
        )
        add_products(targets, 2, picks, donor, coup, at, into(out))
        add_products(targets, 2, picks, donor, coup_t, at, into(out_t))
        return carry

    lax.fori_loop(0, height // 16 * 2, slab, 0)


def home_sums(table, src, coup, coup_t, targets):
    chunks, _, half, energies, rows, norb = src.shape
    points = coup.shape[0]
    height = rows // 2
    steps = rows // height
    given = pl.BlockSpec(
        (1, 8, half, energies, height, norb), lambda i, q: (i // steps, 0, 0, 0, i % steps, 0)
    )
    factor = pl.BlockSpec((points, height, norb), lambda i, q: (0, i, 0))
    result = pl.BlockSpec((targets, energies, height, norb), lambda i, q: (0, 0, i, 0))
    out = jax.ShapeDtypeStruct((targets, energies, chunks * rows, norb), jnp.bfloat16)
    return pl.pallas_call(
        home_kernel,
        grid_spec=pltpu.PrefetchScalarGridSpec(
            num_scalar_prefetch=1,
            grid=(chunks * steps,),
            in_specs=[given] + [factor] * 2,
            out_specs=[result] * 2,
        ),
        out_shape=[out, out],
        compiler_params=pltpu.CompilerParams(vmem_limit_bytes=60 * MIB),
        name="home",
    )(table, src, coup, coup_t)


def finish_kernel(
    inverse, table, green, gamma, us, vs, rows_of, cols_of, coup, out, density,
    source, part, came, send, recv,
):
    energy, mom = lax.axis_index("energy"), lax.axis_index("mom")
    owners = lax.axis_size("energy")
    packs = part.shape[0]
    count = packs * 2
    targets, _, _, height, norb = out.shape
    index = pl.program_id(0)
    pack = jnp.minimum(index, count - 1) // 2

    @pl.when(index == 0)
    def _():
        barrier = pltpu.get_barrier_semaphore()

        def greet(n, carry):
            pl.semaphore_signal(
                barrier,
                inc=1,
                device_id=((energy + n) % owners, mom),
                device_id_type=pl.DeviceIdType.MESH,
            )
            return carry

        lax.fori_loop(1, owners, greet, 0)
        pl.semaphore_wait(barrier, owners - 1)

    @pl.when(index < count)
    def _():
        d_re = d_im = None
        for e in range(green.shape[1]):
            g_re, g_im = green[0, e, 0], green[0, e, 1]
            gam = gamma[index, e : e + 1, :]
            wide_re, wide_im = g_re.astype(jnp.float32), g_im.astype(jnp.float32)
            less = (wide_re - wide_im).astype(jnp.bfloat16)
            more = (wide_re + wide_im).astype(jnp.bfloat16)
            u, v = us[0, e], vs[0, e]
            m_re = dot_nn(less, u) + dot_nt(more, v) + scale(g_re, gam).astype(jnp.float32)
            m_im = dot_nn(more, u) - dot_nt(less, v) + scale(g_im, gam).astype(jnp.float32)
            m_re, m_im = m_re.astype(jnp.bfloat16), m_im.astype(jnp.bfloat16)
            one = dot_nt(m_re, g_re) + dot_nt(m_im, g_im)
            two = dot_nt(m_im, g_re) - dot_nt(m_re, g_im)
            d_re = one if d_re is None else d_re + one
            d_im = two if d_im is None else d_im + two
        shape = (owners, norb // owners, norb)
        part[pack, :, index % 2, 0] = (d_re * inverse).astype(jnp.bfloat16).reshape(shape)
        part[pack, :, index % 2, 1] = (d_im * inverse).astype(jnp.bfloat16).reshape(shape)

    @pl.when(jnp.logical_and(index < count, index % 2 == 1))
    def _():
        came[pack, energy] = part[pack, energy]

        def post(n, carry):
            peer = (energy + n) % owners
            pltpu.make_async_remote_copy(
                src_ref=part.at[pack, peer],
                dst_ref=came.at[pack, energy],
                send_sem=send.at[pack],
                recv_sem=recv.at[pack],
                device_id=(peer, mom),
                device_id_type=pl.DeviceIdType.MESH,
            ).start()
            return carry

        lax.fori_loop(1, owners, post, 0)

    place = index - count
    group = place % 4 * targets

    @pl.when(jnp.logical_and(index >= count, place % 4 == 0))
    def _():
        turn = identity(height)
        for d in range(16):
            for b in range(norb // height):
                span = slice(b * height, (b + 1) * height)
                straight = rows_of[0, d // 2, d % 2, 0, :, span].astype(jnp.float32)
                turned = dot_nt(turn, cols_of[b, d // 2, d % 2, 0])
                source[d, 0, :, span] = (straight + turned).astype(jnp.bfloat16)
                source[d, 1, :, span] = (straight - turned).astype(jnp.bfloat16)

    def picks(t, d):
        return table[group + t, d]

    def donor(d, n, at):
        return source[d, n, at[0], at[1]]

    def store(t, n, at, value):
        out[t, 0, n, at[0], at[1]] = value.astype(jnp.bfloat16)

    @pl.when(index >= count)
    def _():
        def slab(i, carry):
            at = (
                pl.ds(pl.multiple_of(i // 2 * 16, 16), 16),
                pl.ds(pl.multiple_of(i % 2 * (norb // 2), norb // 2), norb // 2),
            )
            add_products(targets, 2, picks, donor, coup, at, store)
            return carry

        lax.fori_loop(0, height // 16 * 2, slab, 0)

    @pl.when(index == pl.num_programs(0) - 1)
    def _():
        for k in range(packs):
            every = pltpu.make_async_remote_copy(
                src_ref=part.at[k, pl.ds(0, owners - 1)],
                dst_ref=came.at[k, pl.ds(0, owners - 1)],
                send_sem=send.at[k],
                recv_sem=recv.at[k],
                device_id=((energy + 1) % owners, mom),
                device_id_type=pl.DeviceIdType.MESH,
            )
            every.wait_recv()
            every.wait_send()

            def add(n, total):
                return total + came[k, n].astype(jnp.float32)

            total = lax.fori_loop(1, owners, add, came[k, 0].astype(jnp.float32))
            for kk in range(2):
                for c in range(2):
                    density[:, 2 * k + kk, c, :] = total[kk, c]


def finished(table, green, gamma, us, vs, src, coupling, owners, targets):
    chunks, _, half, energies, rows, norb = src.shape
    points, height, _ = coupling.shape
    count = green.shape[0]
    own_rows = norb // owners
    groups = points // targets

    def of_k(i):
        return jnp.minimum(i, count - 1)

    def of_e(i):
        return jnp.maximum(i - count, 0) // groups

    def of_g(i):
        return jnp.maximum(i - count, 0) % groups

    part = pl.BlockSpec((1, energies, norb, norb), lambda i: (of_k(i), 0, 0, 0))
    return pl.pallas_call(
        functools.partial(finish_kernel, 1.0 / (energies * owners)),
        grid=(count + energies * groups,),
        in_specs=[
            pl.BlockSpec(memory_space=pltpu.SMEM),
            pl.BlockSpec((1, energies, 2, norb, norb), lambda i: (of_k(i), 0, 0, 0, 0)),
            pl.BlockSpec(gamma.shape, lambda i: (0, 0, 0)),
            part,
            part,
            pl.BlockSpec(
                (1, 8, half, 1, rows, norb),
                lambda i: (lax.axis_index("mom"), 0, 0, of_e(i), 0, 0),
            ),
            pl.BlockSpec(
                (chunks, 8, half, 1, rows, height),
                lambda i: (0, 0, 0, of_e(i), 0, lax.axis_index("mom")),
            ),
            pl.BlockSpec((points, height, norb), lambda i: (0, 0, 0)),
        ],
        out_specs=[
            pl.BlockSpec((targets, 1, 2, height, norb), lambda i: (of_g(i), of_e(i), 0, 0, 0)),
            pl.BlockSpec((own_rows, count, 2, norb), lambda i: (0, 0, 0, 0)),
        ],
        out_shape=[
            jax.ShapeDtypeStruct((points, energies, 2, height, norb), jnp.bfloat16),
            jax.ShapeDtypeStruct((own_rows, count, 2, norb), jnp.float32),
        ],
        scratch_shapes=[
            pltpu.VMEM((16, 2, height, norb), jnp.bfloat16),
            pltpu.VMEM((count // 2, owners, 2, 2, own_rows, norb), jnp.bfloat16),
            pltpu.VMEM((count // 2, owners, 2, 2, own_rows, norb), jnp.bfloat16),
            pltpu.SemaphoreType.DMA((count // 2,)),
            pltpu.SemaphoreType.DMA((count // 2,)),
        ],
        compiler_params=pltpu.CompilerParams(
            collective_id=1, has_side_effects=True, vmem_limit_bytes=60 * MIB
        ),
        name="finish",
    )(table, green, gamma, us, vs, src, src, coupling)


def on_device(green, broadening, coupling, shift_steps, mode_weight, occupation, momentum_map):
    n_energy, n_mom = lax.axis_size("energy"), lax.axis_size("mom")
    local_k = green.shape[0]
    half = local_k // 2
    points = momentum_map.shape[1]
    energy, mom = lax.axis_index("energy"), lax.axis_index("mom")
    x_lo = energy % 2

    sent, own = packed_lesser(x_lo.astype(jnp.int32)[None], green, broadening, n_mom)
    src, coup, coup_t = exchanged(
        shift_steps, mode_weight, occupation, sent, own, coupling
    )

    moves = [(0, 0), (1, 0), (1, 2), (0, 2)]
    moves = moves + [(lo, mo ^ 1) for lo, mo in moves]
    donors = jnp.stack(
        [(mom ^ mo) * local_k + (x_lo ^ lo) * half + kk for lo, mo in moves for kk in range(half)]
    ).astype(jnp.int32)
    table = jnp.sum(
        jnp.where(
            momentum_map[:, :, None] == donors[None, None, :],
            jnp.arange(points, dtype=jnp.int32)[None, :, None],
            0,
        ),
        axis=1,
    ).astype(jnp.int32)
    us, vs = home_sums(table, src, coup, coup_t, local_k)
    return tuple(
        finished(table, green, broadening, us, vs, src, coupling, n_energy, local_k)
    )


def solution(mesh):
    return jax.shard_map(
        on_device,
        mesh=mesh,
        in_specs=(
            P("mom", "energy", None, None, None),
            P("mom", "energy", None),
            P(None, "mom", None),
            P(),
            P(),
            P(),
            P(),
        ),
        out_specs=(P(None, "energy", None, "mom", None), P("energy", "mom", None, None)),
        check_vma=False,
    )
```

```python
import functools

import jax
import jax.numpy as jnp
from jax import lax
from jax.experimental import pallas as pl
from jax.experimental.pallas import tpu as pltpu
from jax.sharding import PartitionSpec as P

MIB = 1 << 20
NT = (((1,), (1,)), ((), ()))


def dot_nt(left, right):
    return lax.dot_general(left, right, NT, preferred_element_type=jnp.float32)


def dot_nn(left, right):
    return jnp.dot(left, right, preferred_element_type=jnp.float32)


def scale(block, gamma):
    return (block.astype(jnp.float32) * gamma).astype(jnp.bfloat16)


def lesser_kernel(place, green, gamma, *outs):
    norb = green.shape[-1]
    rows = outs[0].shape[3]
    half = gamma.shape[0] // 2
    step = pl.program_id(0)
    gam = gamma[(place[0] + 1 + step // half) % 2 * half + step % half, pl.ds(pl.program_id(1), 1), :]
    g_re, g_im = green[0, 0, 0], green[0, 0, 1]
    wide_re = g_re.astype(jnp.float32)
    wide_im = g_im.astype(jnp.float32)
    less = (wide_re - wide_im).astype(jnp.bfloat16)
    more = (wide_re + wide_im).astype(jnp.bfloat16)
    total = dot_nt(scale(g_re, gam), less) + dot_nt(scale(g_im, gam), more)
    total = total.astype(jnp.bfloat16)
    for side in range(2):

        @pl.when(pl.program_id(0) // 2 == side)
        def _():
            for c in range(norb // rows):
                outs[side][c, 0, 0] = total[c * rows : (c + 1) * rows]


def packed_lesser(place, green, gamma, chunks):
    energies, norb = green.shape[1], green.shape[-1]
    half = green.shape[0] // 2
    rows = norb // chunks

    def which(k, p):
        return ((p[0] + 1 + k // half) % 2) * half + k % half

    def block_of(side):
        def index(k, e, p):
            if side == 0:
                return (0, jnp.minimum(k, half - 1), jnp.where(k < half, e, energies - 1), 0, 0)
            return (0, jnp.maximum(k - half, 0), jnp.where(k < half, 0, e), 0, 0)

        return pl.BlockSpec((chunks, 1, 1, rows, norb), index)

    out = jax.ShapeDtypeStruct((chunks, half, energies, rows, norb), jnp.bfloat16)
    outs = pl.pallas_call(
        lesser_kernel,
        grid_spec=pltpu.PrefetchScalarGridSpec(
            num_scalar_prefetch=1,
            grid=(2 * half, energies),
            in_specs=[
                pl.BlockSpec((1, 1, 2, norb, norb), lambda k, e, p: (which(k, p), e, 0, 0, 0)),
                pl.BlockSpec(gamma.shape, lambda k, e, p: (0, 0, 0)),
            ],
            out_specs=[block_of(0), block_of(1)],
        ),
        out_shape=[out] * 2,
        compiler_params=pltpu.CompilerParams(vmem_limit_bytes=60 * MIB),
        cost_estimate=pl.CostEstimate(
            flops=8 * half * energies * norb**3,
            bytes_accessed=12 * half * energies * norb**2,
            transcendentals=0,
        ),
        name="lesser",
    )(place, green, gamma)
    return outs


def identity(n):
    rows = lax.broadcasted_iota(jnp.int32, (n, n), 0)
    cols = lax.broadcasted_iota(jnp.int32, (n, n), 1)
    return (rows == cols).astype(jnp.float32).astype(jnp.bfloat16)


def exchange_kernel(
    shift_steps, mode_weight, occupation, sent, own, coupling, src, coup, coup_t,
    got, own_halo, got_halo, mine, other, tiles, turned, send, recv, local,
):
    energy, mom = lax.axis_index("energy"), lax.axis_index("mom")
    pairs = lax.axis_size("energy") // 2
    x_lo, pair = energy % 2, energy // 2
    chunks, half, _, rows, norb = sent.shape
    points, height, _ = coupling.shape
    energy_a = energy + 1 - 2 * x_lo
    mom_core = mom + 1 - 2 * (mom % 2)
    mom_hi = mom + 2 - 4 * (mom // 2)
    mom_both = 3 - mom
    place = [mom, mom_core, mom_hi, mom_both]
    ring_a, ring_b, ring_ab = (energy_a, mom), (energy_a, mom_hi), (energy, mom_hi)
    core = (energy, mom_core)
    own_to = (energy - 2 + 4 * x_lo, mom)
    got_to = (energy + 2 - 4 * x_lo, mom)
    low, high = pair > 0, pair < pairs - 1
    first = x_lo == 0
    has_own_to = jnp.logical_or(
        jnp.logical_and(first, low), jnp.logical_and(jnp.logical_not(first), high)
    )
    has_got_to = jnp.logical_or(
        jnp.logical_and(first, high), jnp.logical_and(jnp.logical_not(first), low)
    )

    weights = [0.0] * 4
    for m in range(shift_steps.shape[0]):
        two = shift_steps[m].astype(jnp.float32) - 1.0
        up = 0.5 * mode_weight[m] * (occupation[m] + 1.0)
        down = 0.5 * mode_weight[m] * occupation[m]
        weights[0] += (1.0 - two) * up
        weights[1] += two * up
        weights[2] += (1.0 - two) * down
        weights[3] += two * down

    def remote(kind, c, source, target, device):
        return pltpu.make_async_remote_copy(
            src_ref=source,
            dst_ref=target,
            send_sem=send.at[kind, c],
            recv_sem=recv.at[kind, c],
            device_id=device,
            device_id_type=pl.DeviceIdType.MESH,
        )

    swap = [remote(0, c, sent.at[c], got.at[c], ring_a) for c in range(chunks)]
    to_own = [remote(1, c, own.at[c], own_halo.at[c], own_to) for c in range(chunks)]
    to_got = [remote(2, c, got.at[c], got_halo.at[c], got_to) for c in range(chunks)]
    near = [
        [
            remote(3, c, other.at[c], src.at[c, 1], ring_a),
            remote(4, c, other.at[c], src.at[c, 2], ring_b),
            remote(5, c, mine.at[c], src.at[c, 3], ring_ab),
        ]
        for c in range(chunks)
    ]
    far = [
        [remote(6, c, mine.at[c], src.at[c, 4], core)]
        + [remote(6 + s, c, src.at[c, s], src.at[c, 4 + s], core) for s in (1, 2, 3)]
        for c in range(chunks)
    ]
    stay = [pltpu.make_async_copy(mine.at[c], src.at[c, 0], local.at[c]) for c in range(chunks)]
    tile_core = remote(10, 0, coupling, tiles.at[1], core)
    tile_b = remote(10, 1, coupling, tiles.at[2], ring_b)
    tile_bc = remote(10, 2, tiles.at[2], tiles.at[3], core)
    tile_own = pltpu.make_async_copy(coupling, tiles.at[0], local.at[chunks])
    placed = [
        (
            pltpu.make_async_copy(
                tiles.at[s],
                coup.at[:, pl.ds(pl.multiple_of(place[s] * height, height), height), :],
                local.at[chunks + 1 + 2 * s],
            ),
            pltpu.make_async_copy(
                turned.at[s],
                coup_t.at[:, :, pl.ds(pl.multiple_of(place[s] * height, height), height)],
                local.at[chunks + 2 + 2 * s],
            ),
        )
        for s in range(4)
    ]

    barrier = pltpu.get_barrier_semaphore()

    def greet(device):
        pl.semaphore_signal(
            barrier, inc=1, device_id=device, device_id_type=pl.DeviceIdType.MESH
        )

    for device in (ring_a, ring_b, ring_ab, core):
        greet(device)

    @pl.when(has_own_to)
    def _():
        greet(own_to)

    @pl.when(has_got_to)
    def _():
        greet(got_to)

    pl.semaphore_wait(barrier, 4 + jnp.where(low, 1, 0) + jnp.where(high, 1, 0))

    swap[0].start()
    swap[1].start()

    @pl.when(has_own_to)
    def _():
        for c in range(chunks):
            to_own[c].start()

    tile_b.start()
    tile_core.start()
    tile_own.start()

    step = 16
    slabs = rows // step

    def clear(halo):
        def one(i, carry):
            c, r = i // slabs, i % slabs
            at = pl.ds(pl.multiple_of(r * step, step), step)
            for k in range(half):
                for e in range(2):
                    halo[c, k, e, at, :] = jnp.zeros((step, norb), halo.dtype)
            return carry

        lax.fori_loop(0, chunks * slabs, one, 0)

    @pl.when(jnp.logical_not(has_got_to))
    def _():
        clear(own_halo)

    @pl.when(jnp.logical_not(has_own_to))
    def _():
        clear(got_halo)

    turn = identity(norb // 2)

    def fold(s):
        def one(q, carry):
            for b in range(2):
                span = slice(b * (norb // 2), (b + 1) * (norb // 2))
                turned[s, q, span, :] = dot_nt(turn, tiles[s, q, :, span]).astype(turned.dtype)
            return carry

        lax.fori_loop(0, points, one, 0)
        for copy in placed[s]:
            copy.start()

    def shift(c, parts, outs):
        def one(i, carry):
            k, r = i // slabs, i % slabs
            at = pl.ds(pl.multiple_of(r * step, step), step)
            levels = [ref[c, k, e, at, :].astype(jnp.float32) for ref in parts for e in range(2)]
            for o in range(4):
                total = weights[0] * levels[o + 3] + weights[1] * levels[o + 4]
                total = total + weights[2] * levels[o + 1] + weights[3] * levels[o]
                outs[o // 2][c, k, o % 2, at, :] = total.astype(mine.dtype)
            return carry

        lax.fori_loop(0, half * slabs, one, 0)

    for c in range(chunks + 1):
        if c < chunks:
            swap[c].wait_recv()

            @pl.when(has_got_to)
            def _(copy=to_got[c]):
                copy.start()

            if c + 2 < chunks:
                swap[c + 2].start()
        if c == 0:
            tile_own.wait()
            fold(0)
        else:
            d = c - 1

            @pl.when(has_got_to)
            def _(copy=to_own[d]):
                copy.wait_recv()

            @pl.when(has_own_to)
            def _(copy=to_got[d]):
                copy.wait_recv()

            @pl.when(first)
            def _(d=d):
                shift(d, (got_halo, own, got, own_halo), (mine, other))

            @pl.when(jnp.logical_not(first))
            def _(d=d):
                shift(d, (own_halo, got, own, got_halo), (other, mine))

            for copy in near[d]:
                copy.start()
            far[d][0].start()
            stay[d].start()
        if c == 1:
            tile_core.wait_recv()
            fold(1)

    tile_b.wait_recv()
    tile_bc.start()
    fold(2)
    for c in range(chunks):
        for s in (1, 2, 3):
            near[c][s - 1].wait_recv()
            far[c][s].start()
        if c == 0:
            tile_bc.wait_recv()
            fold(3)
    for c in range(chunks):
        for copy in far[c]:
            copy.wait_recv()
        for copy in [swap[c]] + near[c] + far[c]:
            copy.wait_send()
        stay[c].wait()

        @pl.when(has_own_to)
        def _(copy=to_own[c]):
            copy.wait_send()

        @pl.when(has_got_to)
        def _(copy=to_got[c]):
            copy.wait_send()

    for copy in (tile_core, tile_b, tile_bc):
        copy.wait_send()
    for pair_of in placed:
        for copy in pair_of:
            copy.wait()


def exchanged(shift_steps, mode_weight, occupation, sent, own, coupling):
    chunks, half, energies, rows, norb = sent.shape
    points, height, _ = coupling.shape
    whole = jax.ShapeDtypeStruct((points, norb, norb), jnp.bfloat16)
    vmem = pl.BlockSpec(memory_space=pltpu.VMEM)
    hbm = pl.BlockSpec(memory_space=pl.ANY)
    part = pltpu.VMEM(sent.shape, jnp.bfloat16)
    return pl.pallas_call(
        exchange_kernel,
        in_specs=[pl.BlockSpec(memory_space=pltpu.SMEM)] * 3 + [vmem, vmem, hbm],
        out_specs=[hbm] * 3,
        out_shape=[
            jax.ShapeDtypeStruct((chunks, 8, half, energies, rows, norb), jnp.bfloat16),
            whole,
            whole,
        ],
        scratch_shapes=[part] * 5
        + [
            pltpu.VMEM((4, points, height, norb), jnp.bfloat16),
            pltpu.VMEM((4, points, norb, height), jnp.bfloat16),
            pltpu.SemaphoreType.DMA((11, chunks)),
            pltpu.SemaphoreType.DMA((11, chunks)),
            pltpu.SemaphoreType.DMA((chunks + 9,)),
        ],
        compiler_params=pltpu.CompilerParams(
            collective_id=0, has_side_effects=True, vmem_limit_bytes=60 * MIB
        ),
        name="exchange",
    )(shift_steps, mode_weight, occupation, sent, own, coupling)


def add_products(targets, streams, picks, donor, factor, at, store):
    acc = [[None] * streams for _ in range(targets)]
    kept = {}
    for quad in range(4):
        held = [[donor(4 * quad + d, n, at) for n in range(streams)] for d in range(4)]
        for t in range(targets):
            c = [factor[picks(t, 4 * quad + d), at[0], at[1]] for d in range(4)]
            for n in range(streams):
                part = (c[0] * held[0][n] + c[1] * held[1][n]) + (
                    c[2] * held[2][n] + c[3] * held[3][n]
                )
                if quad % 2 == 0:
                    kept[t, n] = part
                    continue
                part = (kept.pop((t, n)) + part).astype(jnp.float32)
                acc[t][n] = part if acc[t][n] is None else acc[t][n] + part
    for t in range(targets):
        for n in range(streams):
            store(t, n, at, acc[t][n])


def home_kernel(table, *refs):
    sources, coup, coup_t, out, out_t = refs
    targets, _, height, norb = out.shape
    home = lax.axis_index("mom") * targets

    def picks(t, d):
        return table[home + t, d]

    def donor(d, n, at):
        return sources[0, d // 2, d % 2, n, at[0], at[1]]

    def into(ref):
        def store(t, n, at, value):
            ref[t, n, at[0], at[1]] = value.astype(jnp.bfloat16)

        return store

    def slab(i, carry):
        at = (
            pl.ds(pl.multiple_of(i // 2 * 16, 16), 16),
            pl.ds(pl.multiple_of(i % 2 * (norb // 2), norb // 2), norb // 2),
        )
        add_products(targets, 2, picks, donor, coup, at, into(out))
        add_products(targets, 2, picks, donor, coup_t, at, into(out_t))
        return carry

    lax.fori_loop(0, height // 16 * 2, slab, 0)


def home_sums(table, src, coup, coup_t, targets):
    chunks, _, half, energies, rows, norb = src.shape
    points = coup.shape[0]
    height = rows // 2
    steps = rows // height
    given = pl.BlockSpec(
        (1, 8, half, energies, height, norb), lambda i, q: (i // steps, 0, 0, 0, i % steps, 0)
    )
    factor = pl.BlockSpec((points, height, norb), lambda i, q: (0, i, 0))
    result = pl.BlockSpec((targets, energies, height, norb), lambda i, q: (0, 0, i, 0))
    out = jax.ShapeDtypeStruct((targets, energies, chunks * rows, norb), jnp.bfloat16)
    return pl.pallas_call(
        home_kernel,
        grid_spec=pltpu.PrefetchScalarGridSpec(
            num_scalar_prefetch=1,
            grid=(chunks * steps,),
            in_specs=[given] + [factor] * 2,
            out_specs=[result] * 2,
        ),
        out_shape=[out, out],
        compiler_params=pltpu.CompilerParams(vmem_limit_bytes=60 * MIB),
        name="home",
    )(table, src, coup, coup_t)


def finish_kernel(
    inverse, table, green, gamma, us, vs, rows_of, cols_of, coup, out, density,
    source, part, came, send, recv,
):
    energy, mom = lax.axis_index("energy"), lax.axis_index("mom")
    owners = lax.axis_size("energy")
    count = part.shape[0]
    targets, _, _, height, norb = out.shape
    index = pl.program_id(0)

    @pl.when(index == 0)
    def _():
        barrier = pltpu.get_barrier_semaphore()

        def greet(n, carry):
            pl.semaphore_signal(
                barrier,
                inc=1,
                device_id=((energy + n) % owners, mom),
                device_id_type=pl.DeviceIdType.MESH,
            )
            return carry

        lax.fori_loop(1, owners, greet, 0)
        pl.semaphore_wait(barrier, owners - 1)

    @pl.when(index < count)
    def _():
        d_re = d_im = None
        for e in range(green.shape[1]):
            g_re, g_im = green[0, e, 0], green[0, e, 1]
            gam = gamma[index, e : e + 1, :]
            wide_re, wide_im = g_re.astype(jnp.float32), g_im.astype(jnp.float32)
            less = (wide_re - wide_im).astype(jnp.bfloat16)
            more = (wide_re + wide_im).astype(jnp.bfloat16)
            u, v = us[0, e], vs[0, e]
            m_re = dot_nn(less, u) + dot_nt(more, v) + scale(g_re, gam).astype(jnp.float32)
            m_im = dot_nn(more, u) - dot_nt(less, v) + scale(g_im, gam).astype(jnp.float32)
            m_re, m_im = m_re.astype(jnp.bfloat16), m_im.astype(jnp.bfloat16)
            one = dot_nt(m_re, g_re) + dot_nt(m_im, g_im)
            two = dot_nt(m_im, g_re) - dot_nt(m_re, g_im)
            d_re = one if d_re is None else d_re + one
            d_im = two if d_im is None else d_im + two
        shape = (owners, norb // owners, norb)
        part[index, :, 0] = (d_re * inverse).astype(jnp.bfloat16).reshape(shape)
        part[index, :, 1] = (d_im * inverse).astype(jnp.bfloat16).reshape(shape)
        came[index, energy] = part[index, energy]

        def post(n, carry):
            peer = (energy + n * 13) % owners
            pltpu.make_async_remote_copy(
                src_ref=part.at[index, peer],
                dst_ref=came.at[index, energy],
                send_sem=send.at[index],
                recv_sem=recv.at[index],
                device_id=(peer, mom),
                device_id_type=pl.DeviceIdType.MESH,
            ).start()
            return carry

        lax.fori_loop(1, owners, post, 0)

    place = index - count
    group = place % 4 * targets

    @pl.when(jnp.logical_and(index >= count, place % 4 == 0))
    def _():
        turn = identity(height)
        for d in range(16):
            for b in range(norb // height):
                span = slice(b * height, (b + 1) * height)
                straight = rows_of[0, d // 2, d % 2, 0, :, span].astype(jnp.float32)
                turned = dot_nt(turn, cols_of[b, d // 2, d % 2, 0])
                source[d, 0, :, span] = (straight + turned).astype(jnp.bfloat16)
                source[d, 1, :, span] = (straight - turned).astype(jnp.bfloat16)

    def picks(t, d):
        return table[group + t, d]

    def donor(d, n, at):
        return source[d, n, at[0], at[1]]

    def store(t, n, at, value):
        out[t, 0, n, at[0], at[1]] = value.astype(jnp.bfloat16)

    @pl.when(index >= count)
    def _():
        def slab(i, carry):
            at = (
                pl.ds(pl.multiple_of(i // 2 * 16, 16), 16),
                pl.ds(pl.multiple_of(i % 2 * (norb // 2), norb // 2), norb // 2),
            )
            add_products(targets, 2, picks, donor, coup, at, store)
            return carry

        lax.fori_loop(0, height // 16 * 2, slab, 0)

    @pl.when(index == pl.num_programs(0) - 1)
    def _():
        for k in range(count):
            every = pltpu.make_async_remote_copy(
                src_ref=part.at[k, pl.ds(0, owners - 1)],
                dst_ref=came.at[k, pl.ds(0, owners - 1)],
                send_sem=send.at[k],
                recv_sem=recv.at[k],
                device_id=((energy + 1) % owners, mom),
                device_id_type=pl.DeviceIdType.MESH,
            )
            every.wait_recv()
            every.wait_send()

            def add(n, total):
                return total + came[k, n].astype(jnp.float32)

            total = lax.fori_loop(1, owners, add, came[k, 0].astype(jnp.float32))
            for c in range(2):
                density[:, k, c, :] = total[c]


def finished(table, green, gamma, us, vs, src, coupling, owners, targets):
    chunks, _, half, energies, rows, norb = src.shape
    points, height, _ = coupling.shape
    count = green.shape[0]
    own_rows = norb // owners
    groups = points // targets

    def of_k(i):
        return jnp.minimum(i, count - 1)

    def of_e(i):
        return jnp.maximum(i - count, 0) // groups

    def of_g(i):
        return jnp.maximum(i - count, 0) % groups

    part = pl.BlockSpec((1, energies, norb, norb), lambda i: (of_k(i), 0, 0, 0))
    return pl.pallas_call(
        functools.partial(finish_kernel, 1.0 / (energies * owners)),
        grid=(count + energies * groups,),
        in_specs=[
            pl.BlockSpec(memory_space=pltpu.SMEM),
            pl.BlockSpec((1, energies, 2, norb, norb), lambda i: (of_k(i), 0, 0, 0, 0)),
            pl.BlockSpec(gamma.shape, lambda i: (0, 0, 0)),
            part,
            part,
            pl.BlockSpec(
                (1, 8, half, 1, rows, norb),
                lambda i: (lax.axis_index("mom"), 0, 0, of_e(i), 0, 0),
            ),
            pl.BlockSpec(
                (chunks, 8, half, 1, rows, height),
                lambda i: (0, 0, 0, of_e(i), 0, lax.axis_index("mom")),
            ),
            pl.BlockSpec((points, height, norb), lambda i: (0, 0, 0)),
        ],
        out_specs=[
            pl.BlockSpec((targets, 1, 2, height, norb), lambda i: (of_g(i), of_e(i), 0, 0, 0)),
            pl.BlockSpec((own_rows, count, 2, norb), lambda i: (0, 0, 0, 0)),
        ],
        out_shape=[
            jax.ShapeDtypeStruct((points, energies, 2, height, norb), jnp.bfloat16),
            jax.ShapeDtypeStruct((own_rows, count, 2, norb), jnp.float32),
        ],
        scratch_shapes=[
            pltpu.VMEM((16, 2, height, norb), jnp.bfloat16),
            pltpu.VMEM((count, owners, 2, own_rows, norb), jnp.bfloat16),
            pltpu.VMEM((count, owners, 2, own_rows, norb), jnp.bfloat16),
            pltpu.SemaphoreType.DMA((count,)),
            pltpu.SemaphoreType.DMA((count,)),
        ],
        compiler_params=pltpu.CompilerParams(
            collective_id=1, has_side_effects=True, vmem_limit_bytes=60 * MIB
        ),
        name="finish",
    )(table, green, gamma, us, vs, src, src, coupling)


def on_device(green, broadening, coupling, shift_steps, mode_weight, occupation, momentum_map):
    n_energy, n_mom = lax.axis_size("energy"), lax.axis_size("mom")
    local_k = green.shape[0]
    half = local_k // 2
    points = momentum_map.shape[1]
    energy, mom = lax.axis_index("energy"), lax.axis_index("mom")
    x_lo = energy % 2

    sent, own = packed_lesser(x_lo.astype(jnp.int32)[None], green, broadening, n_mom)
    src, coup, coup_t = exchanged(
        shift_steps, mode_weight, occupation, sent, own, coupling
    )

    moves = [(0, 0), (1, 0), (1, 2), (0, 2)]
    moves = moves + [(lo, mo ^ 1) for lo, mo in moves]
    donors = jnp.stack(
        [(mom ^ mo) * local_k + (x_lo ^ lo) * half + kk for lo, mo in moves for kk in range(half)]
    ).astype(jnp.int32)
    table = jnp.sum(
        jnp.where(
            momentum_map[:, :, None] == donors[None, None, :],
            jnp.arange(points, dtype=jnp.int32)[None, :, None],
            0,
        ),
        axis=1,
    ).astype(jnp.int32)
    us, vs = home_sums(table, src, coup, coup_t, local_k)
    return tuple(
        finished(table, green, broadening, us, vs, src, coupling, n_energy, local_k)
    )


def solution(mesh):
    return jax.shard_map(
        on_device,
        mesh=mesh,
        in_specs=(
            P("mom", "energy", None, None, None),
            P("mom", "energy", None),
            P(None, "mom", None),
            P(),
            P(),
            P(),
            P(),
        ),
        out_specs=(P(None, "energy", None, "mom", None), P("energy", "mom", None, None)),
        check_vma=False,
    )
```

```python
import functools

import jax
import jax.numpy as jnp
from jax import lax
from jax.experimental import pallas as pl
from jax.experimental.pallas import tpu as pltpu
from jax.sharding import PartitionSpec as P

MIB = 1 << 20
NT = (((1,), (1,)), ((), ()))


def dot_nt(left, right):
    return lax.dot_general(left, right, NT, preferred_element_type=jnp.float32)


def dot_nn(left, right):
    return jnp.dot(left, right, preferred_element_type=jnp.float32)


def scale(block, gamma):
    return (block.astype(jnp.float32) * gamma).astype(jnp.bfloat16)


def lesser_kernel(place, green, gamma, *outs):
    norb = green.shape[-1]
    rows = outs[0].shape[3]
    half = gamma.shape[0] // 2
    step = pl.program_id(0)
    gam = gamma[(place[0] + 1 + step // half) % 2 * half + step % half, pl.ds(pl.program_id(1), 1), :]
    g_re, g_im = green[0, 0, 0], green[0, 0, 1]
    wide_re = g_re.astype(jnp.float32)
    wide_im = g_im.astype(jnp.float32)
    less = (wide_re - wide_im).astype(jnp.bfloat16)
    more = (wide_re + wide_im).astype(jnp.bfloat16)
    total = dot_nt(scale(g_re, gam), less) + dot_nt(scale(g_im, gam), more)
    total = total.astype(jnp.bfloat16)
    for side in range(2):

        @pl.when(pl.program_id(0) // 2 == side)
        def _():
            for c in range(norb // rows):
                outs[side][c, 0, 0] = total[c * rows : (c + 1) * rows]


def packed_lesser(place, green, gamma, chunks):
    energies, norb = green.shape[1], green.shape[-1]
    half = green.shape[0] // 2
    rows = norb // chunks

    def which(k, p):
        return ((p[0] + 1 + k // half) % 2) * half + k % half

    def block_of(side):
        def index(k, e, p):
            if side == 0:
                return (0, jnp.minimum(k, half - 1), jnp.where(k < half, e, energies - 1), 0, 0)
            return (0, jnp.maximum(k - half, 0), jnp.where(k < half, 0, e), 0, 0)

        return pl.BlockSpec((chunks, 1, 1, rows, norb), index)

    out = jax.ShapeDtypeStruct((chunks, half, energies, rows, norb), jnp.bfloat16)
    outs = pl.pallas_call(
        lesser_kernel,
        grid_spec=pltpu.PrefetchScalarGridSpec(
            num_scalar_prefetch=1,
            grid=(2 * half, energies),
            in_specs=[
                pl.BlockSpec((1, 1, 2, norb, norb), lambda k, e, p: (which(k, p), e, 0, 0, 0)),
                pl.BlockSpec(gamma.shape, lambda k, e, p: (0, 0, 0)),
            ],
            out_specs=[block_of(0), block_of(1)],
        ),
        out_shape=[out] * 2,
        compiler_params=pltpu.CompilerParams(vmem_limit_bytes=60 * MIB),
        cost_estimate=pl.CostEstimate(
            flops=8 * half * energies * norb**3,
            bytes_accessed=12 * half * energies * norb**2,
            transcendentals=0,
        ),
        name="lesser",
    )(place, green, gamma)
    return outs


def identity(n):
    rows = lax.broadcasted_iota(jnp.int32, (n, n), 0)
    cols = lax.broadcasted_iota(jnp.int32, (n, n), 1)
    return (rows == cols).astype(jnp.float32).astype(jnp.bfloat16)


def exchange_kernel(
    shift_steps, mode_weight, occupation, table, sent, own, coupling, src, us, vs,
    got, own_halo, got_halo, mine, other, tiles, turned, held, sums, sums_t, send, recv, local,
):
    energy, mom = lax.axis_index("energy"), lax.axis_index("mom")
    pairs = lax.axis_size("energy") // 2
    x_lo, pair = energy % 2, energy // 2
    chunks, half, _, rows, norb = sent.shape
    points, height, _ = coupling.shape
    energy_a = energy + 1 - 2 * x_lo
    mom_core = mom + 1 - 2 * (mom % 2)
    mom_hi = mom + 2 - 4 * (mom // 2)
    mom_both = 3 - mom
    place = [mom, mom_core, mom_hi, mom_both]
    ring_a, ring_b, ring_ab = (energy_a, mom), (energy_a, mom_hi), (energy, mom_hi)
    core = (energy, mom_core)
    own_to = (energy - 2 + 4 * x_lo, mom)
    got_to = (energy + 2 - 4 * x_lo, mom)
    low, high = pair > 0, pair < pairs - 1
    first = x_lo == 0
    has_own_to = jnp.logical_or(
        jnp.logical_and(first, low), jnp.logical_and(jnp.logical_not(first), high)
    )
    has_got_to = jnp.logical_or(
        jnp.logical_and(first, high), jnp.logical_and(jnp.logical_not(first), low)
    )

    weights = [0.0] * 4
    for m in range(shift_steps.shape[0]):
        two = shift_steps[m].astype(jnp.float32) - 1.0
        up = 0.5 * mode_weight[m] * (occupation[m] + 1.0)
        down = 0.5 * mode_weight[m] * occupation[m]
        weights[0] += (1.0 - two) * up
        weights[1] += two * up
        weights[2] += (1.0 - two) * down
        weights[3] += two * down

    def remote(kind, c, source, target, device):
        return pltpu.make_async_remote_copy(
            src_ref=source,
            dst_ref=target,
            send_sem=send.at[kind, c],
            recv_sem=recv.at[kind, c],
            device_id=device,
            device_id_type=pl.DeviceIdType.MESH,
        )

    swap = [remote(0, c, sent.at[c], got.at[c], ring_a) for c in range(chunks)]
    to_own = [remote(1, c, own.at[c], own_halo.at[c], own_to) for c in range(chunks)]
    to_got = [remote(2, c, got.at[c], got_halo.at[c], got_to) for c in range(chunks)]
    near = [
        [
            remote(3, c, other.at[c], src.at[c, 1], ring_a),
            remote(4, c, other.at[c], src.at[c, 2], ring_b),
            remote(5, c, mine.at[c], src.at[c, 3], ring_ab),
        ]
        for c in range(chunks)
    ]
    far = [
        [remote(6, c, mine.at[c], src.at[c, 4], core)]
        + [remote(6 + s, c, src.at[c, s], src.at[c, 4 + s], core) for s in (1, 2, 3)]
        for c in range(chunks)
    ]
    stay = [pltpu.make_async_copy(mine.at[c], src.at[c, 0], local.at[c]) for c in range(chunks)]
    tile_core = remote(10, 0, coupling, tiles.at[1], core)
    tile_b = remote(10, 1, coupling, tiles.at[2], ring_b)
    tile_bc = remote(10, 2, tiles.at[2], tiles.at[3], core)
    tile_own = pltpu.make_async_copy(coupling, tiles.at[0], local.at[chunks])
    taken = [
        pltpu.make_async_copy(src.at[c], held.at[c % 2], local.at[chunks + 1 + c])
        for c in range(chunks)
    ]
    summed = [
        (
            pltpu.make_async_copy(
                sums.at[c], us.at[:, :, c * rows : (c + 1) * rows, :], local.at[2 * chunks + 1 + c]
            ),
            pltpu.make_async_copy(
                sums_t.at[c], vs.at[:, :, c * rows : (c + 1) * rows, :], local.at[3 * chunks + 1 + c]
            ),
        )
        for c in range(chunks)
    ]
    targets = us.shape[0]
    home = mom * targets

    def picks(t, d):
        return table[home + t, d]

    def convolve(c):
        low_bit = (mom + c) % 2
        slot = low_bit + 2 * ((mom // 2 + c // 2) % 2)

        def donor(d, n, at):
            return held[c % 2, d // 2, d % 2, n, at[0], at[1]]

        def store(t, n, at, value):
            sums[c, t, n, at[0], at[1]] = value.astype(sums.dtype)

        def store_t(t, n, at, value):
            sums_t[c, t, n, at[0], at[1]] = value.astype(sums.dtype)

        def straight(i, carry):
            at = (
                pl.ds(pl.multiple_of(i // 2 * 16, 16), 16),
                pl.ds(pl.multiple_of(i % 2 * (norb // 2), norb // 2), norb // 2),
            )
            add_products(targets, 2, picks, donor, tiles.at[slot], at, store)
            return carry

        lax.fori_loop(0, rows // 16 * 2, straight, 0)
        for s in range(4):

            def across(i, carry, s=s):
                span = pl.ds(pl.multiple_of(place[s] * height, height), height)
                at = (pl.ds(pl.multiple_of(i * 32, 32), 32), span)
                inner = (pl.ds(pl.multiple_of(c * rows + i * 32, 32), 32), slice(None))
                add_products(targets, 2, picks, donor, turned.at[s], at, store_t, inner)
                return carry

            lax.fori_loop(0, rows // 32, across, 0)
        for copy in summed[c]:
            copy.start()

    barrier = pltpu.get_barrier_semaphore()

    def greet(device):
        pl.semaphore_signal(
            barrier, inc=1, device_id=device, device_id_type=pl.DeviceIdType.MESH
        )

    for device in (ring_a, ring_b, ring_ab, core):
        greet(device)

    @pl.when(has_own_to)
    def _():
        greet(own_to)

    @pl.when(has_got_to)
    def _():
        greet(got_to)

    pl.semaphore_wait(barrier, 4 + jnp.where(low, 1, 0) + jnp.where(high, 1, 0))

    swap[0].start()
    swap[1].start()

    @pl.when(has_own_to)
    def _():
        for c in range(chunks):
            to_own[c].start()

    tile_b.start()
    tile_core.start()
    tile_own.start()

    step = 16
    slabs = rows // step

    def clear(halo):
        def one(i, carry):
            c, r = i // slabs, i % slabs
            at = pl.ds(pl.multiple_of(r * step, step), step)
            for k in range(half):
                for e in range(2):
                    halo[c, k, e, at, :] = jnp.zeros((step, norb), halo.dtype)
            return carry

        lax.fori_loop(0, chunks * slabs, one, 0)

    @pl.when(jnp.logical_not(has_got_to))
    def _():
        clear(own_halo)

    @pl.when(jnp.logical_not(has_own_to))
    def _():
        clear(got_halo)

    turn = identity(norb // 2)

    def fold(s):
        def one(q, carry):
            for b in range(2):
                span = slice(b * (norb // 2), (b + 1) * (norb // 2))
                turned[s, q, span, :] = dot_nt(turn, tiles[s, q, :, span]).astype(turned.dtype)
            return carry

        lax.fori_loop(0, points, one, 0)

    def shift(c, parts, outs):
        def one(i, carry):
            k, r = i // slabs, i % slabs
            at = pl.ds(pl.multiple_of(r * step, step), step)
            levels = [ref[c, k, e, at, :].astype(jnp.float32) for ref in parts for e in range(2)]
            for o in range(4):
                total = weights[0] * levels[o + 3] + weights[1] * levels[o + 4]
                total = total + weights[2] * levels[o + 1] + weights[3] * levels[o]
                outs[o // 2][c, k, o % 2, at, :] = total.astype(mine.dtype)
            return carry

        lax.fori_loop(0, half * slabs, one, 0)

    for c in range(chunks + 1):
        if c < chunks:
            swap[c].wait_recv()

            @pl.when(has_got_to)
            def _(copy=to_got[c]):
                copy.start()

            if c + 2 < chunks:
                swap[c + 2].start()
        if c == 0:
            tile_own.wait()
            fold(0)
        else:
            d = c - 1

            @pl.when(has_got_to)
            def _(copy=to_own[d]):
                copy.wait_recv()

            @pl.when(has_own_to)
            def _(copy=to_got[d]):
                copy.wait_recv()

            @pl.when(first)
            def _(d=d):
                shift(d, (got_halo, own, got, own_halo), (mine, other))

            @pl.when(jnp.logical_not(first))
            def _(d=d):
                shift(d, (own_halo, got, own, got_halo), (other, mine))

            for copy in near[d]:
                copy.start()
            far[d][0].start()
            stay[d].start()
        if c == 1:
            tile_core.wait_recv()
            fold(1)

    tile_b.wait_recv()
    tile_bc.start()
    fold(2)
    def take(c):
        for copy in far[c]:
            copy.wait_recv()
        stay[c].wait()
        taken[c].start()

    for c in range(chunks):
        for s in (1, 2, 3):
            near[c][s - 1].wait_recv()
            far[c][s].start()
        if c == 0:
            tile_bc.wait_recv()
            fold(3)
        else:
            take(c - 1)
            taken[c - 1].wait()
            convolve(c - 1)
    take(chunks - 1)
    taken[chunks - 1].wait()
    convolve(chunks - 1)
    for c in range(chunks):
        for copy in [swap[c]] + near[c] + far[c]:
            copy.wait_send()

        @pl.when(has_own_to)
        def _(copy=to_own[c]):
            copy.wait_send()

        @pl.when(has_got_to)
        def _(copy=to_got[c]):
            copy.wait_send()

    for copy in (tile_core, tile_b, tile_bc):
        copy.wait_send()
    for two in summed:
        for copy in two:
            copy.wait()


def exchanged(shift_steps, mode_weight, occupation, table, sent, own, coupling, targets):
    chunks, half, energies, rows, norb = sent.shape
    points, height, _ = coupling.shape
    whole = jax.ShapeDtypeStruct((targets, energies, norb, norb), jnp.bfloat16)
    result = pltpu.VMEM((chunks, targets, energies, rows, norb), jnp.bfloat16)
    vmem = pl.BlockSpec(memory_space=pltpu.VMEM)
    hbm = pl.BlockSpec(memory_space=pl.ANY)
    part = pltpu.VMEM(sent.shape, jnp.bfloat16)
    return pl.pallas_call(
        exchange_kernel,
        in_specs=[pl.BlockSpec(memory_space=pltpu.SMEM)] * 4 + [vmem, vmem, hbm],
        out_specs=[hbm] * 3,
        out_shape=[
            jax.ShapeDtypeStruct((chunks, 8, half, energies, rows, norb), jnp.bfloat16),
            whole,
            whole,
        ],
        scratch_shapes=[part] * 5
        + [
            pltpu.VMEM((4, points, height, norb), jnp.bfloat16),
            pltpu.VMEM((4, points, norb, height), jnp.bfloat16),
            pltpu.VMEM((2, 8, half, energies, rows, norb), jnp.bfloat16),
            result,
            result,
            pltpu.SemaphoreType.DMA((11, chunks)),
            pltpu.SemaphoreType.DMA((11, chunks)),
            pltpu.SemaphoreType.DMA((4 * chunks + 1,)),
        ],
        compiler_params=pltpu.CompilerParams(
            collective_id=0, has_side_effects=True, vmem_limit_bytes=60 * MIB
        ),
        name="exchange",
    )(shift_steps, mode_weight, occupation, table, sent, own, coupling)


def add_products(targets, streams, picks, donor, factor, at, store, inner=None):
    inner = at if inner is None else inner
    acc = [[None] * streams for _ in range(targets)]
    kept = {}
    for quad in range(4):
        held = [[donor(4 * quad + d, n, at) for n in range(streams)] for d in range(4)]
        for t in range(targets):
            c = [factor[picks(t, 4 * quad + d), inner[0], inner[1]] for d in range(4)]
            for n in range(streams):
                part = (c[0] * held[0][n] + c[1] * held[1][n]) + (
                    c[2] * held[2][n] + c[3] * held[3][n]
                )
                if quad % 2 == 0:
                    kept[t, n] = part
                    continue
                part = (kept.pop((t, n)) + part).astype(jnp.float32)
                acc[t][n] = part if acc[t][n] is None else acc[t][n] + part
    for t in range(targets):
        for n in range(streams):
            store(t, n, at, acc[t][n])


def finish_kernel(
    inverse, table, green, gamma, us, vs, rows_of, cols_of, coup, out, density,
    source, part, came, send, recv,
):
    energy, mom = lax.axis_index("energy"), lax.axis_index("mom")
    owners = lax.axis_size("energy")
    count = part.shape[0]
    targets, _, _, height, norb = out.shape
    index = pl.program_id(0)

    @pl.when(index == 0)
    def _():
        barrier = pltpu.get_barrier_semaphore()

        def greet(n, carry):
            pl.semaphore_signal(
                barrier,
                inc=1,
                device_id=((energy + n) % owners, mom),
                device_id_type=pl.DeviceIdType.MESH,
            )
            return carry

        lax.fori_loop(1, owners, greet, 0)
        pl.semaphore_wait(barrier, owners - 1)

    @pl.when(index < count)
    def _():
        d_re = d_im = None
        for e in range(green.shape[1]):
            g_re, g_im = green[0, e, 0], green[0, e, 1]
            gam = gamma[index, e : e + 1, :]
            wide_re, wide_im = g_re.astype(jnp.float32), g_im.astype(jnp.float32)
            less = (wide_re - wide_im).astype(jnp.bfloat16)
            more = (wide_re + wide_im).astype(jnp.bfloat16)
            u, v = us[0, e], vs[0, e]
            m_re = dot_nn(less, u) + dot_nt(more, v) + scale(g_re, gam).astype(jnp.float32)
            m_im = dot_nn(more, u) - dot_nt(less, v) + scale(g_im, gam).astype(jnp.float32)
            m_re, m_im = m_re.astype(jnp.bfloat16), m_im.astype(jnp.bfloat16)
            one = dot_nt(m_re, g_re) + dot_nt(m_im, g_im)
            two = dot_nt(m_im, g_re) - dot_nt(m_re, g_im)
            d_re = one if d_re is None else d_re + one
            d_im = two if d_im is None else d_im + two
        shape = (owners, norb // owners, norb)
        part[index, :, 0] = (d_re * inverse).astype(jnp.bfloat16).reshape(shape)
        part[index, :, 1] = (d_im * inverse).astype(jnp.bfloat16).reshape(shape)
        came[index, energy] = part[index, energy]

        def post(n, carry):
            peer = (energy + n * 13) % owners
            pltpu.make_async_remote_copy(
                src_ref=part.at[index, peer],
                dst_ref=came.at[index, energy],
                send_sem=send.at[index],
                recv_sem=recv.at[index],
                device_id=(peer, mom),
                device_id_type=pl.DeviceIdType.MESH,
            ).start()
            return carry

        lax.fori_loop(1, owners, post, 0)

    place = index - count
    group = place % 4 * targets

    @pl.when(jnp.logical_and(index >= count, place % 4 == 0))
    def _():
        turn = identity(height)
        for d in range(16):
            for b in range(norb // height):
                span = slice(b * height, (b + 1) * height)
                straight = rows_of[0, d // 2, d % 2, 0, :, span].astype(jnp.float32)
                turned = dot_nt(turn, cols_of[b, d // 2, d % 2, 0])
                source[d, 0, :, span] = (straight + turned).astype(jnp.bfloat16)
                source[d, 1, :, span] = (straight - turned).astype(jnp.bfloat16)

    def picks(t, d):
        return table[group + t, d]

    def donor(d, n, at):
        return source[d, n, at[0], at[1]]

    def store(t, n, at, value):
        out[t, 0, n, at[0], at[1]] = value.astype(jnp.bfloat16)

    @pl.when(index >= count)
    def _():
        def slab(i, carry):
            at = (
                pl.ds(pl.multiple_of(i // 2 * 16, 16), 16),
                pl.ds(pl.multiple_of(i % 2 * (norb // 2), norb // 2), norb // 2),
            )
            add_products(targets, 2, picks, donor, coup, at, store)
            return carry

        lax.fori_loop(0, height // 16 * 2, slab, 0)

    @pl.when(index == pl.num_programs(0) - 1)
    def _():
        for k in range(count):
            every = pltpu.make_async_remote_copy(
                src_ref=part.at[k, pl.ds(0, owners - 1)],
                dst_ref=came.at[k, pl.ds(0, owners - 1)],
                send_sem=send.at[k],
                recv_sem=recv.at[k],
                device_id=((energy + 1) % owners, mom),
                device_id_type=pl.DeviceIdType.MESH,
            )
            every.wait_recv()
            every.wait_send()

            def add(n, total):
                return total + came[k, n].astype(jnp.float32)

            total = lax.fori_loop(1, owners, add, came[k, 0].astype(jnp.float32))
            for c in range(2):
                density[:, k, c, :] = total[c]


def finished(table, green, gamma, us, vs, src, coupling, owners, targets):
    chunks, _, half, energies, rows, norb = src.shape
    points, height, _ = coupling.shape
    count = green.shape[0]
    own_rows = norb // owners
    groups = points // targets

    def of_k(i):
        return jnp.minimum(i, count - 1)

    def of_e(i):
        return jnp.maximum(i - count, 0) // groups

    def of_g(i):
        return jnp.maximum(i - count, 0) % groups

    part = pl.BlockSpec((1, energies, norb, norb), lambda i: (of_k(i), 0, 0, 0))
    return pl.pallas_call(
        functools.partial(finish_kernel, 1.0 / (energies * owners)),
        grid=(count + energies * groups,),
        in_specs=[
            pl.BlockSpec(memory_space=pltpu.SMEM),
            pl.BlockSpec((1, energies, 2, norb, norb), lambda i: (of_k(i), 0, 0, 0, 0)),
            pl.BlockSpec(gamma.shape, lambda i: (0, 0, 0)),
            part,
            part,
            pl.BlockSpec(
                (1, 8, half, 1, rows, norb),
                lambda i: (lax.axis_index("mom"), 0, 0, of_e(i), 0, 0),
            ),
            pl.BlockSpec(
                (chunks, 8, half, 1, rows, height),
                lambda i: (0, 0, 0, of_e(i), 0, lax.axis_index("mom")),
            ),
            pl.BlockSpec((points, height, norb), lambda i: (0, 0, 0)),
        ],
        out_specs=[
            pl.BlockSpec((targets, 1, 2, height, norb), lambda i: (of_g(i), of_e(i), 0, 0, 0)),
            pl.BlockSpec((own_rows, count, 2, norb), lambda i: (0, 0, 0, 0)),
        ],
        out_shape=[
            jax.ShapeDtypeStruct((points, energies, 2, height, norb), jnp.bfloat16),
            jax.ShapeDtypeStruct((own_rows, count, 2, norb), jnp.float32),
        ],
        scratch_shapes=[
            pltpu.VMEM((16, 2, height, norb), jnp.bfloat16),
            pltpu.VMEM((count, owners, 2, own_rows, norb), jnp.bfloat16),
            pltpu.VMEM((count, owners, 2, own_rows, norb), jnp.bfloat16),
            pltpu.SemaphoreType.DMA((count,)),
            pltpu.SemaphoreType.DMA((count,)),
        ],
        compiler_params=pltpu.CompilerParams(
            collective_id=1, has_side_effects=True, vmem_limit_bytes=60 * MIB
        ),
        name="finish",
    )(table, green, gamma, us, vs, src, src, coupling)


def on_device(green, broadening, coupling, shift_steps, mode_weight, occupation, momentum_map):
    n_energy, n_mom = lax.axis_size("energy"), lax.axis_size("mom")
    local_k = green.shape[0]
    half = local_k // 2
    points = momentum_map.shape[1]
    energy, mom = lax.axis_index("energy"), lax.axis_index("mom")
    x_lo = energy % 2

    sent, own = packed_lesser(x_lo.astype(jnp.int32)[None], green, broadening, n_mom)
    moves = [(0, 0), (1, 0), (1, 2), (0, 2)]
    moves = moves + [(lo, mo ^ 1) for lo, mo in moves]
    donors = jnp.stack(
        [(mom ^ mo) * local_k + (x_lo ^ lo) * half + kk for lo, mo in moves for kk in range(half)]
    ).astype(jnp.int32)
    table = jnp.sum(
        jnp.where(
            momentum_map[:, :, None] == donors[None, None, :],
            jnp.arange(points, dtype=jnp.int32)[None, :, None],
            0,
        ),
        axis=1,
    ).astype(jnp.int32)
    src, us, vs = exchanged(
        shift_steps, mode_weight, occupation, table, sent, own, coupling, local_k
    )
    return tuple(
        finished(table, green, broadening, us, vs, src, coupling, n_energy, local_k)
    )


def solution(mesh):
    return jax.shard_map(
        on_device,
        mesh=mesh,
        in_specs=(
            P("mom", "energy", None, None, None),
            P("mom", "energy", None),
            P(None, "mom", None),
            P(),
            P(),
            P(),
            P(),
        ),
        out_specs=(P(None, "energy", None, "mom", None), P("energy", "mom", None, None)),
        check_vma=False,
    )
```

```python
import functools

import jax
import jax.numpy as jnp
from jax import lax
from jax.experimental import pallas as pl
from jax.experimental.pallas import tpu as pltpu
from jax.sharding import PartitionSpec as P

MIB = 1 << 20
NT = (((1,), (1,)), ((), ()))


def dot_nt(left, right):
    return lax.dot_general(left, right, NT, preferred_element_type=jnp.float32)


def dot_nn(left, right):
    return jnp.dot(left, right, preferred_element_type=jnp.float32)


def scale(block, gamma):
    return (block.astype(jnp.float32) * gamma).astype(jnp.bfloat16)


def lesser_kernel(place, green, gamma, *outs):
    norb = green.shape[-1]
    rows = outs[0].shape[3]
    half = gamma.shape[0] // 2
    step = pl.program_id(0)
    gam = gamma[(place[0] + 1 + step // half) % 2 * half + step % half, pl.ds(pl.program_id(1), 1), :]
    g_re, g_im = green[0, 0, 0], green[0, 0, 1]
    wide_re = g_re.astype(jnp.float32)
    wide_im = g_im.astype(jnp.float32)
    less = (wide_re - wide_im).astype(jnp.bfloat16)
    more = (wide_re + wide_im).astype(jnp.bfloat16)
    total = dot_nt(scale(g_re, gam), less) + dot_nt(scale(g_im, gam), more)
    total = total.astype(jnp.bfloat16)
    for side in range(2):

        @pl.when(pl.program_id(0) // 2 == side)
        def _():
            for c in range(norb // rows):
                outs[side][c, 0, 0] = total[c * rows : (c + 1) * rows]


def packed_lesser(place, green, gamma, chunks):
    energies, norb = green.shape[1], green.shape[-1]
    half = green.shape[0] // 2
    rows = norb // chunks

    def which(k, p):
        return ((p[0] + 1 + k // half) % 2) * half + k % half

    def block_of(side):
        def index(k, e, p):
            if side == 0:
                return (0, jnp.minimum(k, half - 1), jnp.where(k < half, e, energies - 1), 0, 0)
            return (0, jnp.maximum(k - half, 0), jnp.where(k < half, 0, e), 0, 0)

        return pl.BlockSpec((chunks, 1, 1, rows, norb), index)

    out = jax.ShapeDtypeStruct((chunks, half, energies, rows, norb), jnp.bfloat16)
    outs = pl.pallas_call(
        lesser_kernel,
        grid_spec=pltpu.PrefetchScalarGridSpec(
            num_scalar_prefetch=1,
            grid=(2 * half, energies),
            in_specs=[
                pl.BlockSpec((1, 1, 2, norb, norb), lambda k, e, p: (which(k, p), e, 0, 0, 0)),
                pl.BlockSpec(gamma.shape, lambda k, e, p: (0, 0, 0)),
            ],
            out_specs=[block_of(0), block_of(1)],
        ),
        out_shape=[out] * 2,
        compiler_params=pltpu.CompilerParams(vmem_limit_bytes=60 * MIB),
        cost_estimate=pl.CostEstimate(
            flops=8 * half * energies * norb**3,
            bytes_accessed=12 * half * energies * norb**2,
            transcendentals=0,
        ),
        name="lesser",
    )(place, green, gamma)
    return outs


def identity(n):
    rows = lax.broadcasted_iota(jnp.int32, (n, n), 0)
    cols = lax.broadcasted_iota(jnp.int32, (n, n), 1)
    return (rows == cols).astype(jnp.float32).astype(jnp.bfloat16)


def exchange_kernel(
    shift_steps, mode_weight, occupation, table, sent, own, coupling, src, us, vs,
    got, own_halo, got_halo, mine, other, tiles, turned, held, sums, sums_t, send, recv, local,
):
    energy, mom = lax.axis_index("energy"), lax.axis_index("mom")
    pairs = lax.axis_size("energy") // 2
    x_lo, pair = energy % 2, energy // 2
    chunks, half, _, rows, norb = sent.shape
    points, height, _ = coupling.shape
    energy_a = energy + 1 - 2 * x_lo
    mom_core = mom + 1 - 2 * (mom % 2)
    mom_hi = mom + 2 - 4 * (mom // 2)
    mom_both = 3 - mom
    place = [mom, mom_core, mom_hi, mom_both]
    ring_a, ring_b, ring_ab = (energy_a, mom), (energy_a, mom_hi), (energy, mom_hi)
    core = (energy, mom_core)
    own_to = (energy - 2 + 4 * x_lo, mom)
    got_to = (energy + 2 - 4 * x_lo, mom)
    low, high = pair > 0, pair < pairs - 1
    first = x_lo == 0
    has_own_to = jnp.logical_or(
        jnp.logical_and(first, low), jnp.logical_and(jnp.logical_not(first), high)
    )
    has_got_to = jnp.logical_or(
        jnp.logical_and(first, high), jnp.logical_and(jnp.logical_not(first), low)
    )

    weights = [0.0] * 4
    for m in range(shift_steps.shape[0]):
        two = shift_steps[m].astype(jnp.float32) - 1.0
        up = 0.5 * mode_weight[m] * (occupation[m] + 1.0)
        down = 0.5 * mode_weight[m] * occupation[m]
        weights[0] += (1.0 - two) * up
        weights[1] += two * up
        weights[2] += (1.0 - two) * down
        weights[3] += two * down

    def remote(kind, c, source, target, device):
        return pltpu.make_async_remote_copy(
            src_ref=source,
            dst_ref=target,
            send_sem=send.at[kind, c],
            recv_sem=recv.at[kind, c],
            device_id=device,
            device_id_type=pl.DeviceIdType.MESH,
        )

    swap = [remote(0, c, sent.at[c], got.at[c], ring_a) for c in range(chunks)]
    to_own = [remote(1, c, own.at[c], own_halo.at[c], own_to) for c in range(chunks)]
    to_got = [remote(2, c, got.at[c], got_halo.at[c], got_to) for c in range(chunks)]
    near = [
        [
            remote(3, c, other.at[c], src.at[c, 1], ring_a),
            remote(4, c, other.at[c], src.at[c, 2], ring_b),
            remote(5, c, mine.at[c], src.at[c, 3], ring_ab),
        ]
        for c in range(chunks)
    ]
    far = [
        [remote(6, c, mine.at[c], src.at[c, 4], core)]
        + [remote(6 + s, c, src.at[c, s], src.at[c, 4 + s], core) for s in (1, 2, 3)]
        for c in range(chunks)
    ]
    stay = [pltpu.make_async_copy(mine.at[c], src.at[c, 0], local.at[c]) for c in range(chunks)]
    tile_core = remote(10, 0, coupling, tiles.at[1], core)
    tile_b = remote(10, 1, coupling, tiles.at[2], ring_b)
    tile_bc = remote(10, 2, tiles.at[2], tiles.at[3], core)
    tile_own = pltpu.make_async_copy(coupling, tiles.at[0], local.at[chunks])
    taken = [
        pltpu.make_async_copy(src.at[c], held.at[c % 2], local.at[chunks + 1 + c])
        for c in range(chunks)
    ]
    summed = [
        (
            pltpu.make_async_copy(
                sums.at[c], us.at[:, :, c * rows : (c + 1) * rows, :], local.at[2 * chunks + 1 + c]
            ),
            pltpu.make_async_copy(
                sums_t.at[c], vs.at[:, :, c * rows : (c + 1) * rows, :], local.at[3 * chunks + 1 + c]
            ),
        )
        for c in range(chunks)
    ]
    targets = us.shape[0]
    home = mom * targets

    def picks(t, d):
        return table[home + t, d]

    def convolve(c):
        low_bit = (mom + c) % 2
        slot = low_bit + 2 * ((mom // 2 + c // 2) % 2)

        def donor(d, n, at):
            return held[c % 2, d // 2, d % 2, n, at[0], at[1]]

        def store(t, n, at, value):
            sums[c, t, n, at[0], at[1]] = value.astype(sums.dtype)

        def store_t(t, n, at, value):
            sums_t[c, t, n, at[0], at[1]] = value.astype(sums.dtype)

        def straight(i, carry):
            at = (
                pl.ds(pl.multiple_of(i // 2 * 16, 16), 16),
                pl.ds(pl.multiple_of(i % 2 * (norb // 2), norb // 2), norb // 2),
            )
            add_products(targets, 2, picks, donor, tiles.at[slot], at, store)
            return carry

        lax.fori_loop(0, rows // 16 * 2, straight, 0)
        for s in range(4):

            def across(i, carry, s=s):
                span = pl.ds(pl.multiple_of(place[s] * height, height), height)
                at = (pl.ds(pl.multiple_of(i * 32, 32), 32), span)
                inner = (pl.ds(pl.multiple_of(c * rows + i * 32, 32), 32), slice(None))
                add_products(targets, 2, picks, donor, turned.at[s], at, store_t, inner)
                return carry

            lax.fori_loop(0, rows // 32, across, 0)
        for copy in summed[c]:
            copy.start()

    barrier = pltpu.get_barrier_semaphore()

    def greet(device):
        pl.semaphore_signal(
            barrier, inc=1, device_id=device, device_id_type=pl.DeviceIdType.MESH
        )

    for device in (ring_a, ring_b, ring_ab, core):
        greet(device)

    @pl.when(has_own_to)
    def _():
        greet(own_to)

    @pl.when(has_got_to)
    def _():
        greet(got_to)

    pl.semaphore_wait(barrier, 4 + jnp.where(low, 1, 0) + jnp.where(high, 1, 0))

    swap[0].start()
    swap[1].start()

    @pl.when(has_own_to)
    def _():
        for c in range(chunks):
            to_own[c].start()

    tile_b.start()
    tile_core.start()
    tile_own.start()

    step = 16
    slabs = rows // step

    def clear(halo):
        def one(i, carry):
            c, r = i // slabs, i % slabs
            at = pl.ds(pl.multiple_of(r * step, step), step)
            for k in range(half):
                for e in range(2):
                    halo[c, k, e, at, :] = jnp.zeros((step, norb), halo.dtype)
            return carry

        lax.fori_loop(0, chunks * slabs, one, 0)

    @pl.when(jnp.logical_not(has_got_to))
    def _():
        clear(own_halo)

    @pl.when(jnp.logical_not(has_own_to))
    def _():
        clear(got_halo)

    turn = identity(norb // 2)

    def fold(s):
        def one(q, carry):
            for b in range(2):
                span = slice(b * (norb // 2), (b + 1) * (norb // 2))
                turned[s, q, span, :] = dot_nt(turn, tiles[s, q, :, span]).astype(turned.dtype)
            return carry

        lax.fori_loop(0, points, one, 0)

    def shift(c, parts, outs):
        def one(i, carry):
            k, r = i // slabs, i % slabs
            at = pl.ds(pl.multiple_of(r * step, step), step)
            levels = [ref[c, k, e, at, :].astype(jnp.float32) for ref in parts for e in range(2)]
            for o in range(4):
                total = weights[0] * levels[o + 3] + weights[1] * levels[o + 4]
                total = total + weights[2] * levels[o + 1] + weights[3] * levels[o]
                outs[o // 2][c, k, o % 2, at, :] = total.astype(mine.dtype)
            return carry

        lax.fori_loop(0, half * slabs, one, 0)

    for c in range(chunks + 1):
        if c < chunks:
            swap[c].wait_recv()

            @pl.when(has_got_to)
            def _(copy=to_got[c]):
                copy.start()

            if c + 2 < chunks:
                swap[c + 2].start()
        if c == 0:
            tile_own.wait()
            fold(0)
        else:
            d = c - 1

            @pl.when(has_got_to)
            def _(copy=to_own[d]):
                copy.wait_recv()

            @pl.when(has_own_to)
            def _(copy=to_got[d]):
                copy.wait_recv()

            @pl.when(first)
            def _(d=d):
                shift(d, (got_halo, own, got, own_halo), (mine, other))

            @pl.when(jnp.logical_not(first))
            def _(d=d):
                shift(d, (own_halo, got, own, got_halo), (other, mine))

            for copy in near[d]:
                copy.start()
            far[d][0].start()
            stay[d].start()
        if c == 1:
            tile_core.wait_recv()
            fold(1)

    tile_b.wait_recv()
    tile_bc.start()
    fold(2)
    def take(c):
        for copy in far[c]:
            copy.wait_recv()
        stay[c].wait()
        taken[c].start()

    for c in range(chunks):
        if c > 0:
            take(c - 1)
            taken[c - 1].wait()
            convolve(c - 1)
        for s in (1, 2, 3):
            near[c][s - 1].wait_recv()
            far[c][s].start()
        if c == 0:
            tile_bc.wait_recv()
            fold(3)
    take(chunks - 1)
    taken[chunks - 1].wait()
    convolve(chunks - 1)
    for c in range(chunks):
        for copy in [swap[c]] + near[c] + far[c]:
            copy.wait_send()

        @pl.when(has_own_to)
        def _(copy=to_own[c]):
            copy.wait_send()

        @pl.when(has_got_to)
        def _(copy=to_got[c]):
            copy.wait_send()

    for copy in (tile_core, tile_b, tile_bc):
        copy.wait_send()
    for two in summed:
        for copy in two:
            copy.wait()


def exchanged(shift_steps, mode_weight, occupation, table, sent, own, coupling, targets):
    chunks, half, energies, rows, norb = sent.shape
    points, height, _ = coupling.shape
    whole = jax.ShapeDtypeStruct((targets, energies, norb, norb), jnp.bfloat16)
    result = pltpu.VMEM((chunks, targets, energies, rows, norb), jnp.bfloat16)
    vmem = pl.BlockSpec(memory_space=pltpu.VMEM)
    hbm = pl.BlockSpec(memory_space=pl.ANY)
    part = pltpu.VMEM(sent.shape, jnp.bfloat16)
    return pl.pallas_call(
        exchange_kernel,
        in_specs=[pl.BlockSpec(memory_space=pltpu.SMEM)] * 4 + [vmem, vmem, hbm],
        out_specs=[hbm] * 3,
        out_shape=[
            jax.ShapeDtypeStruct((chunks, 8, half, energies, rows, norb), jnp.bfloat16),
            whole,
            whole,
        ],
        scratch_shapes=[part] * 5
        + [
            pltpu.VMEM((4, points, height, norb), jnp.bfloat16),
            pltpu.VMEM((4, points, norb, height), jnp.bfloat16),
            pltpu.VMEM((2, 8, half, energies, rows, norb), jnp.bfloat16),
            result,
            result,
            pltpu.SemaphoreType.DMA((11, chunks)),
            pltpu.SemaphoreType.DMA((11, chunks)),
            pltpu.SemaphoreType.DMA((4 * chunks + 1,)),
        ],
        compiler_params=pltpu.CompilerParams(
            collective_id=0, has_side_effects=True, vmem_limit_bytes=60 * MIB
        ),
        name="exchange",
    )(shift_steps, mode_weight, occupation, table, sent, own, coupling)


def add_products(targets, streams, picks, donor, factor, at, store, inner=None):
    inner = at if inner is None else inner
    acc = [[None] * streams for _ in range(targets)]
    kept = {}
    for quad in range(4):
        held = [[donor(4 * quad + d, n, at) for n in range(streams)] for d in range(4)]
        for t in range(targets):
            c = [factor[picks(t, 4 * quad + d), inner[0], inner[1]] for d in range(4)]
            for n in range(streams):
                part = (c[0] * held[0][n] + c[1] * held[1][n]) + (
                    c[2] * held[2][n] + c[3] * held[3][n]
                )
                if quad % 2 == 0:
                    kept[t, n] = part
                    continue
                part = (kept.pop((t, n)) + part).astype(jnp.float32)
                acc[t][n] = part if acc[t][n] is None else acc[t][n] + part
    for t in range(targets):
        for n in range(streams):
            store(t, n, at, acc[t][n])


def finish_kernel(
    inverse, table, green, gamma, us, vs, rows_of, cols_of, coup, out, density,
    source, part, came, send, recv,
):
    energy, mom = lax.axis_index("energy"), lax.axis_index("mom")
    owners = lax.axis_size("energy")
    count = part.shape[0]
    targets, _, _, height, norb = out.shape
    index = pl.program_id(0)

    @pl.when(index == 0)
    def _():
        barrier = pltpu.get_barrier_semaphore()

        def greet(n, carry):
            pl.semaphore_signal(
                barrier,
                inc=1,
                device_id=((energy + n) % owners, mom),
                device_id_type=pl.DeviceIdType.MESH,
            )
            return carry

        lax.fori_loop(1, owners, greet, 0)
        pl.semaphore_wait(barrier, owners - 1)

    @pl.when(index < count)
    def _():
        d_re = d_im = None
        for e in range(green.shape[1]):
            g_re, g_im = green[0, e, 0], green[0, e, 1]
            gam = gamma[index, e : e + 1, :]
            wide_re, wide_im = g_re.astype(jnp.float32), g_im.astype(jnp.float32)
            less = (wide_re - wide_im).astype(jnp.bfloat16)
            more = (wide_re + wide_im).astype(jnp.bfloat16)
            u, v = us[0, e], vs[0, e]
            m_re = dot_nn(less, u) + dot_nt(more, v) + scale(g_re, gam).astype(jnp.float32)
            m_im = dot_nn(more, u) - dot_nt(less, v) + scale(g_im, gam).astype(jnp.float32)
            m_re, m_im = m_re.astype(jnp.bfloat16), m_im.astype(jnp.bfloat16)
            one = dot_nt(m_re, g_re) + dot_nt(m_im, g_im)
            two = dot_nt(m_im, g_re) - dot_nt(m_re, g_im)
            d_re = one if d_re is None else d_re + one
            d_im = two if d_im is None else d_im + two
        shape = (owners, norb // owners, norb)
        part[index, :, 0] = (d_re * inverse).astype(jnp.bfloat16).reshape(shape)
        part[index, :, 1] = (d_im * inverse).astype(jnp.bfloat16).reshape(shape)
        came[index, energy] = part[index, energy]

        def post(n, carry):
            peer = (energy + n * 13) % owners
            pltpu.make_async_remote_copy(
                src_ref=part.at[index, peer],
                dst_ref=came.at[index, energy],
                send_sem=send.at[index],
                recv_sem=recv.at[index],
                device_id=(peer, mom),
                device_id_type=pl.DeviceIdType.MESH,
            ).start()
            return carry

        lax.fori_loop(1, owners, post, 0)

    place = index - count
    group = place % 4 * targets

    @pl.when(jnp.logical_and(index >= count, place % 4 == 0))
    def _():
        turn = identity(height)
        for d in range(16):
            for b in range(norb // height):
                span = slice(b * height, (b + 1) * height)
                straight = rows_of[0, d // 2, d % 2, 0, :, span].astype(jnp.float32)
                turned = dot_nt(turn, cols_of[b, d // 2, d % 2, 0])
                source[d, 0, :, span] = (straight + turned).astype(jnp.bfloat16)
                source[d, 1, :, span] = (straight - turned).astype(jnp.bfloat16)

    def picks(t, d):
        return table[group + t, d]

    def donor(d, n, at):
        return source[d, n, at[0], at[1]]

    def store(t, n, at, value):
        out[t, 0, n, at[0], at[1]] = value.astype(jnp.bfloat16)

    @pl.when(index >= count)
    def _():
        def slab(i, carry):
            at = (
                pl.ds(pl.multiple_of(i // 2 * 16, 16), 16),
                pl.ds(pl.multiple_of(i % 2 * (norb // 2), norb // 2), norb // 2),
            )
            add_products(targets, 2, picks, donor, coup, at, store)
            return carry

        lax.fori_loop(0, height // 16 * 2, slab, 0)

    @pl.when(index == pl.num_programs(0) - 1)
    def _():
        for k in range(count):
            every = pltpu.make_async_remote_copy(
                src_ref=part.at[k, pl.ds(0, owners - 1)],
                dst_ref=came.at[k, pl.ds(0, owners - 1)],
                send_sem=send.at[k],
                recv_sem=recv.at[k],
                device_id=((energy + 1) % owners, mom),
                device_id_type=pl.DeviceIdType.MESH,
            )
            every.wait_recv()
            every.wait_send()

            def add(n, total):
                return total + came[k, n].astype(jnp.float32)

            total = lax.fori_loop(1, owners, add, came[k, 0].astype(jnp.float32))
            for c in range(2):
                density[:, k, c, :] = total[c]


def finished(table, green, gamma, us, vs, src, coupling, owners, targets):
    chunks, _, half, energies, rows, norb = src.shape
    points, height, _ = coupling.shape
    count = green.shape[0]
    own_rows = norb // owners
    groups = points // targets

    def of_k(i):
        return jnp.minimum(i, count - 1)

    def of_e(i):
        return jnp.maximum(i - count, 0) // groups

    def of_g(i):
        return jnp.maximum(i - count, 0) % groups

    part = pl.BlockSpec((1, energies, norb, norb), lambda i: (of_k(i), 0, 0, 0))
    return pl.pallas_call(
        functools.partial(finish_kernel, 1.0 / (energies * owners)),
        grid=(count + energies * groups,),
        in_specs=[
            pl.BlockSpec(memory_space=pltpu.SMEM),
            pl.BlockSpec((1, energies, 2, norb, norb), lambda i: (of_k(i), 0, 0, 0, 0)),
            pl.BlockSpec(gamma.shape, lambda i: (0, 0, 0)),
            part,
            part,
            pl.BlockSpec(
                (1, 8, half, 1, rows, norb),
                lambda i: (lax.axis_index("mom"), 0, 0, of_e(i), 0, 0),
            ),
            pl.BlockSpec(
                (chunks, 8, half, 1, rows, height),
                lambda i: (0, 0, 0, of_e(i), 0, lax.axis_index("mom")),
            ),
            pl.BlockSpec((points, height, norb), lambda i: (0, 0, 0)),
        ],
        out_specs=[
            pl.BlockSpec((targets, 1, 2, height, norb), lambda i: (of_g(i), of_e(i), 0, 0, 0)),
            pl.BlockSpec((own_rows, count, 2, norb), lambda i: (0, 0, 0, 0)),
        ],
        out_shape=[
            jax.ShapeDtypeStruct((points, energies, 2, height, norb), jnp.bfloat16),
            jax.ShapeDtypeStruct((own_rows, count, 2, norb), jnp.float32),
        ],
        scratch_shapes=[
            pltpu.VMEM((16, 2, height, norb), jnp.bfloat16),
            pltpu.VMEM((count, owners, 2, own_rows, norb), jnp.bfloat16),
            pltpu.VMEM((count, owners, 2, own_rows, norb), jnp.bfloat16),
            pltpu.SemaphoreType.DMA((count,)),
            pltpu.SemaphoreType.DMA((count,)),
        ],
        compiler_params=pltpu.CompilerParams(
            collective_id=1, has_side_effects=True, vmem_limit_bytes=60 * MIB
        ),
        name="finish",
    )(table, green, gamma, us, vs, src, src, coupling)


def on_device(green, broadening, coupling, shift_steps, mode_weight, occupation, momentum_map):
    n_energy, n_mom = lax.axis_size("energy"), lax.axis_size("mom")
    local_k = green.shape[0]
    half = local_k // 2
    points = momentum_map.shape[1]
    energy, mom = lax.axis_index("energy"), lax.axis_index("mom")
    x_lo = energy % 2

    sent, own = packed_lesser(x_lo.astype(jnp.int32)[None], green, broadening, n_mom)
    moves = [(0, 0), (1, 0), (1, 2), (0, 2)]
    moves = moves + [(lo, mo ^ 1) for lo, mo in moves]
    donors = jnp.stack(
        [(mom ^ mo) * local_k + (x_lo ^ lo) * half + kk for lo, mo in moves for kk in range(half)]
    ).astype(jnp.int32)
    table = jnp.sum(
        jnp.where(
            momentum_map[:, :, None] == donors[None, None, :],
            jnp.arange(points, dtype=jnp.int32)[None, :, None],
            0,
        ),
        axis=1,
    ).astype(jnp.int32)
    src, us, vs = exchanged(
        shift_steps, mode_weight, occupation, table, sent, own, coupling, local_k
    )
    return tuple(
        finished(table, green, broadening, us, vs, src, coupling, n_energy, local_k)
    )


def solution(mesh):
    return jax.shard_map(
        on_device,
        mesh=mesh,
        in_specs=(
            P("mom", "energy", None, None, None),
            P("mom", "energy", None),
            P(None, "mom", None),
            P(),
            P(),
            P(),
            P(),
        ),
        out_specs=(P(None, "energy", None, "mom", None), P("energy", "mom", None, None)),
        check_vma=False,
    )
```
